128 devices in a mesh: agent: 16 (over x, y_hi, core), mode: 8 (over z, y_lo).
Axes of the slice: x: 4, y: 4 (y_hi: 2, y_lo: 2; y = y_hi * 2 + y_lo), z: 4, core: 2. Of those that a mesh axis runs over, the one named last changes fastest.
Arguments:
- tokens: bfloat16 [128, 64, 4, 1024], P('agent', 'mode'), may hold values from -8 to 8
- cotangent: bfloat16 [128, 64, 4, 1024], P('agent', 'mode'), may hold values from -6 to 6
- weights: bfloat16 [8, 1024, 1024], replicated, may hold values from -2 to 2
- agent_mask: int32 [128], replicated, may hold values from 0 to 1, as said below
Outputs:
- token_grads: bfloat16 [128, 64, 4, 1024], P('agent', 'mode')
- agent_weight_grads: float32 [4096, 1024], P(('agent', 'mode'))
- mode_weight_grads: float32 [4096, 1024], P(('agent', 'mode'))
The draws below stay inside these ranges and needn't reach their ends.
Inputs may be any that keep to these rules, and one draw needn't show every extreme that they name: `agent_mask`: 1 marks a valid agent; at least one agent is valid.
All inputs are finite; a program needn't handle non-finite values.
Results may differ from the reference program's by a relative error of at most 0.034.
The reference program's roundings to bfloat16 on the way count: a program that leaves them out, or rounds other values in their place, can miss the bound.
Values may be sent and summed in bfloat16 or wider, within the bound.
No kernel may reach another device: no remote copies, remote signals or barrier semaphores. Data moves between devices by JAX's collectives and lax.ppermute only.
A program may use at most 192 MiB of HBM per device.

```python
import jax
import jax.numpy as jnp
from jax import lax

STEPS = 4
D = 1024
HEADS = 16
HEAD_DIM = 64
AGENTS = 128
MODES = 64


def draw_tokens(key, part):
    key = jax.random.fold_in(key, 11)
    array_shape = (AGENTS, MODES, STEPS, D)
    values = jax.random.normal(key, array_shape, jnp.float32)
    return jnp.clip(values, -8.0, 8.0).astype(jnp.bfloat16)


def draw_weights(key, part):
    key = jax.random.fold_in(key, 23)
    key_main = jax.random.fold_in(key, 0)
    matrices = jax.random.normal(key_main, (8, D, D), jnp.float32) * D ** (-0.5)
    return jnp.clip(matrices, -2.0, 2.0).astype(jnp.bfloat16)


def draw_agent_mask(key, part):
    key = jax.random.fold_in(key, 37)
    key_bits, key_spot = jax.random.split(key)
    raw_bits = jax.random.randint(key_bits, (AGENTS,), 0, 2)
    chosen = jax.random.randint(key_spot, (), 0, AGENTS)
    return jnp.where(jnp.arange(AGENTS) == chosen, 1, raw_bits).astype(jnp.int32)


def level_of(stream_key, dims, cuts, least, top_value):
    level, own = 1.0, jax.random.fold_in(stream_key, 6)
    for axis_at, shards_of in cuts:
        heights = jnp.exp(jax.random.uniform(jax.random.fold_in(own, axis_at), (shards_of,), jnp.float32, least / len(cuts), top_value / len(cuts)))
        level = level * jnp.repeat(heights, dims[axis_at] // shards_of).reshape([-1 if axis == axis_at else 1 for axis in range(len(dims))])
    return level


def centred(own_key, dims, deviation, most, cuts=(), dtype=jnp.bfloat16):
    values = deviation * jax.random.normal(own_key, dims, jnp.float32)
    if cuts:
        values = values * level_of(own_key, dims, cuts, -0.22, 0.18)
    return jnp.clip(values, -most, most).astype(dtype)


def setup_inputs(seed: int = 0) -> dict:
    arg_keys = jax.random.split(jax.random.key(seed), 5)
    return {
        "tokens": draw_tokens(jax.random.fold_in(arg_keys[4], 71), 0),
        "cotangent": centred(arg_keys[1], (AGENTS, MODES, STEPS, D), 1.0, 6.0, ((0, 16), (1, 8))),
        "weights": draw_weights(jax.random.fold_in(arg_keys[4], 71), 0),
        "agent_mask": draw_agent_mask(jax.random.fold_in(arg_keys[4], 71), 0),
    }


epsilon = 1e-06
masked_score = -1000000000.0

def normalize(values):
    wide = values.astype(jnp.float32)
    factor = lax.rsqrt(lax.optimization_barrier(jnp.mean(wide * wide, -1, keepdims=True)) + epsilon)
    return (wide * factor, factor)

def normalize_back(values, factor, upstream):
    normed = values.astype(jnp.float32) * factor
    return factor * (upstream - normed * lax.optimization_barrier(jnp.mean(upstream * normed, -1, keepdims=True)))

def probabilities(query_in, keys_in, offset_add, forms):
    query_form, keys_form, score_form = forms
    scores = jnp.einsum(query_form + ',' + keys_form + '->' + score_form, query_in.astype(jnp.float32), keys_in.astype(jnp.float32)) * HEAD_DIM ** (-0.5) + offset_add
    largest = lax.optimization_barrier(jnp.max(scores, -1, keepdims=True))
    raised = jnp.exp(scores - largest)
    return raised / lax.optimization_barrier(jnp.sum(raised, -1, keepdims=True))

def heads_forward(query_in, keys_in, values_in, offset_add, forms):
    query_form, keys_form, score_form = forms

    def one_head(pieces):
        query_head, keys_head, values_head = pieces
        table = probabilities(query_head, keys_head, offset_add, forms)
        rounded = lax.optimization_barrier(table.astype(jnp.bfloat16)).astype(jnp.float32)
        return jnp.einsum(score_form + ',' + keys_form + '->' + query_form, rounded, values_head.astype(jnp.float32)).astype(jnp.bfloat16)
    result = lax.map(one_head, (jnp.moveaxis(query_in, 3, 0), jnp.moveaxis(keys_in, 3, 0), jnp.moveaxis(values_in, 3, 0)))
    return jnp.moveaxis(result, 0, 3)

def heads_backward(query_in, keys_in, values_in, upstream, offset_add, forms):
    query_form, keys_form, score_form = forms

    def one_head(pieces):
        query_head, keys_head, values_head, upstream_head = pieces
        table = probabilities(query_head, keys_head, offset_add, forms)
        rounded = lax.optimization_barrier(table.astype(jnp.bfloat16)).astype(jnp.float32)
        upstream_wide = upstream_head.astype(jnp.float32)
        through = jnp.einsum(query_form + ',' + keys_form + '->' + score_form, upstream_wide, values_head.astype(jnp.float32))
        value_grad = jnp.einsum(score_form + ',' + query_form + '->' + keys_form, rounded, upstream_wide).astype(jnp.bfloat16)
        centre = lax.optimization_barrier(jnp.sum(through * table, -1, keepdims=True))
        score_grad = (table * (through - centre) * HEAD_DIM ** (-0.5)).astype(jnp.bfloat16)
        score_wide = lax.optimization_barrier(score_grad).astype(jnp.float32)
        query_grad = jnp.einsum(score_form + ',' + keys_form + '->' + query_form, score_wide, keys_head.astype(jnp.float32)).astype(jnp.bfloat16)
        keys_grad = jnp.einsum(score_form + ',' + query_form + '->' + keys_form, score_wide, query_head.astype(jnp.float32)).astype(jnp.bfloat16)
        return (query_grad, keys_grad, value_grad)
    moved = (jnp.moveaxis(query_in, 3, 0), jnp.moveaxis(keys_in, 3, 0), jnp.moveaxis(values_in, 3, 0), jnp.moveaxis(upstream, 3, 0))
    grads = lax.map(one_head, moved)
    return tuple((jnp.moveaxis(entry, 0, 3) for entry in grads))

def reference(tokens, cotangent, weights, agent_mask):
    key_offset = jnp.where(agent_mask == 1, 0.0, masked_score).astype(jnp.float32)
    agent_forms = ('amse', 'bmse', 'msab')
    mode_forms = ('amse', 'anse', 'asmn')
    split_shape = (AGENTS, MODES, STEPS, HEADS, HEAD_DIM)
    token_rows = tokens.reshape(-1, D)
    grad_rows = cotangent.reshape(-1, D)

    def project(inputs, matrix_slot):
        return jnp.dot(inputs, weights[matrix_slot], preferred_element_type=jnp.float32).astype(jnp.bfloat16)

    def project_back(grads, matrix_slot):
        return lax.dot_general(grads.reshape(-1, D), weights[matrix_slot], (((1,), (1,)), ((), ())), preferred_element_type=jnp.float32)

    def outer_sum(left_rows, right_rows):
        return lax.dot_general(left_rows.reshape(-1, D), right_rows.reshape(-1, D), (((0,), (0,)), ((), ())), preferred_element_type=jnp.float32)
    normed_one, factor_one = normalize(token_rows)
    hidden_one = normed_one.astype(jnp.bfloat16)
    query_one = project(hidden_one, 0).reshape(split_shape)
    keys_one = project(hidden_one, 1).reshape(split_shape)
    values_one = project(hidden_one, 2).reshape(split_shape)
    mixed_one = heads_forward(query_one, keys_one, values_one, key_offset, agent_forms).reshape(-1, D)
    after_agents = (token_rows.astype(jnp.float32) + jnp.dot(mixed_one, weights[3], preferred_element_type=jnp.float32)).astype(jnp.bfloat16)
    normed_two, factor_two = normalize(after_agents)
    hidden_two = normed_two.astype(jnp.bfloat16)
    query_two = project(hidden_two, 4).reshape(split_shape)
    keys_two = project(hidden_two, 5).reshape(split_shape)
    values_two = project(hidden_two, 6).reshape(split_shape)
    zero_offset = jnp.zeros((), jnp.float32)
    mixed_two = heads_forward(query_two, keys_two, values_two, zero_offset, mode_forms).reshape(-1, D)
    upstream_two = project_back(grad_rows, 7).astype(jnp.bfloat16).reshape(split_shape)
    query_grad_two, keys_grad_two, value_grad_two = heads_backward(query_two, keys_two, values_two, upstream_two, zero_offset, mode_forms)
    hidden_grad_two = project_back(query_grad_two, 4) + project_back(keys_grad_two, 5) + project_back(value_grad_two, 6)
    grad_after = (grad_rows.astype(jnp.float32) + normalize_back(after_agents, factor_two, hidden_grad_two)).astype(jnp.bfloat16)
    upstream_one = project_back(grad_after, 3).astype(jnp.bfloat16).reshape(split_shape)
    query_grad_one, keys_grad_one, value_grad_one = heads_backward(query_one, keys_one, values_one, upstream_one, key_offset, agent_forms)
    hidden_grad_one = project_back(query_grad_one, 0) + project_back(keys_grad_one, 1) + project_back(value_grad_one, 2)
    token_grads = (grad_after.astype(jnp.float32) + normalize_back(token_rows, factor_one, hidden_grad_one)).astype(jnp.bfloat16)
    agent_weight_grads = jnp.concatenate([outer_sum(hidden_one, query_grad_one), outer_sum(hidden_one, keys_grad_one), outer_sum(hidden_one, value_grad_one), outer_sum(mixed_one, grad_after)], 0)
    mode_weight_grads = jnp.concatenate([outer_sum(hidden_two, query_grad_two), outer_sum(hidden_two, keys_grad_two), outer_sum(hidden_two, value_grad_two), outer_sum(mixed_two, grad_rows)], 0)
    return (token_grads.reshape(tokens.shape), agent_weight_grads, mode_weight_grads)
```

```python
import functools

import jax
import jax.numpy as jnp
from jax import lax
from jax.experimental import pallas as pl
from jax.experimental.pallas import tpu as pltpu
from jax.sharding import PartitionSpec as P

epsilon = 1e-06
masked_score = -1000000000.0

BF = jnp.bfloat16
F32 = jnp.float32
D = 1024
ROWS = 256
SCALE = 0.125
MIB = 1024 * 1024


def decode(row, order):
    if order == "o":
        return row >> 5, (row >> 2) & 7, row & 3
    if order == "a":
        return row & 7, row >> 5, (row >> 3) & 3
    return (row >> 3) & 7, row & 7, row >> 6


def encode(agent, mode, step, order):
    if order == "o":
        return agent * 32 + mode * 4 + step
    if order == "a":
        return mode * 32 + step * 8 + agent
    return step * 64 + agent * 8 + mode


def reorder(values, source, target):
    rows = lax.broadcasted_iota(jnp.int32, (ROWS, ROWS), 0)
    columns = lax.broadcasted_iota(jnp.int32, (ROWS, ROWS), 1)
    chosen = encode(*decode(rows, target), source)
    table = (chosen == columns).astype(F32).astype(BF)
    return jnp.dot(table, values, preferred_element_type=F32).astype(BF)


def dot_nt(left, right):
    return lax.dot_general(left, right, (((1,), (1,)), ((), ())), preferred_element_type=F32)


def dot_tn(left, right):
    return lax.dot_general(left, right, (((0,), (0,)), ((), ())), preferred_element_type=F32)


def factor_of(wide):
    return lax.rsqrt(jnp.mean(wide * wide, -1, keepdims=True) + epsilon)


def normalize_back(values, upstream):
    wide = values.astype(F32)
    factor = factor_of(wide)
    normed = wide * factor
    return factor * (upstream - normed * jnp.mean(upstream * normed, -1, keepdims=True))


def params(limit=32):
    return pltpu.CompilerParams(vmem_limit_bytes=limit * MIB)


def cost(flops, read):
    return pl.CostEstimate(flops=int(flops), bytes_accessed=int(read), transcendentals=0)


def fixed(shape):
    return pl.BlockSpec(shape, lambda *i: (0,) * len(shape))


def stack_heads(values):
    lanes = lax.broadcasted_iota(jnp.int32, (1, 128), 1)
    first = (lanes < 64).astype(F32).astype(BF)
    second = (lanes >= 64).astype(F32).astype(BF)
    return jnp.concatenate([values * first, values * second], 0)


def beside(table):
    return jnp.concatenate([table[:128], table[128:]], 1)


def probabilities(query_stack, keys, offset):
    scores = dot_nt(query_stack, keys) * SCALE + offset
    raised = jnp.exp(scores - jnp.max(scores, -1, keepdims=True))
    return raised / jnp.sum(raised, -1, keepdims=True)


def attend(table, values):
    return jnp.dot(beside(table.astype(BF)), stack_heads(values), preferred_element_type=F32)


def attention_back(table, query_stack, keys, values, upstream):
    upstream_stack = stack_heads(upstream)
    through = dot_nt(upstream_stack, values)
    value_grad = dot_tn(table.astype(BF), upstream_stack)
    centre = jnp.sum(through * table, -1, keepdims=True)
    score_grad = (table * (through - centre) * SCALE).astype(BF)
    query_grad = jnp.dot(beside(score_grad), stack_heads(keys), preferred_element_type=F32)
    keys_grad = dot_tn(score_grad, query_stack)
    return query_grad, keys_grad, value_grad


def enter_kernel(tokens_ref, weights_ref, send_ref, tokens_out_ref, hidden_out_ref, hidden_ref):
    step = pl.program_id(0)

    @pl.when(step == 0)
    def _():
        rows = reorder(tokens_ref[...], "o", "a")
        tokens_out_ref[...] = rows
        wide = rows.astype(F32)
        hidden = (wide * factor_of(wide)).astype(BF)
        hidden_ref[...] = hidden
        for block in range(8):
            hidden_out_ref[block] = hidden[:, 128 * block : 128 * block + 128]

    result = jnp.dot(hidden_ref[...], weights_ref[0], preferred_element_type=F32).astype(BF)
    for pair in range(8):
        for half in range(2):
            send_ref[2 * pair + half] = result[
                128 * half : 128 * half + 128, 128 * pair : 128 * pair + 128
            ]


def enter(tokens, weights):
    return pl.pallas_call(
        enter_kernel,
        grid=(3,),
        in_specs=[fixed((ROWS, D)), pl.BlockSpec((1, D, D), lambda i: (i, 0, 0))],
        out_specs=[
            pl.BlockSpec((16, 128, 128), lambda i: (0, i, 0)),
            fixed((ROWS, D)),
            fixed((8, ROWS, 128)),
        ],
        out_shape=[
            jax.ShapeDtypeStruct((16, 384, 128), BF),
            jax.ShapeDtypeStruct((ROWS, D), BF),
            jax.ShapeDtypeStruct((8, ROWS, 128), BF),
        ],
        scratch_shapes=[pltpu.VMEM((ROWS, D), BF)],
        compiler_params=params(),
        cost_estimate=cost(3 * 2 * ROWS * D * D, 8 * MIB),
        name="enter",
    )(tokens, weights)


def agent_rows(block, step):
    return block[:, 8 * step : 8 * step + 8, :].reshape(128, 128).astype(BF)


def agent_forward_kernel(query_ref, keys_ref, values_ref, offset_ref, out_ref, table_ref):
    query = query_ref[...].astype(F32)
    keys = keys_ref[...].astype(F32)
    values = values_ref[...].astype(F32)
    offset = offset_ref[...]
    outs = []
    for step in range(4):
        table = probabilities(
            stack_heads(agent_rows(query, step)), agent_rows(keys, step), offset
        )
        table_ref[0, step] = table
        outs.append(attend(table, agent_rows(values, step)).reshape(16, 8, 128))
    out_ref[...] = jnp.concatenate(outs, 1).astype(BF)


def agent_specs():
    return [pl.BlockSpec((16, 32, 128), lambda i, k=k: (0, 4 * k + i, 0)) for k in range(3)]


def agent_forward(arrived, offset):
    return pl.pallas_call(
        agent_forward_kernel,
        grid=(4,),
        in_specs=agent_specs() + [fixed((1, 128))],
        out_specs=[
            pl.BlockSpec((16, 32, 128), lambda i: (0, i, 0)),
            pl.BlockSpec((1, 4, 256, 128), lambda i: (i, 0, 0, 0)),
        ],
        out_shape=[
            jax.ShapeDtypeStruct((16, 128, 128), BF),
            jax.ShapeDtypeStruct((4, 4, 256, 128), F32),
        ],
        compiler_params=params(),
        cost_estimate=cost(3e9, 4 * MIB),
        name="agent_forward",
    )(arrived, arrived, arrived, offset)


def agent_backward_kernel(
    query_ref, keys_ref, values_ref, upstream_ref, table_ref, query_out, keys_out, values_out
):
    query = query_ref[...].astype(F32)
    keys = keys_ref[...].astype(F32)
    values = values_ref[...].astype(F32)
    upstream = upstream_ref[...].astype(F32)
    outs = [[], [], []]
    for step in range(4):
        grads = attention_back(
            table_ref[0, step],
            stack_heads(agent_rows(query, step)),
            agent_rows(keys, step),
            agent_rows(values, step),
            agent_rows(upstream, step),
        )
        for kept, grad in zip(outs, grads):
            kept.append(grad.reshape(16, 8, 128))
    for ref, kept in zip((query_out, keys_out, values_out), outs):
        ref[...] = jnp.concatenate(kept, 1).astype(BF)


def agent_backward_all_kernel(q, k, v, g, table_ref, out_ref):
    agent_backward_kernel(
        q,
        k,
        v,
        g,
        table_ref,
        out_ref.at[:, 0],
        out_ref.at[:, 1],
        out_ref.at[:, 2],
    )


def agent_backward(arrived, upstream, tables):
    return pl.pallas_call(
        agent_backward_all_kernel,
        grid=(4,),
        in_specs=agent_specs()
        + [
            pl.BlockSpec((16, 32, 128), lambda i: (0, i, 0)),
            pl.BlockSpec((1, 4, 256, 128), lambda i: (i, 0, 0, 0)),
        ],
        out_specs=pl.BlockSpec((16, 3, 32, 128), lambda i: (0, 0, i, 0)),
        out_shape=jax.ShapeDtypeStruct((16, 3, 128, 128), BF),
        compiler_params=params(),
        cost_estimate=cost(6e9, 6 * MIB),
        name="agent_backward",
    )(arrived, arrived, arrived, upstream, tables)


def middle_kernel(
    tokens_ref, mixed_ref, cotangent_ref, weights_ref,
    send_ref, after_ref, hidden_out_ref, cotangent_out_ref, hidden_ref,
):
    step = pl.program_id(0)

    @pl.when(step == 0)
    def _():
        mixed = jnp.concatenate([mixed_ref[pair] for pair in range(8)], 1)
        after = (
            tokens_ref[...].astype(F32)
            + jnp.dot(mixed, weights_ref[0], preferred_element_type=F32)
        ).astype(BF)
        after = reorder(after, "a", "m")
        after_ref[...] = after
        wide = after.astype(F32)
        hidden = (wide * factor_of(wide)).astype(BF)
        hidden_ref[...] = hidden
        for block in range(8):
            hidden_out_ref[block] = hidden[:, 128 * block : 128 * block + 128]
        cotangent_out_ref[...] = reorder(cotangent_ref[...], "o", "m")

    def send(result):
        result = result.astype(BF)
        for pair in range(8):
            send_ref[pair, 0] = result[:, 128 * pair : 128 * pair + 128]

    @pl.when((step > 0) & (step < 4))
    def _():
        send(jnp.dot(hidden_ref[...], weights_ref[0], preferred_element_type=F32))

    @pl.when(step == 4)
    def _():
        send(dot_nt(cotangent_out_ref[...], weights_ref[0]))


def middle(tokens, mixed, cotangent, weights):
    return pl.pallas_call(
        middle_kernel,
        grid=(5,),
        in_specs=[
            fixed((ROWS, D)),
            fixed((8, ROWS, 128)),
            fixed((ROWS, D)),
            pl.BlockSpec((1, D, D), lambda i: (3 + i, 0, 0)),
        ],
        out_specs=[
            pl.BlockSpec((8, 1, ROWS, 128), lambda i: (0, jnp.maximum(i - 1, 0), 0, 0)),
            fixed((ROWS, D)),
            fixed((8, ROWS, 128)),
            fixed((ROWS, D)),
        ],
        out_shape=[
            jax.ShapeDtypeStruct((8, 4, ROWS, 128), BF),
            jax.ShapeDtypeStruct((ROWS, D), BF),
            jax.ShapeDtypeStruct((8, ROWS, 128), BF),
            jax.ShapeDtypeStruct((ROWS, D), BF),
        ],
        scratch_shapes=[pltpu.VMEM((ROWS, D), BF)],
        compiler_params=params(),
        cost_estimate=cost(5 * 2 * ROWS * D * D, 13 * MIB),
        name="middle",
    )(tokens, mixed, cotangent, weights)


def mode_kernel(arrived_ref, out_ref):
    rows = lax.broadcasted_iota(jnp.int32, (256, 128), 0)
    columns = lax.broadcasted_iota(jnp.int32, (256, 128), 1)
    same = ((rows >> 6) & 1) == (columns >> 6)
    offset = jnp.where(same, 0.0, -1e30).astype(F32)
    for pair in range(4):

        def take(which):
            block = arrived_ref[:, which, 16 * pair : 16 * pair + 16, :].astype(F32)
            parts = [block[:, 8 * n : 8 * n + 8, :].reshape(64, 128) for n in range(2)]
            return jnp.concatenate(parts, 0).astype(BF)

        query, keys, values, upstream = (take(which) for which in range(4))
        query_stack = stack_heads(query)
        table = probabilities(query_stack, keys, offset)
        results = (attend(table, values),) + attention_back(
            table, query_stack, keys, values, upstream
        )
        for which, result in enumerate(results):
            parts = [result[64 * n : 64 * n + 64].reshape(8, 8, 128) for n in range(2)]
            out_ref[:, which, 16 * pair : 16 * pair + 16, :] = jnp.concatenate(parts, 1).astype(BF)


def mode_attention(arrived):
    spec = pl.BlockSpec((8, 4, 64, 128), lambda i: (0, 0, i, 0))
    return pl.pallas_call(
        mode_kernel,
        grid=(4,),
        in_specs=[spec],
        out_specs=spec,
        out_shape=jax.ShapeDtypeStruct((8, 4, ROWS, 128), BF),
        compiler_params=params(),
        cost_estimate=cost(8e9, 4 * MIB),
        name="mode_attention",
    )(arrived)


def turn_kernel(
    returned_ref, cotangent_ref, after_ref, weights_ref, send_ref, grad_after_ref, total_ref
):
    step = pl.program_id(0)

    @pl.when(step < 3)
    def _():
        grads = jnp.concatenate([returned_ref[pair, 0] for pair in range(8)], 1)
        product = dot_nt(grads, weights_ref[0])

        @pl.when(step == 0)
        def _():
            total_ref[...] = product

        @pl.when(step > 0)
        def _():
            total_ref[...] += product

    @pl.when(step == 3)
    def _():
        grad_after = (
            cotangent_ref[...].astype(F32) + normalize_back(after_ref[...], total_ref[...])
        ).astype(BF)
        grad_after = reorder(grad_after, "m", "a")
        grad_after_ref[...] = grad_after
        result = dot_nt(grad_after, weights_ref[0]).astype(BF)
        for pair in range(8):
            for half in range(2):
                send_ref[2 * pair + half] = result[
                    128 * half : 128 * half + 128, 128 * pair : 128 * pair + 128
                ]


def turn(returned, cotangent, after, weights):
    return pl.pallas_call(
        turn_kernel,
        grid=(4,),
        in_specs=[
            pl.BlockSpec((8, 1, ROWS, 128), lambda i: (0, jnp.minimum(i + 1, 3), 0, 0)),
            fixed((ROWS, D)),
            fixed((ROWS, D)),
            pl.BlockSpec((1, D, D), lambda i: (jnp.where(i < 3, i + 4, 3), 0, 0)),
        ],
        out_specs=[fixed((16, 128, 128)), fixed((ROWS, D))],
        out_shape=[
            jax.ShapeDtypeStruct((16, 128, 128), BF),
            jax.ShapeDtypeStruct((ROWS, D), BF),
        ],
        scratch_shapes=[pltpu.VMEM((ROWS, D), F32)],
        compiler_params=params(),
        cost_estimate=cost(4 * 2 * ROWS * D * D, 12 * MIB),
        name="turn",
    )(returned, cotangent, after, weights)


def whole_rows(ref):
    return jnp.concatenate([ref[:, 0].reshape(8, ROWS, 128)[pair] for pair in range(8)], 1)


def leave_kernel(returned_ref, tokens_ref, grad_after_ref, weights_ref, out_ref, total_ref):
    step = pl.program_id(0)
    product = dot_nt(whole_rows(returned_ref), weights_ref[0])

    @pl.when(step == 0)
    def _():
        total_ref[...] = product

    @pl.when(step > 0)
    def _():
        total_ref[...] += product

    @pl.when(step == 2)
    def _():
        grads = (
            grad_after_ref[...].astype(F32) + normalize_back(tokens_ref[...], total_ref[...])
        ).astype(BF)
        out_ref[...] = reorder(grads, "a", "o")


def leave(returned, tokens, grad_after, weights):
    return pl.pallas_call(
        leave_kernel,
        grid=(3,),
        in_specs=[
            pl.BlockSpec((16, 1, 128, 128), lambda i: (0, i, 0, 0)),
            fixed((ROWS, D)),
            fixed((ROWS, D)),
            pl.BlockSpec((1, D, D), lambda i: (i, 0, 0)),
        ],
        out_specs=fixed((ROWS, D)),
        out_shape=jax.ShapeDtypeStruct((ROWS, D), BF),
        scratch_shapes=[pltpu.VMEM((ROWS, D), F32)],
        compiler_params=params(),
        cost_estimate=cost(3 * 2 * ROWS * D * D, 9 * MIB),
        name="leave",
    )(returned, tokens, grad_after, weights)


def weight_kernel(of_agents, add, core_ref, hidden_ref, mixed_ref, grads_ref, last_ref, *rest):
    step = pl.program_id(0)
    if add:
        arrived_ref, out_ref = rest
    else:
        (out_ref,) = rest

    def finish(left_ref, right):
        left = jnp.concatenate([left_ref[0], left_ref[1]], 1)
        product = dot_tn(left, right)
        if add:
            total = product + arrived_ref[0].astype(F32)
            out_ref[...] = total.astype(BF).reshape(8, 1, 32, D)
        else:
            out_ref[0] = product.astype(BF)

    @pl.when(step < 6)
    def _():
        if of_agents:
            right = whole_rows(grads_ref)
        else:
            right = jnp.concatenate([grads_ref[pair, 0] for pair in range(8)], 1)
        finish(hidden_ref, right)

    @pl.when(step >= 6)
    def _():
        finish(mixed_ref.at[:, 0] if not of_agents else mixed_ref, last_ref[...])


def weight_products(of_agents, core, hidden, mixed, grads, last, arrived=None):
    add = arrived is not None

    def feature(i, core_ref):
        return 2 * (i % 2) + core_ref[0]

    if of_agents:
        mixed_spec = pl.BlockSpec((2, ROWS, 128), lambda i, c: (feature(i, c), 0, 0))
        grads_spec = pl.BlockSpec(
            (16, 1, 128, 128), lambda i, c: (0, jnp.minimum(i // 2, 2), 0, 0)
        )
    else:
        mixed_spec = pl.BlockSpec((2, 1, ROWS, 128), lambda i, c: (feature(i, c), 0, 0, 0))
        grads_spec = pl.BlockSpec(
            (8, 1, ROWS, 128), lambda i, c: (0, jnp.minimum(i // 2, 2) + 1, 0, 0)
        )
    in_specs = [
        pl.BlockSpec((2, ROWS, 128), lambda i, c: (feature(i, c), 0, 0)),
        mixed_spec,
        grads_spec,
        pl.BlockSpec((ROWS, D), lambda i, c: (0, 0)),
    ]
    operands = [core, hidden, mixed, grads, last]
    if add:
        in_specs.append(pl.BlockSpec((1, ROWS, D), lambda i, c: (i, 0, 0)))
        operands.append(arrived)
        out_spec = pl.BlockSpec((8, 1, 32, D), lambda i, c: (0, i, 0, 0))
        out_shape = jax.ShapeDtypeStruct((8, 8, 32, D), BF)
    else:
        out_spec = pl.BlockSpec((1, ROWS, D), lambda i, c: (i, 0, 0))
        out_shape = jax.ShapeDtypeStruct((8, ROWS, D), BF)
    return pl.pallas_call(
        functools.partial(weight_kernel, of_agents, add),
        grid_spec=pltpu.PrefetchScalarGridSpec(
            num_scalar_prefetch=1, grid=(8,), in_specs=in_specs, out_specs=out_spec
        ),
        out_shape=out_shape,
        compiler_params=params(),
        cost_estimate=cost(4 * 2 * ROWS * D * D // 2, 8 * MIB),
        name="weights_add" if add else "weights_first",
    )(*operands)


def swap_cores(values, axis_size):
    return lax.ppermute(values, "agent", [(n, n ^ 1) for n in range(axis_size)])


def exchange(values, axis):
    return lax.all_to_all(values, axis, split_axis=0, concat_axis=0, tiled=True)


def reduce_grads(of_agents, hidden, mixed, grads, last):
    agent_size = lax.axis_size("agent")
    core = (lax.axis_index("agent") % 2).astype(jnp.int32).reshape(1)
    theirs = weight_products(of_agents, 1 - core, hidden, mixed, grads, last)
    arrived = swap_cores(theirs, agent_size)
    mine = weight_products(of_agents, core, hidden, mixed, grads, last, arrived)
    over_modes = exchange(mine.reshape(8, 256, D), "mode").reshape(8, 256, D)
    partial = jnp.sum(over_modes.astype(F32), 0).astype(BF).reshape(8, 32, D)
    groups = [list(range(c, agent_size, 2)) for c in range(2)]
    over_agents = lax.all_to_all(
        partial, "agent", split_axis=0, concat_axis=0, tiled=True, axis_index_groups=groups
    )
    return jnp.sum(over_agents.astype(F32), 0)


def local(tokens, cotangent, weights, agent_mask):
    token_rows = tokens.reshape(ROWS, D)
    grad_rows = cotangent.reshape(ROWS, D)
    offset = jnp.where(agent_mask == 1, 0.0, masked_score).astype(F32).reshape(1, 128)

    outgoing, tokens_a, hidden_one = enter(token_rows, weights)
    arrived_one = exchange(outgoing, "agent")
    mixed, tables = agent_forward(arrived_one, offset)
    mixed_one = exchange(mixed, "agent").reshape(8, ROWS, 128)
    outgoing, after, hidden_two, cotangent_m = middle(tokens_a, mixed_one, grad_rows, weights)
    arrived_two = exchange(outgoing.reshape(8, 1024, 128), "mode").reshape(8, 4, ROWS, 128)
    returning = mode_attention(arrived_two)
    returned_two = exchange(returning.reshape(8, 1024, 128), "mode").reshape(8, 4, ROWS, 128)
    outgoing, grad_after = turn(returned_two, cotangent_m, after, weights)
    upstream = exchange(outgoing, "agent")
    returning = agent_backward(arrived_one, upstream, tables)
    returned_one = exchange(returning.reshape(16, 384, 128), "agent").reshape(16, 3, 128, 128)
    token_grads = leave(returned_one, tokens_a, grad_after, weights)
    mode_weight_grads = reduce_grads(False, hidden_two, returned_two, returned_two, cotangent_m)
    agent_weight_grads = reduce_grads(True, hidden_one, mixed_one, returned_one, grad_after)
    return (token_grads.reshape(tokens.shape), agent_weight_grads, mode_weight_grads)


def solution(mesh):
    placed = (P("agent", "mode", None, None), P("agent", "mode", None, None), P(), P())
    return jax.shard_map(
        local,
        mesh=mesh,
        in_specs=placed,
        out_specs=(
            P("agent", "mode", None, None),
            P(("agent", "mode"), None),
            P(("agent", "mode"), None),
        ),
        check_vma=False,
    )
```

```python
import functools

import jax
import jax.numpy as jnp
from jax import lax
from jax.experimental import pallas as pl
from jax.experimental.pallas import tpu as pltpu
from jax.sharding import PartitionSpec as P

epsilon = 1e-06
masked_score = -1000000000.0

BF = jnp.bfloat16
F32 = jnp.float32
D = 1024
ROWS = 256
SCALE = 0.125
MIB = 1024 * 1024


def decode(row, order):
    if order == "o":
        return row >> 5, (row >> 2) & 7, row & 3
    if order == "a":
        return row & 7, row >> 5, (row >> 3) & 3
    return (row >> 3) & 7, row & 7, row >> 6


def encode(agent, mode, step, order):
    if order == "o":
        return agent * 32 + mode * 4 + step
    if order == "a":
        return mode * 32 + step * 8 + agent
    return step * 64 + agent * 8 + mode


def reorder(values, source, target):
    rows = lax.broadcasted_iota(jnp.int32, (ROWS, ROWS), 0)
    columns = lax.broadcasted_iota(jnp.int32, (ROWS, ROWS), 1)
    chosen = encode(*decode(rows, target), source)
    table = (chosen == columns).astype(F32).astype(BF)
    return jnp.dot(table, values, preferred_element_type=F32).astype(BF)


def dot_nt(left, right):
    return lax.dot_general(left, right, (((1,), (1,)), ((), ())), preferred_element_type=F32)


def dot_tn(left, right):
    return lax.dot_general(left, right, (((0,), (0,)), ((), ())), preferred_element_type=F32)


def factor_of(wide):
    return lax.rsqrt(jnp.mean(wide * wide, -1, keepdims=True) + epsilon)


def normalize_back(values, upstream):
    wide = values.astype(F32)
    factor = factor_of(wide)
    normed = wide * factor
    return factor * (upstream - normed * jnp.mean(upstream * normed, -1, keepdims=True))


def weight_specs(slot):
    return [pl.BlockSpec((1, 256, D), lambda i, *c, q=q: (slot(i), q, 0)) for q in range(4)]


def joined(refs):
    return jnp.concatenate([ref[0] for ref in refs], 0)


def params(limit=32):
    return pltpu.CompilerParams(vmem_limit_bytes=limit * MIB)


def cost(flops, read):
    return pl.CostEstimate(flops=int(flops), bytes_accessed=int(read), transcendentals=0)


unused = pl.BlockSpec(memory_space=pl.ANY)


def fixed(shape):
    return pl.BlockSpec(shape, lambda *i: (0,) * len(shape))


def stack_heads(values):
    lanes = lax.broadcasted_iota(jnp.int32, (1, 128), 1)
    first = (lanes < 64).astype(F32).astype(BF)
    second = (lanes >= 64).astype(F32).astype(BF)
    return jnp.concatenate([values * first, values * second], 0)


def beside(table):
    return jnp.concatenate([table[:128], table[128:]], 1)


def probabilities(query_stack, keys, offset):
    scores = dot_nt(query_stack, keys) * SCALE + offset
    raised = jnp.exp(scores - jnp.max(scores, -1, keepdims=True))
    return raised / jnp.sum(raised, -1, keepdims=True)


def attend(table, values):
    return jnp.dot(beside(table.astype(BF)), stack_heads(values), preferred_element_type=F32)


def attention_back(table, query_stack, keys, values, upstream):
    upstream_stack = stack_heads(upstream)
    through = dot_nt(upstream_stack, values)
    value_grad = dot_tn(table.astype(BF), upstream_stack)
    centre = jnp.sum(through * table, -1, keepdims=True)
    score_grad = (table * (through - centre) * SCALE).astype(BF)
    query_grad = jnp.dot(beside(score_grad), stack_heads(keys), preferred_element_type=F32)
    keys_grad = dot_tn(score_grad, query_stack)
    return query_grad, keys_grad, value_grad


def enter_kernel(
    ids_ref, tokens_ref, w0, w1, w2, w3,
    send_ref, tokens_out_ref, keep_ref, give_ref, hidden_ref,
):
    step = pl.program_id(0)

    @pl.when(step == 0)
    def _():
        rows = reorder(tokens_ref[...], "o", "a")
        tokens_out_ref[...] = rows
        wide = rows.astype(F32)
        hidden = (wide * factor_of(wide)).astype(BF)
        hidden_ref[...] = hidden
        core = ids_ref[0]

        @pl.when(core == 0)
        def _():
            keep_ref[...] = hidden[:128]
            give_ref[...] = hidden[128:]

        @pl.when(core == 1)
        def _():
            keep_ref[...] = hidden[128:]
            give_ref[...] = hidden[:128]

    weights = joined((w0, w1, w2, w3))
    result = jnp.dot(hidden_ref[...], weights, preferred_element_type=F32).astype(BF)
    for pair in range(8):
        for half in range(2):
            send_ref[2 * pair + half] = result[
                128 * half : 128 * half + 128, 128 * pair : 128 * pair + 128
            ]


def enter(ids, tokens, weights):
    return pl.pallas_call(
        enter_kernel,
        grid_spec=pltpu.PrefetchScalarGridSpec(
            num_scalar_prefetch=1,
            grid=(3,),
            in_specs=[fixed((ROWS, D))] + weight_specs(lambda i: i),
            out_specs=[
                pl.BlockSpec((16, 128, 128), lambda i, c: (0, i, 0)),
                fixed((ROWS, D)),
                fixed((128, D)),
                fixed((128, D)),
            ],
            scratch_shapes=[pltpu.VMEM((ROWS, D), BF)],
        ),
        out_shape=[
            jax.ShapeDtypeStruct((16, 384, 128), BF),
            jax.ShapeDtypeStruct((ROWS, D), BF),
            jax.ShapeDtypeStruct((128, D), BF),
            jax.ShapeDtypeStruct((128, D), BF),
        ],
        compiler_params=params(52),
        cost_estimate=cost(3 * 2 * ROWS * D * D, 8 * MIB),
        name="enter",
    )(ids, tokens, *[weights] * 4)


def agent_rows(block, step):
    return block[:, 8 * step : 8 * step + 8, :].reshape(128, 128).astype(BF)


def agent_forward_kernel(query_ref, keys_ref, values_ref, offset_ref, out_ref, table_ref):
    query = query_ref[...].astype(F32)
    keys = keys_ref[...].astype(F32)
    values = values_ref[...].astype(F32)
    offset = offset_ref[...]
    outs = []
    for step in range(4):
        table = probabilities(
            stack_heads(agent_rows(query, step)), agent_rows(keys, step), offset
        )
        table_ref[0, step] = table
        outs.append(attend(table, agent_rows(values, step)).reshape(16, 8, 128))
    out_ref[...] = jnp.concatenate(outs, 1).astype(BF)


def agent_specs():
    return [pl.BlockSpec((16, 32, 128), lambda i, k=k: (0, 4 * k + i, 0)) for k in range(3)]


def agent_forward(arrived, offset):
    return pl.pallas_call(
        agent_forward_kernel,
        grid=(4,),
        in_specs=agent_specs() + [fixed((1, 128))],
        out_specs=[
            pl.BlockSpec((16, 32, 128), lambda i: (0, i, 0)),
            pl.BlockSpec((1, 4, 256, 128), lambda i: (i, 0, 0, 0)),
        ],
        out_shape=[
            jax.ShapeDtypeStruct((16, 128, 128), BF),
            jax.ShapeDtypeStruct((4, 4, 256, 128), F32),
        ],
        compiler_params=params(),
        cost_estimate=cost(3e9, 4 * MIB),
        name="agent_forward",
    )(arrived, arrived, arrived, offset)


def agent_backward_kernel(
    query_ref, keys_ref, values_ref, upstream_ref, table_ref, query_out, keys_out, values_out
):
    query = query_ref[...].astype(F32)
    keys = keys_ref[...].astype(F32)
    values = values_ref[...].astype(F32)
    upstream = upstream_ref[...].astype(F32)
    outs = [[], [], []]
    for step in range(4):
        grads = attention_back(
            table_ref[0, step],
            stack_heads(agent_rows(query, step)),
            agent_rows(keys, step),
            agent_rows(values, step),
            agent_rows(upstream, step),
        )
        for kept, grad in zip(outs, grads):
            kept.append(grad.reshape(16, 8, 128))
    for ref, kept in zip((query_out, keys_out, values_out), outs):
        ref[...] = jnp.concatenate(kept, 1).astype(BF)


def agent_backward_all_kernel(q, k, v, g, table_ref, *rest):
    out_ref = rest[-1]
    agent_backward_kernel(
        q,
        k,
        v,
        g,
        table_ref,
        out_ref.at[:, 0],
        out_ref.at[:, 1],
        out_ref.at[:, 2],
    )


def agent_backward(arrived, upstream, tables, waits=()):
    return pl.pallas_call(
        agent_backward_all_kernel,
        grid=(4,),
        in_specs=agent_specs()
        + [
            pl.BlockSpec((16, 32, 128), lambda i: (0, i, 0)),
            pl.BlockSpec((1, 4, 256, 128), lambda i: (i, 0, 0, 0)),
        ]
        + [unused] * len(waits),
        out_specs=pl.BlockSpec((16, 3, 32, 128), lambda i: (0, 0, i, 0)),
        out_shape=jax.ShapeDtypeStruct((16, 3, 128, 128), BF),
        compiler_params=params(),
        cost_estimate=cost(6e9, 6 * MIB),
        name="agent_backward",
    )(arrived, arrived, arrived, upstream, tables, *waits)


def middle_kernel(
    tokens_ref, mixed_ref, cotangent_ref, w0, w1, w2, w3, *rest
):
    send_ref, after_ref, hidden_out_ref, cotangent_out_ref, hidden_ref = rest[-5:]
    quarters = (w0, w1, w2, w3)
    step = pl.program_id(0)

    @pl.when(step == 0)
    def _():
        mixed = jnp.concatenate([mixed_ref[pair] for pair in range(8)], 1)
        after = (
            tokens_ref[...].astype(F32)
            + jnp.dot(mixed, joined(quarters), preferred_element_type=F32)
        ).astype(BF)
        after = reorder(after, "a", "m")
        after_ref[...] = after
        wide = after.astype(F32)
        hidden = (wide * factor_of(wide)).astype(BF)
        hidden_ref[...] = hidden
        for block in range(8):
            hidden_out_ref[block] = hidden[:, 128 * block : 128 * block + 128]
        cotangent_out_ref[...] = reorder(cotangent_ref[...], "o", "m")

    def send(result):
        result = result.astype(BF)
        for pair in range(8):
            send_ref[pair, 0] = result[:, 128 * pair : 128 * pair + 128]

    @pl.when((step > 0) & (step < 4))
    def _():
        send(jnp.dot(hidden_ref[...], joined(quarters), preferred_element_type=F32))

    @pl.when(step == 4)
    def _():
        send(dot_nt(cotangent_out_ref[...], joined(quarters)))


def middle(tokens, mixed, cotangent, weights, waits=()):
    return pl.pallas_call(
        middle_kernel,
        grid=(5,),
        in_specs=[
            fixed((ROWS, D)),
            fixed((8, ROWS, 128)),
            fixed((ROWS, D)),
        ]
        + weight_specs(lambda i: 3 + i)
        + [unused] * len(waits),
        out_specs=[
            pl.BlockSpec((8, 1, ROWS, 128), lambda i: (0, jnp.maximum(i - 1, 0), 0, 0)),
            fixed((ROWS, D)),
            fixed((8, ROWS, 128)),
            fixed((ROWS, D)),
        ],
        out_shape=[
            jax.ShapeDtypeStruct((8, 4, ROWS, 128), BF),
            jax.ShapeDtypeStruct((ROWS, D), BF),
            jax.ShapeDtypeStruct((8, ROWS, 128), BF),
            jax.ShapeDtypeStruct((ROWS, D), BF),
        ],
        scratch_shapes=[pltpu.VMEM((ROWS, D), BF)],
        compiler_params=params(52),
        cost_estimate=cost(5 * 2 * ROWS * D * D, 13 * MIB),
        name="middle",
    )(tokens, mixed, cotangent, *[weights] * 4, *waits)


def mode_kernel(arrived_ref, *rest):
    out_ref = rest[-1]
    rows = lax.broadcasted_iota(jnp.int32, (256, 128), 0)
    columns = lax.broadcasted_iota(jnp.int32, (256, 128), 1)
    same = ((rows >> 6) & 1) == (columns >> 6)
    offset = jnp.where(same, 0.0, -1e30).astype(F32)
    for pair in range(4):

        def take(which):
            block = arrived_ref[:, which, 16 * pair : 16 * pair + 16, :].astype(F32)
            parts = [block[:, 8 * n : 8 * n + 8, :].reshape(64, 128) for n in range(2)]
            return jnp.concatenate(parts, 0).astype(BF)

        query, keys, values, upstream = (take(which) for which in range(4))
        query_stack = stack_heads(query)
        table = probabilities(query_stack, keys, offset)
        results = (attend(table, values),) + attention_back(
            table, query_stack, keys, values, upstream
        )
        for which, result in enumerate(results):
            parts = [result[64 * n : 64 * n + 64].reshape(8, 8, 128) for n in range(2)]
            out_ref[:, which, 16 * pair : 16 * pair + 16, :] = jnp.concatenate(parts, 1).astype(BF)


def mode_attention(arrived, after=()):
    spec = pl.BlockSpec((8, 4, 64, 128), lambda i: (0, 0, i, 0))
    return pl.pallas_call(
        mode_kernel,
        grid=(4,),
        in_specs=[spec] + [unused] * len(after),
        out_specs=spec,
        out_shape=jax.ShapeDtypeStruct((8, 4, ROWS, 128), BF),
        compiler_params=params(),
        cost_estimate=cost(8e9, 4 * MIB),
        name="mode_attention",
    )(arrived, *after)


def turn_kernel(returned_ref, cotangent_ref, after_ref, w0, w1, w2, w3, *rest):
    quarters = (w0, w1, w2, w3)
    send_ref, grad_after_ref, total_ref = rest[-3:]
    step = pl.program_id(0)

    @pl.when(step < 3)
    def _():
        grads = jnp.concatenate([returned_ref[pair, 0] for pair in range(8)], 1)
        product = dot_nt(grads, joined(quarters))

        @pl.when(step == 0)
        def _():
            total_ref[...] = product

        @pl.when(step > 0)
        def _():
            total_ref[...] += product

    @pl.when(step == 3)
    def _():
        grad_after = (
            cotangent_ref[...].astype(F32) + normalize_back(after_ref[...], total_ref[...])
        ).astype(BF)
        grad_after = reorder(grad_after, "m", "a")
        grad_after_ref[...] = grad_after
        result = dot_nt(grad_after, joined(quarters)).astype(BF)
        for pair in range(8):
            for half in range(2):
                send_ref[2 * pair + half] = result[
                    128 * half : 128 * half + 128, 128 * pair : 128 * pair + 128
                ]


def turn(returned, cotangent, after, weights, waits=()):
    return pl.pallas_call(
        turn_kernel,
        grid=(4,),
        in_specs=[
            pl.BlockSpec((8, 1, ROWS, 128), lambda i: (0, jnp.minimum(i + 1, 3), 0, 0)),
            fixed((ROWS, D)),
            fixed((ROWS, D)),
        ]
        + weight_specs(lambda i: jnp.where(i < 3, i + 4, 3))
        + [unused] * len(waits),
        out_specs=[fixed((16, 128, 128)), fixed((ROWS, D))],
        out_shape=[
            jax.ShapeDtypeStruct((16, 128, 128), BF),
            jax.ShapeDtypeStruct((ROWS, D), BF),
        ],
        scratch_shapes=[pltpu.VMEM((ROWS, D), F32)],
        compiler_params=params(52),
        cost_estimate=cost(4 * 2 * ROWS * D * D, 12 * MIB),
        name="turn",
    )(returned, cotangent, after, *[weights] * 4, *waits)


def whole_rows(ref):
    return jnp.concatenate([ref[:, 0].reshape(8, ROWS, 128)[pair] for pair in range(8)], 1)


def leave_kernel(returned_ref, tokens_ref, grad_after_ref, w0, w1, w2, w3, *rest):
    out_ref, total_ref = rest[-2:]
    step = pl.program_id(0)
    product = dot_nt(whole_rows(returned_ref), joined((w0, w1, w2, w3)))

    @pl.when(step == 0)
    def _():
        total_ref[...] = product

    @pl.when(step > 0)
    def _():
        total_ref[...] += product

    @pl.when(step == 2)
    def _():
        grads = (
            grad_after_ref[...].astype(F32) + normalize_back(tokens_ref[...], total_ref[...])
        ).astype(BF)
        out_ref[...] = reorder(grads, "a", "o")


def leave(returned, tokens, grad_after, weights, waits=()):
    return pl.pallas_call(
        leave_kernel,
        grid=(3,),
        in_specs=[
            pl.BlockSpec((16, 1, 128, 128), lambda i: (0, i, 0, 0)),
            fixed((ROWS, D)),
            fixed((ROWS, D)),
        ]
        + weight_specs(lambda i: i)
        + [unused] * len(waits),
        out_specs=fixed((ROWS, D)),
        out_shape=jax.ShapeDtypeStruct((ROWS, D), BF),
        scratch_shapes=[pltpu.VMEM((ROWS, D), F32)],
        compiler_params=params(52),
        cost_estimate=cost(3 * 2 * ROWS * D * D, 9 * MIB),
        name="leave",
    )(returned, tokens, grad_after, *[weights] * 4, *waits)


CORE, MODE, CHIP, Z, YLO, X, YHI = range(7)


def swap(values, axis, bits):
    size = lax.axis_size(axis)
    return lax.ppermute(values, axis, [(n, n ^ bits) for n in range(size)])


def swap_all(parts, axis, bit):
    return [parts[0]] + [swap(parts[o], axis, o * bit) for o in range(1, 4)]


def prefetched(kernel, ids, operands, in_specs, out_specs, out_shape, name, grid=(), scratch=()):
    return pl.pallas_call(
        kernel,
        grid_spec=pltpu.PrefetchScalarGridSpec(
            num_scalar_prefetch=1,
            grid=grid,
            in_specs=in_specs,
            out_specs=out_specs,
            scratch_shapes=list(scratch),
        ),
        out_shape=out_shape,
        compiler_params=params(),
        cost_estimate=cost(1e9, 5 * MIB),
        name=name,
    )(ids, *operands)


def rows_of(values, start, count):
    return values[pl.ds(pl.multiple_of(start, count), count), :]


def early_kernel(add, ids_ref, hidden_ref, mixed_ref, grads_ref, last_ref, *rest):
    step = pl.program_id(0)

    def finish(first, second, right):
        product = dot_tn(jnp.concatenate([first, second], 1), right)
        if add:
            arrived_ref, total_ref = rest[0], rest[-1]
            total_ref[...] = product + arrived_ref[0].astype(F32)
            for partner, out_ref in enumerate(rest[-5:-1]):
                out_ref[0] = rows_of(total_ref, (ids_ref[Z] ^ partner) * 64, 64).astype(BF)
        else:
            rest[-1][0] = product.astype(BF)

    @pl.when(step < 6)
    def _():
        right = jnp.concatenate([grads_ref[pair, 0] for pair in range(8)], 1)
        finish(hidden_ref[0], hidden_ref[1], right)

    @pl.when(step >= 6)
    def _():
        finish(mixed_ref[0, 0], mixed_ref[1, 0], last_ref[...])


def early_products(ids, hidden, returned, last, arrived=None, waits=()):
    def feature(i, ids_ref):
        return 2 * (i % 2) + ids_ref[CORE]

    in_specs = [
        pl.BlockSpec((2, ROWS, 128), lambda i, c: (feature(i, c), 0, 0)),
        pl.BlockSpec((2, 1, ROWS, 128), lambda i, c: (feature(i, c), 0, 0, 0)),
        pl.BlockSpec((8, 1, ROWS, 128), lambda i, c: (0, jnp.minimum(i // 2, 2) + 1, 0, 0)),
        pl.BlockSpec((ROWS, D), lambda i, c: (0, 0)),
    ]
    operands = [hidden, returned, returned, last]
    if arrived is None:
        return prefetched(
            functools.partial(early_kernel, False), ids, operands + list(waits),
            in_specs + [unused] * len(waits),
            pl.BlockSpec((1, ROWS, D), lambda i, c: (i, 0, 0)),
            jax.ShapeDtypeStruct((8, ROWS, D), BF), "early_first", (8,),
        )
    return prefetched(
        functools.partial(early_kernel, True), ids, operands + [arrived, *waits],
        in_specs + [pl.BlockSpec((1, ROWS, D), lambda i, c: (i, 0, 0))] + [unused] * len(waits),
        [pl.BlockSpec((1, 64, D), lambda i, c: (i, 0, 0))] * 4,
        [jax.ShapeDtypeStruct((8, 64, D), BF)] * 4, "early_add", (8,),
        [pltpu.VMEM((ROWS, D), F32)],
    )


def sum_split_kernel(split, count, inputs, ids_ref, *refs):
    total_ref = refs[-1]
    total = refs[0][0].astype(F32)
    for ref in refs[1:inputs]:
        total += ref[0].astype(F32)
    total_ref[...] = total
    share = total_ref.shape[0] // count
    for partner, out_ref in enumerate(refs[inputs:-1]):
        out_ref[0] = rows_of(total_ref, (ids_ref[split] ^ partner) * share, share).astype(BF)


def sum_split(ids, parts, split, count, name):
    blocks, rows, columns = parts[0].shape
    return prefetched(
        functools.partial(sum_split_kernel, split, count, len(parts)), ids, parts,
        [pl.BlockSpec((1, rows, columns), lambda i, c: (i, 0, 0))] * len(parts),
        [pl.BlockSpec((1, rows // count, columns), lambda i, c: (i, 0, 0))] * count,
        [jax.ShapeDtypeStruct((blocks, rows // count, columns), BF)] * count, name, (blocks,),
        [pltpu.VMEM((rows, columns), F32)],
    )


def early_chips_kernel(ids_ref, own_ref, arrived_ref, *rest):
    for partner, out_ref in enumerate(rest[-4:]):
        for n in range(2):
            block = (ids_ref[X] ^ partner) * 2 + n
            out_ref[n] = (own_ref[block].astype(F32) + arrived_ref[block].astype(F32)).astype(BF)


def early_last_kernel(ids_ref, *refs):
    for partner, out_ref in enumerate(refs[4:]):
        block = ids_ref[YHI] ^ partner
        total = refs[0][block].astype(F32)
        for ref in refs[1:4]:
            total += ref[block].astype(F32)
        out_ref[...] = total.astype(BF)


def early_sums(ids, parts, waits):
    keep, give = sum_split(ids, parts, YLO, 2, "early_z")
    arrived = swap(give, "mode", 1)
    whole = pl.BlockSpec(memory_space=pltpu.VMEM)
    parts = prefetched(
        early_chips_kernel, ids, [keep, arrived, *waits],
        [whole] * 2 + [unused] * len(waits), [whole] * 4,
        [jax.ShapeDtypeStruct((2, 32, D), BF)] * 4, "early_chips",
    )
    keep, give = prefetched(
        early_last_kernel, ids, swap_all(parts, "agent", 4), [whole] * 4, [whole] * 2,
        [jax.ShapeDtypeStruct((32, D), BF)] * 2, "early_last",
    )
    return keep.astype(F32) + swap(give, "agent", 2).astype(F32)


WIDE = 384 + D


def gather_hidden(keep, give):
    chip = jnp.concatenate([keep, swap(give, "agent", 1)], 0)
    here = jnp.stack([chip, swap(chip, "agent", 2)])
    return here


def late_kernel(ids_ref, *refs):
    hiddens, first_ref, second_ref, mixed_ref, after_ref, mine_ref, theirs_ref, total_ref = (
        refs[:4],
        *refs[4:8],
        *refs[-3:],
    )
    step = pl.program_id(0)
    core = ids_ref[CORE]

    @pl.when(step == 0)
    def _():
        total_ref[...] = jnp.zeros_like(total_ref)

    for partner, ref in enumerate(hiddens):

        @pl.when(step // 2 == partner)
        def _(ref=ref):
            right = jnp.concatenate(
                [
                    jnp.concatenate([source[0, slot] for slot in range(3)], 1)
                    for source in (first_ref, second_ref)
                ],
                0,
            )
            total_ref[...] += dot_tn(right, ref[0])

    for block in range(4):

        @pl.when(step == 8 + block)
        def _(block=block):
            rows = total_ref[:, 256 * block : 256 * block + 256].T.astype(BF)
            left = jnp.concatenate([mixed_ref[0], mixed_ref[1]], 1)
            other = dot_tn(left, after_ref[...]).astype(BF)

            @pl.when(core == block % 2)
            def _():
                mine_ref[block // 2, :, :384] = rows
                mine_ref[block // 2, :, 384:] = other

            @pl.when(core != block % 2)
            def _():
                theirs_ref[block // 2, :, :384] = rows
                theirs_ref[block // 2, :, 384:] = other


def late_products(ids, hiddens, grads, mixed, grad_after, waits):
    def source(i, c, other):
        chip = (c[X] ^ jnp.minimum(i // 2, 3)) * 2 + (c[YHI] ^ (i % 2))
        return 2 * chip + (c[CORE] ^ other)

    in_specs = [
        pl.BlockSpec((1, ROWS, D), lambda i, c, o=o: (jnp.clip(i - 2 * o, 0, 1), 0, 0))
        for o in range(4)
    ]
    in_specs += [
        pl.BlockSpec((1, 3, 128, 128), lambda i, c, o=o: (source(i, c, o), 0, 0, 0))
        for o in range(2)
    ]
    in_specs += [
        pl.BlockSpec((2, ROWS, 128), lambda i, c: (jnp.clip(i - 8, 0, 3), 0, 0)),
        pl.BlockSpec((ROWS, D), lambda i, c: (0, 0)),
    ]
    return prefetched(
        late_kernel, ids, list(hiddens) + [grads, grads, mixed, grad_after, *waits],
        in_specs + [unused] * len(waits),
        [pl.BlockSpec((2, ROWS, WIDE), lambda i, c: (0, 0, 0))] * 2,
        [jax.ShapeDtypeStruct((2, ROWS, WIDE), BF)] * 2, "late_products", (12,),
        [pltpu.VMEM((384, D), F32)],
    )


def late_chips_kernel(ids_ref, own_ref, arrived_ref, *rest):
    outs, total_ref = rest[:-1], rest[-1]
    total_ref[...] = own_ref[...].astype(F32) + arrived_ref[...].astype(F32)
    for partner, out_ref in enumerate(outs):
        slot = jnp.minimum(ids_ref[X] ^ partner, 2)
        lanes = pl.ds(pl.multiple_of(slot * 128, 128), 128)
        out_ref[:, :, :128] = total_ref[:, :, lanes].astype(BF)
        out_ref[:, :, 128:] = total_ref[:, :, 384:].astype(BF)


def late_turn_kernel(ids_ref, *refs):
    for other, out_ref in enumerate(refs[4:]):
        row = ids_ref[YHI] ^ other
        total = refs[0][row, :, 128:].astype(F32)
        for ref in refs[1:4]:
            total += ref[row, :, 128:].astype(F32)
        for partner, ref in enumerate(refs[:4]):
            out_ref[partner, :, :128] = ref[row, :, :128]
            out_ref[partner, :, 128:] = total[:, 256 * partner : 256 * partner + 256].astype(BF)


def late_last_kernel(ids_ref, keep_ref, arrived_ref, out_ref):
    @pl.when(ids_ref[X] < 3)
    def _():
        for other, ref in enumerate((keep_ref, arrived_ref)):
            for partner in range(4):
                pair = (ids_ref[X] ^ partner) * 2 + (ids_ref[YHI] ^ other)
                lanes = pl.ds(pl.multiple_of(pair * 128, 128), 128)
                out_ref[:, lanes] = ref[partner, :, :128].astype(F32)

    @pl.when(ids_ref[X] == 3)
    def _():
        for partner in range(4):
            out_ref[:, 256 * partner : 256 * partner + 256] = keep_ref[partner, :, 128:].astype(
                F32
            ) + arrived_ref[partner, :, 128:].astype(F32)


def late_sums(ids, mine, theirs):
    whole = pl.BlockSpec(memory_space=pltpu.VMEM)
    parts = sum_split(ids, [mine, swap(theirs, "agent", 1)], Z, 4, "late_add")
    keep, give = sum_split(ids, swap_all(parts, "mode", 2), YLO, 2, "late_z")
    parts = prefetched(
        late_chips_kernel, ids, [keep, swap(give, "mode", 1)], [whole] * 2, [whole] * 4,
        [jax.ShapeDtypeStruct((2, 32, 128 + D), BF)] * 4, "late_chips", (),
        [pltpu.VMEM((2, 32, WIDE), F32)],
    )
    keep, give = prefetched(
        late_turn_kernel, ids, swap_all(parts, "agent", 4), [whole] * 4, [whole] * 2,
        [jax.ShapeDtypeStruct((4, 32, 384), BF)] * 2, "late_turn",
    )
    return prefetched(
        late_last_kernel, ids, [keep, swap(give, "agent", 2)], [whole] * 2, whole,
        jax.ShapeDtypeStruct((32, D), F32), "late_last",
    )


def exchange(values, axis):
    return lax.all_to_all(values, axis, split_axis=0, concat_axis=0, tiled=True)


def local(tokens, cotangent, weights, agent_mask):
    agent, mode = lax.axis_index("agent"), lax.axis_index("mode")
    ids = jnp.stack(
        [agent & 1, mode, agent >> 1, mode >> 1, mode & 1, agent >> 2, (agent >> 1) & 1]
    ).astype(jnp.int32)
    other_ids = ids.at[CORE].set(1 - ids[CORE])
    token_rows = tokens.reshape(ROWS, D)
    grad_rows = cotangent.reshape(ROWS, D)
    offset = jnp.where(agent_mask == 1, 0.0, masked_score).astype(F32).reshape(1, 128)

    outgoing, tokens_a, hidden_keep, hidden_give = enter(ids, token_rows, weights)
    arrived_one = exchange(outgoing, "agent")
    hidden_here = gather_hidden(hidden_keep, hidden_give)
    mixed, tables = agent_forward(arrived_one, offset)
    mixed_one = exchange(mixed, "agent").reshape(8, ROWS, 128)
    outgoing, after, hidden_two, cotangent_m = middle(
        tokens_a, mixed_one, grad_rows, weights, [hidden_here]
    )
    arrived_two = exchange(outgoing.reshape(8, 1024, 128), "mode").reshape(8, 4, ROWS, 128)
    hiddens = [hidden_here] + [swap(hidden_here, "agent", 4 * o) for o in range(1, 4)]
    returning = mode_attention(arrived_two, hiddens[1::2])
    returned_two = exchange(returning.reshape(8, 1024, 128), "mode").reshape(8, 4, ROWS, 128)
    early = (hidden_two, returned_two, cotangent_m)
    theirs = early_products(other_ids, *early, None, hiddens[2:3])
    outgoing, grad_after = turn(returned_two, cotangent_m, after, weights, [theirs])
    parts = early_products(ids, *early, swap(theirs, "agent", 1), [grad_after])
    upstream = exchange(outgoing, "agent")
    returning = agent_backward(arrived_one, upstream, tables, parts[:1])
    parts = swap_all(parts, "mode", 2)
    returned_one = exchange(returning.reshape(16, 384, 128), "agent").reshape(16, 3, 128, 128)
    late_parts = late_products(ids, hiddens, returning, mixed_one, grad_after, parts[1::2])
    token_grads = leave(returned_one, tokens_a, grad_after, weights)
    agent_weight_grads = late_sums(ids, *late_parts)
    mode_weight_grads = early_sums(ids, parts, [token_grads])
    return (token_grads.reshape(tokens.shape), agent_weight_grads, mode_weight_grads)


def solution(mesh):
    placed = (P("agent", "mode", None, None), P("agent", "mode", None, None), P(), P())
    return jax.shard_map(
        local,
        mesh=mesh,
        in_specs=placed,
        out_specs=(
            P("agent", "mode", None, None),
            P(("agent", "mode"), None),
            P(("agent", "mode"), None),
        ),
        check_vma=False,
    )
```

```python
import functools

import jax
import jax.numpy as jnp
from jax import lax
from jax.experimental import pallas as pl
from jax.experimental.pallas import tpu as pltpu
from jax.sharding import PartitionSpec as P

epsilon = 1e-06
masked_score = -1000000000.0

BF = jnp.bfloat16
F32 = jnp.float32
D = 1024
ROWS = 256
SCALE = 0.125
MIB = 1024 * 1024


def decode(row, order):
    if order == "o":
        return row >> 5, (row >> 2) & 7, row & 3
    if order == "a":
        return row & 7, row >> 5, (row >> 3) & 3
    return (row >> 3) & 7, row & 7, row >> 6


def encode(agent, mode, step, order):
    if order == "o":
        return agent * 32 + mode * 4 + step
    if order == "a":
        return mode * 32 + step * 8 + agent
    return step * 64 + agent * 8 + mode


def reorder(values, source, target):
    rows = lax.broadcasted_iota(jnp.int32, (ROWS, ROWS), 0)
    columns = lax.broadcasted_iota(jnp.int32, (ROWS, ROWS), 1)
    chosen = encode(*decode(rows, target), source)
    table = (chosen == columns).astype(F32).astype(BF)
    return jnp.dot(table, values, preferred_element_type=F32).astype(BF)


def dot_nt(left, right):
    return lax.dot_general(left, right, (((1,), (1,)), ((), ())), preferred_element_type=F32)


def dot_tn(left, right):
    return lax.dot_general(left, right, (((0,), (0,)), ((), ())), preferred_element_type=F32)


def factor_of(wide):
    return lax.rsqrt(jnp.mean(wide * wide, -1, keepdims=True) + epsilon)


def normalize_back(values, upstream):
    wide = values.astype(F32)
    factor = factor_of(wide)
    normed = wide * factor
    return factor * (upstream - normed * jnp.mean(upstream * normed, -1, keepdims=True))


def weight_specs(slot):
    return [pl.BlockSpec((1, 256, D), lambda i, *c, q=q: (slot(i), q, 0)) for q in range(4)]


def joined(refs):
    return jnp.concatenate([ref[0] for ref in refs], 0)


def params(limit=32):
    return pltpu.CompilerParams(vmem_limit_bytes=limit * MIB)


def cost(flops, read):
    return pl.CostEstimate(flops=int(flops), bytes_accessed=int(read), transcendentals=0)


unused = pl.BlockSpec(memory_space=pl.ANY)


def fixed(shape):
    return pl.BlockSpec(shape, lambda *i: (0,) * len(shape))


def stack_heads(values):
    lanes = lax.broadcasted_iota(jnp.int32, (1, 128), 1)
    first = (lanes < 64).astype(F32).astype(BF)
    second = (lanes >= 64).astype(F32).astype(BF)
    return jnp.concatenate([values * first, values * second], 0)


def beside(table):
    return jnp.concatenate([table[:128], table[128:]], 1)


def probabilities(query_stack, keys, offset):
    scores = dot_nt(query_stack, keys) * SCALE + offset
    raised = jnp.exp(scores - jnp.max(scores, -1, keepdims=True))
    return raised / jnp.sum(raised, -1, keepdims=True)


def attend(table, values):
    return jnp.dot(beside(table.astype(BF)), stack_heads(values), preferred_element_type=F32)


def attention_back(table, query_stack, keys, values, upstream):
    upstream_stack = stack_heads(upstream)
    through = dot_nt(upstream_stack, values)
    value_grad = dot_tn(table.astype(BF), upstream_stack)
    centre = jnp.sum(through * table, -1, keepdims=True)
    score_grad = (table * (through - centre) * SCALE).astype(BF)
    query_grad = jnp.dot(beside(score_grad), stack_heads(keys), preferred_element_type=F32)
    keys_grad = dot_tn(score_grad, query_stack)
    return query_grad, keys_grad, value_grad


def enter_kernel(
    ids_ref, tokens_ref, w0, w1, w2, w3,
    send_ref, tokens_out_ref, keep_ref, give_ref, hidden_ref,
):
    step = pl.program_id(0)

    @pl.when(step == 0)
    def _():
        rows = reorder(tokens_ref[...], "o", "a")
        tokens_out_ref[...] = rows
        wide = rows.astype(F32)
        hidden = (wide * factor_of(wide)).astype(BF)
        hidden_ref[...] = hidden
        core = ids_ref[0]

        @pl.when(core == 0)
        def _():
            keep_ref[...] = hidden[:128]
            give_ref[...] = hidden[128:]

        @pl.when(core == 1)
        def _():
            keep_ref[...] = hidden[128:]
            give_ref[...] = hidden[:128]

    weights = joined((w0, w1, w2, w3))
    result = jnp.dot(hidden_ref[...], weights, preferred_element_type=F32).astype(BF)
    for pair in range(8):
        for half in range(2):
            send_ref[2 * pair + half] = result[
                128 * half : 128 * half + 128, 128 * pair : 128 * pair + 128
            ]


def enter(ids, tokens, weights):
    return pl.pallas_call(
        enter_kernel,
        grid_spec=pltpu.PrefetchScalarGridSpec(
            num_scalar_prefetch=1,
            grid=(3,),
            in_specs=[fixed((ROWS, D))] + weight_specs(lambda i: i),
            out_specs=[
                pl.BlockSpec((16, 128, 128), lambda i, c: (0, i, 0)),
                fixed((ROWS, D)),
                fixed((128, D)),
                fixed((128, D)),
            ],
            scratch_shapes=[pltpu.VMEM((ROWS, D), BF)],
        ),
        out_shape=[
            jax.ShapeDtypeStruct((16, 384, 128), BF),
            jax.ShapeDtypeStruct((ROWS, D), BF),
            jax.ShapeDtypeStruct((128, D), BF),
            jax.ShapeDtypeStruct((128, D), BF),
        ],
        compiler_params=params(52),
        cost_estimate=cost(3 * 2 * ROWS * D * D, 8 * MIB),
        name="enter",
    )(ids, tokens, *[weights] * 4)


def agent_rows(block, step):
    return block[:, 8 * step : 8 * step + 8, :].reshape(128, 128).astype(BF)


def agent_forward_kernel(query_ref, keys_ref, values_ref, offset_ref, out_ref, table_ref):
    query = query_ref[...].astype(F32)
    keys = keys_ref[...].astype(F32)
    values = values_ref[...].astype(F32)
    offset = offset_ref[...]
    outs = []
    for step in range(4):
        table = probabilities(
            stack_heads(agent_rows(query, step)), agent_rows(keys, step), offset
        )
        table_ref[0, step] = table
        outs.append(attend(table, agent_rows(values, step)).reshape(16, 8, 128))
    out_ref[...] = jnp.concatenate(outs, 1).astype(BF)


def agent_specs():
    return [pl.BlockSpec((16, 32, 128), lambda i, k=k: (0, 4 * k + i, 0)) for k in range(3)]


def agent_forward(arrived, offset):
    return pl.pallas_call(
        agent_forward_kernel,
        grid=(4,),
        in_specs=agent_specs() + [fixed((1, 128))],
        out_specs=[
            pl.BlockSpec((16, 32, 128), lambda i: (0, i, 0)),
            pl.BlockSpec((1, 4, 256, 128), lambda i: (i, 0, 0, 0)),
        ],
        out_shape=[
            jax.ShapeDtypeStruct((16, 128, 128), BF),
            jax.ShapeDtypeStruct((4, 4, 256, 128), F32),
        ],
        compiler_params=params(),
        cost_estimate=cost(3e9, 4 * MIB),
        name="agent_forward",
    )(arrived, arrived, arrived, offset)


def agent_backward_kernel(
    query_ref, keys_ref, values_ref, upstream_ref, table_ref, query_out, keys_out, values_out
):
    query = query_ref[...].astype(F32)
    keys = keys_ref[...].astype(F32)
    values = values_ref[...].astype(F32)
    upstream = upstream_ref[...].astype(F32)
    outs = [[], [], []]
    for step in range(4):
        grads = attention_back(
            table_ref[0, step],
            stack_heads(agent_rows(query, step)),
            agent_rows(keys, step),
            agent_rows(values, step),
            agent_rows(upstream, step),
        )
        for kept, grad in zip(outs, grads):
            kept.append(grad.reshape(16, 8, 128))
    for ref, kept in zip((query_out, keys_out, values_out), outs):
        ref[...] = jnp.concatenate(kept, 1).astype(BF)


def agent_backward_all_kernel(q, k, v, g, table_ref, *rest):
    out_ref = rest[-1]
    agent_backward_kernel(
        q,
        k,
        v,
        g,
        table_ref,
        out_ref.at[:, 0],
        out_ref.at[:, 1],
        out_ref.at[:, 2],
    )


def agent_backward(arrived, upstream, tables, waits=()):
    return pl.pallas_call(
        agent_backward_all_kernel,
        grid=(4,),
        in_specs=agent_specs()
        + [
            pl.BlockSpec((16, 32, 128), lambda i: (0, i, 0)),
            pl.BlockSpec((1, 4, 256, 128), lambda i: (i, 0, 0, 0)),
        ]
        + [unused] * len(waits),
        out_specs=pl.BlockSpec((16, 3, 32, 128), lambda i: (0, 0, i, 0)),
        out_shape=jax.ShapeDtypeStruct((16, 3, 128, 128), BF),
        compiler_params=params(),
        cost_estimate=cost(6e9, 6 * MIB),
        name="agent_backward",
    )(arrived, arrived, arrived, upstream, tables, *waits)


def middle_kernel(
    tokens_ref, mixed_ref, cotangent_ref, w0, w1, w2, w3, *rest
):
    send_ref, after_ref, hidden_out_ref, cotangent_out_ref, hidden_ref = rest[-5:]
    quarters = (w0, w1, w2, w3)
    step = pl.program_id(0)

    @pl.when(step == 0)
    def _():
        mixed = jnp.concatenate([mixed_ref[pair] for pair in range(8)], 1)
        after = (
            tokens_ref[...].astype(F32)
            + jnp.dot(mixed, joined(quarters), preferred_element_type=F32)
        ).astype(BF)
        after = reorder(after, "a", "m")
        after_ref[...] = after
        wide = after.astype(F32)
        hidden = (wide * factor_of(wide)).astype(BF)
        hidden_ref[...] = hidden
        for block in range(8):
            hidden_out_ref[block] = hidden[:, 128 * block : 128 * block + 128]
        cotangent_out_ref[...] = reorder(cotangent_ref[...], "o", "m")

    def send(result):
        result = result.astype(BF)
        for pair in range(8):
            send_ref[pair, 0] = result[:, 128 * pair : 128 * pair + 128]

    @pl.when((step > 0) & (step < 4))
    def _():
        send(jnp.dot(hidden_ref[...], joined(quarters), preferred_element_type=F32))

    @pl.when(step == 4)
    def _():
        send(dot_nt(cotangent_out_ref[...], joined(quarters)))


def middle(tokens, mixed, cotangent, weights, waits=()):
    return pl.pallas_call(
        middle_kernel,
        grid=(5,),
        in_specs=[
            fixed((ROWS, D)),
            fixed((8, ROWS, 128)),
            fixed((ROWS, D)),
        ]
        + weight_specs(lambda i: 3 + i)
        + [unused] * len(waits),
        out_specs=[
            pl.BlockSpec((8, 1, ROWS, 128), lambda i: (0, jnp.maximum(i - 1, 0), 0, 0)),
            fixed((ROWS, D)),
            fixed((8, ROWS, 128)),
            fixed((ROWS, D)),
        ],
        out_shape=[
            jax.ShapeDtypeStruct((8, 4, ROWS, 128), BF),
            jax.ShapeDtypeStruct((ROWS, D), BF),
            jax.ShapeDtypeStruct((8, ROWS, 128), BF),
            jax.ShapeDtypeStruct((ROWS, D), BF),
        ],
        scratch_shapes=[pltpu.VMEM((ROWS, D), BF)],
        compiler_params=params(52),
        cost_estimate=cost(5 * 2 * ROWS * D * D, 13 * MIB),
        name="middle",
    )(tokens, mixed, cotangent, *[weights] * 4, *waits)


def mode_kernel(arrived_ref, *rest):
    out_ref = rest[-1]
    rows = lax.broadcasted_iota(jnp.int32, (256, 128), 0)
    columns = lax.broadcasted_iota(jnp.int32, (256, 128), 1)
    same = ((rows >> 6) & 1) == (columns >> 6)
    offset = jnp.where(same, 0.0, -1e30).astype(F32)
    for pair in range(4):

        def take(which):
            block = arrived_ref[:, which, 16 * pair : 16 * pair + 16, :].astype(F32)
            parts = [block[:, 8 * n : 8 * n + 8, :].reshape(64, 128) for n in range(2)]
            return jnp.concatenate(parts, 0).astype(BF)

        query, keys, values, upstream = (take(which) for which in range(4))
        query_stack = stack_heads(query)
        table = probabilities(query_stack, keys, offset)
        results = (attend(table, values),) + attention_back(
            table, query_stack, keys, values, upstream
        )
        for which, result in enumerate(results):
            parts = [result[64 * n : 64 * n + 64].reshape(8, 8, 128) for n in range(2)]
            out_ref[:, which, 16 * pair : 16 * pair + 16, :] = jnp.concatenate(parts, 1).astype(BF)


def mode_attention(arrived, after=()):
    spec = pl.BlockSpec((8, 4, 64, 128), lambda i: (0, 0, i, 0))
    return pl.pallas_call(
        mode_kernel,
        grid=(4,),
        in_specs=[spec] + [unused] * len(after),
        out_specs=spec,
        out_shape=jax.ShapeDtypeStruct((8, 4, ROWS, 128), BF),
        compiler_params=params(),
        cost_estimate=cost(8e9, 4 * MIB),
        name="mode_attention",
    )(arrived, *after)


def turn_kernel(returned_ref, cotangent_ref, after_ref, w0, w1, w2, w3, *rest):
    quarters = (w0, w1, w2, w3)
    send_ref, grad_after_ref, total_ref = rest[-3:]
    step = pl.program_id(0)

    @pl.when(step < 3)
    def _():
        grads = jnp.concatenate([returned_ref[pair, 0] for pair in range(8)], 1)
        product = dot_nt(grads, joined(quarters))

        @pl.when(step == 0)
        def _():
            total_ref[...] = product

        @pl.when(step > 0)
        def _():
            total_ref[...] += product

    @pl.when(step == 3)
    def _():
        grad_after = (
            cotangent_ref[...].astype(F32) + normalize_back(after_ref[...], total_ref[...])
        ).astype(BF)
        grad_after = reorder(grad_after, "m", "a")
        grad_after_ref[...] = grad_after
        result = dot_nt(grad_after, joined(quarters)).astype(BF)
        for pair in range(8):
            for half in range(2):
                send_ref[2 * pair + half] = result[
                    128 * half : 128 * half + 128, 128 * pair : 128 * pair + 128
                ]


def turn(returned, cotangent, after, weights, waits=()):
    return pl.pallas_call(
        turn_kernel,
        grid=(4,),
        in_specs=[
            pl.BlockSpec((8, 1, ROWS, 128), lambda i: (0, jnp.minimum(i + 1, 3), 0, 0)),
            fixed((ROWS, D)),
            fixed((ROWS, D)),
        ]
        + weight_specs(lambda i: jnp.where(i < 3, i + 4, 3))
        + [unused] * len(waits),
        out_specs=[fixed((16, 128, 128)), fixed((ROWS, D))],
        out_shape=[
            jax.ShapeDtypeStruct((16, 128, 128), BF),
            jax.ShapeDtypeStruct((ROWS, D), BF),
        ],
        scratch_shapes=[pltpu.VMEM((ROWS, D), F32)],
        compiler_params=params(52),
        cost_estimate=cost(4 * 2 * ROWS * D * D, 12 * MIB),
        name="turn",
    )(returned, cotangent, after, *[weights] * 4, *waits)


def whole_rows(ref):
    return jnp.concatenate([ref[:, 0].reshape(8, ROWS, 128)[pair] for pair in range(8)], 1)


def leave_kernel(returned_ref, tokens_ref, grad_after_ref, w0, w1, w2, w3, *rest):
    out_ref, total_ref = rest[-2:]
    step = pl.program_id(0)
    product = dot_nt(whole_rows(returned_ref), joined((w0, w1, w2, w3)))

    @pl.when(step == 0)
    def _():
        total_ref[...] = product

    @pl.when(step > 0)
    def _():
        total_ref[...] += product

    @pl.when(step == 2)
    def _():
        grads = (
            grad_after_ref[...].astype(F32) + normalize_back(tokens_ref[...], total_ref[...])
        ).astype(BF)
        out_ref[...] = reorder(grads, "a", "o")


def leave(returned, tokens, grad_after, weights, waits=()):
    return pl.pallas_call(
        leave_kernel,
        grid=(3,),
        in_specs=[
            pl.BlockSpec((16, 1, 128, 128), lambda i: (0, i, 0, 0)),
            fixed((ROWS, D)),
            fixed((ROWS, D)),
        ]
        + weight_specs(lambda i: i)
        + [unused] * len(waits),
        out_specs=fixed((ROWS, D)),
        out_shape=jax.ShapeDtypeStruct((ROWS, D), BF),
        scratch_shapes=[pltpu.VMEM((ROWS, D), F32)],
        compiler_params=params(52),
        cost_estimate=cost(3 * 2 * ROWS * D * D, 9 * MIB),
        name="leave",
    )(returned, tokens, grad_after, *[weights] * 4, *waits)


CORE, MODE, CHIP, Z, YLO, X, YHI = range(7)


def swap(values, axis, bits):
    size = lax.axis_size(axis)
    return lax.ppermute(values, axis, [(n, n ^ bits) for n in range(size)])


def swap_all(parts, axis, bit):
    return [parts[0]] + [swap(parts[o], axis, o * bit) for o in range(1, 4)]


def prefetched(kernel, ids, operands, in_specs, out_specs, out_shape, name, grid=(), scratch=()):
    return pl.pallas_call(
        kernel,
        grid_spec=pltpu.PrefetchScalarGridSpec(
            num_scalar_prefetch=1,
            grid=grid,
            in_specs=in_specs,
            out_specs=out_specs,
            scratch_shapes=list(scratch),
        ),
        out_shape=out_shape,
        compiler_params=params(),
        cost_estimate=cost(1e9, 5 * MIB),
        name=name,
    )(ids, *operands)


def rows_of(values, start, count):
    return values[pl.ds(pl.multiple_of(start, count), count), :]


def early_kernel(add, ids_ref, hidden_ref, mixed_ref, grads_ref, last_ref, *rest):
    step = pl.program_id(0)

    def finish(first, second, right):
        product = dot_tn(jnp.concatenate([first, second], 1), right)
        if add:
            arrived_ref, total_ref = rest[0], rest[-1]
            total_ref[...] = product + arrived_ref[0].astype(F32)
            for columns in range(2):
                for give in range(2):
                    out_ref = rest[2 * columns + give - 5]
                    near, far = ((0, 3), (1, 2))[give] if columns == 0 else ((0, 1), (3, 2))[give]
                    for place, partner in enumerate((near, far)):
                        rows = rows_of(total_ref, (ids_ref[Z] ^ partner) * 64, 64)
                        out_ref[0, 64 * place : 64 * place + 64] = rows[
                            :, 512 * columns : 512 * columns + 512
                        ].astype(BF)
        else:
            rest[-1][0] = product.astype(BF)

    @pl.when(step < 6)
    def _():
        right = jnp.concatenate([grads_ref[pair, 0] for pair in range(8)], 1)
        finish(hidden_ref[0], hidden_ref[1], right)

    @pl.when(step >= 6)
    def _():
        finish(mixed_ref[0, 0], mixed_ref[1, 0], last_ref[...])


def early_products(ids, hidden, returned, last, arrived=None, waits=()):
    def feature(i, ids_ref):
        return 2 * (i % 2) + ids_ref[CORE]

    in_specs = [
        pl.BlockSpec((2, ROWS, 128), lambda i, c: (feature(i, c), 0, 0)),
        pl.BlockSpec((2, 1, ROWS, 128), lambda i, c: (feature(i, c), 0, 0, 0)),
        pl.BlockSpec((8, 1, ROWS, 128), lambda i, c: (0, jnp.minimum(i // 2, 2) + 1, 0, 0)),
        pl.BlockSpec((ROWS, D), lambda i, c: (0, 0)),
    ]
    operands = [hidden, returned, returned, last]
    if arrived is None:
        return prefetched(
            functools.partial(early_kernel, False), ids, operands + list(waits),
            in_specs + [unused] * len(waits),
            pl.BlockSpec((1, ROWS, D), lambda i, c: (i, 0, 0)),
            jax.ShapeDtypeStruct((8, ROWS, D), BF), "early_first", (8,),
        )
    return prefetched(
        functools.partial(early_kernel, True), ids, operands + [arrived, *waits],
        in_specs + [pl.BlockSpec((1, ROWS, D), lambda i, c: (i, 0, 0))] + [unused] * len(waits),
        [pl.BlockSpec((1, 128, 512), lambda i, c: (i, 0, 0))] * 4,
        [jax.ShapeDtypeStruct((8, 128, 512), BF)] * 4, "early_add", (8,),
        [pltpu.VMEM((ROWS, D), F32)],
    )


def sum_split_kernel(split, count, inputs, ids_ref, *refs):
    total_ref = refs[-1]
    total = refs[0][0].astype(F32)
    for ref in refs[1:inputs]:
        total += ref[0].astype(F32)
    total_ref[...] = total
    share = total_ref.shape[0] // count
    for partner, out_ref in enumerate(refs[-1 - count : -1]):
        out_ref[0] = rows_of(total_ref, (ids_ref[split] ^ partner) * share, share).astype(BF)


def sum_split(ids, parts, split, count, name, waits=()):
    blocks, rows, columns = parts[0].shape
    return prefetched(
        functools.partial(sum_split_kernel, split, count, len(parts)), ids, [*parts, *waits],
        [pl.BlockSpec((1, rows, columns), lambda i, c: (i, 0, 0))] * len(parts)
        + [unused] * len(waits),
        [pl.BlockSpec((1, rows // count, columns), lambda i, c: (i, 0, 0))] * count,
        [jax.ShapeDtypeStruct((blocks, rows // count, columns), BF)] * count, name, (blocks,),
        [pltpu.VMEM((rows, columns), F32)],
    )


def early_chips_kernel(ids_ref, own_ref, arrived_ref, *rest):
    for partner, out_ref in enumerate(rest[-4:]):
        for n in range(2):
            block = (ids_ref[X] ^ partner) * 2 + n
            out_ref[n] = (own_ref[block].astype(F32) + arrived_ref[block].astype(F32)).astype(BF)


def early_last_kernel(ids_ref, *refs):
    for partner, out_ref in enumerate(refs[4:]):
        block = ids_ref[YHI] ^ partner
        total = refs[0][block].astype(F32)
        for ref in refs[1:4]:
            total += ref[block].astype(F32)
        out_ref[...] = total.astype(BF)


def early_half_kernel(ids_ref, left_ref, left_in, right_ref, right_in, own_ref, *outs):
    for columns, (ref, arrived) in enumerate(((left_ref, left_in), (right_ref, right_in))):
        total = (ref[0].astype(F32) + arrived[0].astype(F32)).astype(BF)
        own_ref[0, :, 512 * columns : 512 * columns + 512] = total[:64]
        outs[columns][0] = total[64:]


def early_half(ids, parts):
    left, left_give, right, right_give = parts
    operands = [left, swap(left_give, "mode", 2), right, swap(right_give, "mode", 6)]
    narrow = pl.BlockSpec((1, 64, 512), lambda i, c: (i, 0, 0))
    return prefetched(
        early_half_kernel, ids, operands,
        [pl.BlockSpec((1, 128, 512), lambda i, c: (i, 0, 0))] * 4,
        [pl.BlockSpec((1, 64, D), lambda i, c: (i, 0, 0)), narrow, narrow],
        [jax.ShapeDtypeStruct((8, 64, D), BF)] + [jax.ShapeDtypeStruct((8, 64, 512), BF)] * 2,
        "early_half", (8,),
    )


def early_z_kernel(ids_ref, own_ref, left_ref, right_ref, keep_ref, give_ref):
    for other, out_ref in enumerate((keep_ref, give_ref)):
        first = pl.multiple_of((ids_ref[YLO] ^ other) * 32, 32)
        for columns, ref in enumerate((left_ref, right_ref)):
            lanes = slice(512 * columns, 512 * columns + 512)
            out_ref[:, :, lanes] = (
                own_ref[:, pl.ds(first, 32), lanes].astype(F32)
                + ref[:, pl.ds(first, 32), :].astype(F32)
            ).astype(BF)


def early_sums(ids, own, left, right, waits):
    narrow = pl.BlockSpec((2, 64, 512), lambda i, c: (i, 0, 0))
    keep, give = prefetched(
        early_z_kernel, ids, [own, left, right],
        [pl.BlockSpec((2, 64, D), lambda i, c: (i, 0, 0)), narrow, narrow],
        [pl.BlockSpec((2, 32, D), lambda i, c: (i, 0, 0))] * 2,
        [jax.ShapeDtypeStruct((8, 32, D), BF)] * 2, "early_z", (4,),
    )
    arrived = swap(give, "mode", 1)
    parts = prefetched(
        early_chips_kernel, ids, [keep, arrived, *waits],
        [fixed((8, 32, D))] * 2 + [unused] * len(waits), [fixed((2, 32, D))] * 4,
        [jax.ShapeDtypeStruct((2, 32, D), BF)] * 4, "early_chips", (1,),
    )
    keep, give = prefetched(
        early_last_kernel, ids, swap_all(parts, "agent", 4),
        [fixed((2, 32, D))] * 4, [fixed((32, D))] * 2,
        [jax.ShapeDtypeStruct((32, D), BF)] * 2, "early_last", (1,),
    )
    return keep.astype(F32) + swap(give, "agent", 2).astype(F32)


WIDE = 384 + D


def gather_hidden(keep, give):
    chip = jnp.concatenate([keep, swap(give, "agent", 1)], 0)
    here = jnp.stack([chip, swap(chip, "agent", 2)])
    return here


def late_kernel(ids_ref, *refs):
    hiddens, first_ref, second_ref, mixed_ref, after_ref, mine_ref, *theirs_refs, total_ref = (
        refs[:4],
        *refs[4:8],
        *refs[-4:],
    )
    step = pl.program_id(0)
    core = ids_ref[CORE]

    @pl.when(step == 0)
    def _():
        total_ref[...] = jnp.zeros_like(total_ref)

    for partner, ref in enumerate(hiddens):

        @pl.when(step // 2 == partner)
        def _(ref=ref):
            right = jnp.concatenate(
                [
                    jnp.concatenate([source[0, slot] for slot in range(3)], 1)
                    for source in (first_ref, second_ref)
                ],
                0,
            )
            total_ref[...] += dot_tn(right, ref[0])

    for block in range(4):

        @pl.when(step == 8 + block)
        def _(block=block):
            rows = total_ref[:, 256 * block : 256 * block + 256].T.astype(BF)
            left = jnp.concatenate([mixed_ref[0], mixed_ref[1]], 1)
            other = dot_tn(left, after_ref[...]).astype(BF)

            @pl.when(core == block % 2)
            def _():
                mine_ref[block // 2, :, :384] = rows
                mine_ref[block // 2, :, 384:] = other

            @pl.when(core != block % 2)
            def _():
                theirs_refs[block // 2][:, :384] = rows
                theirs_refs[block // 2][:, 384:] = other


def late_products(ids, hiddens, grads, mixed, grad_after, waits):
    def source(i, c, other):
        chip = (c[X] ^ jnp.minimum(i // 2, 3)) * 2 + (c[YHI] ^ (i % 2))
        return 2 * chip + (c[CORE] ^ other)

    in_specs = [
        pl.BlockSpec((1, ROWS, D), lambda i, c, o=o: (jnp.clip(i - 2 * o, 0, 1), 0, 0))
        for o in range(4)
    ]
    in_specs += [
        pl.BlockSpec((1, 3, 128, 128), lambda i, c, o=o: (source(i, c, o), 0, 0, 0))
        for o in range(2)
    ]
    in_specs += [
        pl.BlockSpec((2, ROWS, 128), lambda i, c: (jnp.clip(i - 8, 0, 3), 0, 0)),
        pl.BlockSpec((ROWS, D), lambda i, c: (0, 0)),
    ]
    return prefetched(
        late_kernel, ids, list(hiddens) + [grads, grads, mixed, grad_after, *waits],
        in_specs + [unused] * len(waits),
        [pl.BlockSpec((2, ROWS, WIDE), lambda i, c: (0, 0, 0))]
        + [pl.BlockSpec((ROWS, WIDE), lambda i, c: (0, 0))] * 2,
        [jax.ShapeDtypeStruct((2, ROWS, WIDE), BF)]
        + [jax.ShapeDtypeStruct((ROWS, WIDE), BF)] * 2, "late_products", (12,),
        [pltpu.VMEM((384, D), F32)],
    )


def late_chips_kernel(ids_ref, own_ref, arrived_ref, *rest):
    outs, total_ref = rest[:-1], rest[-1]
    total_ref[...] = own_ref[...].astype(F32) + arrived_ref[...].astype(F32)
    for partner, out_ref in enumerate(outs):
        slot = jnp.minimum(ids_ref[X] ^ partner, 2)
        lanes = pl.ds(pl.multiple_of(slot * 128, 128), 128)
        out_ref[:, :, :128] = total_ref[:, :, lanes].astype(BF)
        out_ref[:, :, 128:] = total_ref[:, :, 384:].astype(BF)


def late_turn_kernel(ids_ref, *refs):
    for other, out_ref in enumerate(refs[4:]):
        row = ids_ref[YHI] ^ other
        total = refs[0][row, :, 128:].astype(F32)
        for ref in refs[1:4]:
            total += ref[row, :, 128:].astype(F32)
        for partner, ref in enumerate(refs[:4]):
            out_ref[partner, :, :128] = ref[row, :, :128]
            out_ref[partner, :, 128:] = total[:, 256 * partner : 256 * partner + 256].astype(BF)


def late_last_kernel(ids_ref, keep_ref, arrived_ref, out_ref):
    @pl.when(ids_ref[X] < 3)
    def _():
        for other, ref in enumerate((keep_ref, arrived_ref)):
            for partner in range(4):
                pair = (ids_ref[X] ^ partner) * 2 + (ids_ref[YHI] ^ other)
                lanes = pl.ds(pl.multiple_of(pair * 128, 128), 128)
                out_ref[:, lanes] = ref[partner, :, :128].astype(F32)

    @pl.when(ids_ref[X] == 3)
    def _():
        for partner in range(4):
            out_ref[:, 256 * partner : 256 * partner + 256] = keep_ref[partner, :, 128:].astype(
                F32
            ) + arrived_ref[partner, :, 128:].astype(F32)


def late_add_kernel(ids_ref, mine_ref, first_ref, second_ref, *rest):
    total_ref = rest[-1]
    for block, ref in enumerate((first_ref, second_ref)):
        total_ref[...] = mine_ref[block].astype(F32) + ref[...].astype(F32)
        for partner, out_ref in enumerate(rest[-5:-1]):
            out_ref[block] = rows_of(total_ref, (ids_ref[Z] ^ partner) * 64, 64).astype(BF)


def late_sums(ids, mine, first, second, waits):
    parts = prefetched(
        late_add_kernel, ids,
        [mine, swap(first, "agent", 1), swap(second, "agent", 1), *waits],
        [fixed((2, ROWS, WIDE))] + [fixed((ROWS, WIDE))] * 2 + [unused] * len(waits),
        [fixed((2, 64, WIDE))] * 4,
        [jax.ShapeDtypeStruct((2, 64, WIDE), BF)] * 4, "late_add", (1,),
        [pltpu.VMEM((ROWS, WIDE), F32)],
    )
    keep, give = sum_split(ids, swap_all(parts, "mode", 2), YLO, 2, "late_z")
    parts = prefetched(
        late_chips_kernel, ids, [keep, swap(give, "mode", 1)],
        [fixed((2, 32, WIDE))] * 2, [fixed((2, 32, 128 + D))] * 4,
        [jax.ShapeDtypeStruct((2, 32, 128 + D), BF)] * 4, "late_chips", (1,),
        [pltpu.VMEM((2, 32, WIDE), F32)],
    )
    keep, give = prefetched(
        late_turn_kernel, ids, swap_all(parts, "agent", 4),
        [fixed((2, 32, 128 + D))] * 4, [fixed((4, 32, 384))] * 2,
        [jax.ShapeDtypeStruct((4, 32, 384), BF)] * 2, "late_turn", (1,),
    )
    return prefetched(
        late_last_kernel, ids, [keep, swap(give, "agent", 2)],
        [fixed((4, 32, 384))] * 2, fixed((32, D)),
        jax.ShapeDtypeStruct((32, D), F32), "late_last", (1,),
    )


def exchange(values, axis):
    return lax.all_to_all(values, axis, split_axis=0, concat_axis=0, tiled=True)


def local(tokens, cotangent, weights, agent_mask):
    agent, mode = lax.axis_index("agent"), lax.axis_index("mode")
    ids = jnp.stack(
        [agent & 1, mode, agent >> 1, mode >> 1, mode & 1, agent >> 2, (agent >> 1) & 1]
    ).astype(jnp.int32)
    other_ids = ids.at[CORE].set(1 - ids[CORE])
    token_rows = tokens.reshape(ROWS, D)
    grad_rows = cotangent.reshape(ROWS, D)
    offset = jnp.where(agent_mask == 1, 0.0, masked_score).astype(F32).reshape(1, 128)

    outgoing, tokens_a, hidden_keep, hidden_give = enter(ids, token_rows, weights)
    arrived_one = exchange(outgoing, "agent")
    hidden_here = gather_hidden(hidden_keep, hidden_give)
    mixed, tables = agent_forward(arrived_one, offset)
    mixed_one = exchange(mixed, "agent").reshape(8, ROWS, 128)
    outgoing, after, hidden_two, cotangent_m = middle(
        tokens_a, mixed_one, grad_rows, weights, [hidden_here]
    )
    arrived_two = exchange(outgoing.reshape(8, 1024, 128), "mode").reshape(8, 4, ROWS, 128)
    hiddens = [hidden_here] + [swap(hidden_here, "agent", 4 * o) for o in range(1, 4)]
    returning = mode_attention(arrived_two, hiddens[1::2])
    returned_two = exchange(returning.reshape(8, 1024, 128), "mode").reshape(8, 4, ROWS, 128)
    early = (hidden_two, returned_two, cotangent_m)
    theirs = early_products(other_ids, *early, None, hiddens[2:3])
    parts = early_products(ids, *early, swap(theirs, "agent", 1))
    outgoing, grad_after = turn(returned_two, cotangent_m, after, weights, parts[:1])
    upstream = exchange(outgoing, "agent")
    own, left, right = early_half(ids, parts)
    returning = agent_backward(arrived_one, upstream, tables, [own])
    left, right = swap(left, "mode", 6), swap(right, "mode", 2)
    returned_one = exchange(returning.reshape(16, 384, 128), "agent").reshape(16, 3, 128, 128)
    late_parts = late_products(
        ids, hiddens, returning, mixed_one, grad_after, [left, right]
    )
    token_grads = leave(returned_one, tokens_a, grad_after, weights)
    agent_weight_grads = late_sums(ids, *late_parts, [])
    mode_weight_grads = early_sums(ids, own, left, right, [token_grads])
    return (token_grads.reshape(tokens.shape), agent_weight_grads, mode_weight_grads)


def solution(mesh):
    placed = (P("agent", "mode", None, None), P("agent", "mode", None, None), P(), P())
    return jax.shard_map(
        local,
        mesh=mesh,
        in_specs=placed,
        out_specs=(
            P("agent", "mode", None, None),
            P(("agent", "mode"), None),
            P(("agent", "mode"), None),
        ),
        check_vma=False,
    )
```

```python
import functools

import jax
import jax.numpy as jnp
from jax import lax
from jax.experimental import pallas as pl
from jax.experimental.pallas import tpu as pltpu
from jax.sharding import PartitionSpec as P

epsilon = 1e-06
masked_score = -1000000000.0

BF = jnp.bfloat16
F32 = jnp.float32
D = 1024
ROWS = 256
SCALE = 0.125
MIB = 1024 * 1024


def decode(row, order):
    if order == "o":
        return row >> 5, (row >> 2) & 7, row & 3
    if order == "a":
        return row & 7, row >> 5, (row >> 3) & 3
    return (row >> 3) & 7, row & 7, row >> 6


def encode(agent, mode, step, order):
    if order == "o":
        return agent * 32 + mode * 4 + step
    if order == "a":
        return mode * 32 + step * 8 + agent
    return step * 64 + agent * 8 + mode


def reorder(values, source, target):
    rows = lax.broadcasted_iota(jnp.int32, (ROWS, ROWS), 0)
    columns = lax.broadcasted_iota(jnp.int32, (ROWS, ROWS), 1)
    chosen = encode(*decode(rows, target), source)
    table = (chosen == columns).astype(F32).astype(BF)
    return jnp.dot(table, values, preferred_element_type=F32).astype(BF)


def dot_nt(left, right):
    return lax.dot_general(left, right, (((1,), (1,)), ((), ())), preferred_element_type=F32)


def dot_tn(left, right):
    return lax.dot_general(left, right, (((0,), (0,)), ((), ())), preferred_element_type=F32)


def factor_of(wide):
    return lax.rsqrt(jnp.mean(wide * wide, -1, keepdims=True) + epsilon)


def normalize_back(values, upstream):
    wide = values.astype(F32)
    factor = factor_of(wide)
    normed = wide * factor
    return factor * (upstream - normed * jnp.mean(upstream * normed, -1, keepdims=True))


def fetch(slots, weights_ref, held_ref, sems_ref):
    copies = [
        pltpu.make_async_copy(weights_ref.at[slot], held_ref.at[n], sems_ref.at[n])
        for n, slot in enumerate(slots)
    ]
    step = pl.program_id(0)

    @pl.when(step == 0)
    def _():
        for copy in copies:
            copy.start()

    def ready():
        for n, copy in enumerate(copies):

            @pl.when(step == n)
            def _(copy=copy):
                copy.wait()

        return held_ref[step]

    return ready


def pinned(operand):
    return pltpu.with_memory_space_constraint(operand, pltpu.HBM)


def held(count):
    return [pltpu.VMEM((count, D, D), BF), pltpu.SemaphoreType.DMA((count,))]


def params(limit=32):
    return pltpu.CompilerParams(vmem_limit_bytes=limit * MIB)


def cost(flops, read):
    return pl.CostEstimate(flops=int(flops), bytes_accessed=int(read), transcendentals=0)


unused = pl.BlockSpec(memory_space=pl.ANY)


def fixed(shape):
    return pl.BlockSpec(shape, lambda *i: (0,) * len(shape))


def stack_heads(values):
    lanes = lax.broadcasted_iota(jnp.int32, (1, 128), 1)
    first = (lanes < 64).astype(F32).astype(BF)
    second = (lanes >= 64).astype(F32).astype(BF)
    return jnp.concatenate([values * first, values * second], 0)


def beside(table):
    return jnp.concatenate([table[:128], table[128:]], 1)


def probabilities(query_stack, keys, offset):
    scores = dot_nt(query_stack, keys) * SCALE + offset
    raised = jnp.exp(scores - jnp.max(scores, -1, keepdims=True))
    return raised / jnp.sum(raised, -1, keepdims=True)


def attend(table, values):
    return jnp.dot(beside(table.astype(BF)), stack_heads(values), preferred_element_type=F32)


def attention_back(table, query_stack, keys, values, upstream):
    upstream_stack = stack_heads(upstream)
    through = dot_nt(upstream_stack, values)
    value_grad = dot_tn(table.astype(BF), upstream_stack)
    centre = jnp.sum(through * table, -1, keepdims=True)
    score_grad = (table * (through - centre) * SCALE).astype(BF)
    query_grad = jnp.dot(beside(score_grad), stack_heads(keys), preferred_element_type=F32)
    keys_grad = dot_tn(score_grad, query_stack)
    return query_grad, keys_grad, value_grad


def enter_kernel(
    ids_ref, tokens_ref, weights_ref,
    send_ref, tokens_out_ref, keep_ref, give_ref, hidden_ref, held_ref, sems_ref,
):
    step = pl.program_id(0)
    ready = fetch((0, 1, 2), weights_ref, held_ref, sems_ref)

    @pl.when(step == 0)
    def _():
        rows = reorder(tokens_ref[...], "o", "a")
        tokens_out_ref[...] = rows
        wide = rows.astype(F32)
        hidden = (wide * factor_of(wide)).astype(BF)
        hidden_ref[...] = hidden
        core = ids_ref[0]

        @pl.when(core == 0)
        def _():
            keep_ref[...] = hidden[:128]
            give_ref[...] = hidden[128:]

        @pl.when(core == 1)
        def _():
            keep_ref[...] = hidden[128:]
            give_ref[...] = hidden[:128]

    result = jnp.dot(hidden_ref[...], ready(), preferred_element_type=F32).astype(BF)
    for pair in range(8):
        for half in range(2):
            send_ref[2 * pair + half] = result[
                128 * half : 128 * half + 128, 128 * pair : 128 * pair + 128
            ]


def enter(ids, tokens, weights):
    return pl.pallas_call(
        enter_kernel,
        grid_spec=pltpu.PrefetchScalarGridSpec(
            num_scalar_prefetch=1,
            grid=(3,),
            in_specs=[fixed((ROWS, D)), unused],
            out_specs=[
                pl.BlockSpec((16, 128, 128), lambda i, c: (0, i, 0)),
                fixed((ROWS, D)),
                fixed((128, D)),
                fixed((128, D)),
            ],
            scratch_shapes=[pltpu.VMEM((ROWS, D), BF)] + held(3),
        ),
        out_shape=[
            jax.ShapeDtypeStruct((16, 384, 128), BF),
            pltpu.HBM((ROWS, D), BF),
            pltpu.HBM((128, D), BF),
            jax.ShapeDtypeStruct((128, D), BF),
        ],
        compiler_params=params(45),
        cost_estimate=cost(3 * 2 * ROWS * D * D, 8 * MIB),
        name="enter",
    )(ids, tokens, pinned(weights))


def agent_rows(block, step):
    return block[:, 8 * step : 8 * step + 8, :].reshape(128, 128).astype(BF)


def agent_forward_kernel(query_ref, keys_ref, values_ref, offset_ref, out_ref, table_ref):
    query = query_ref[...].astype(F32)
    keys = keys_ref[...].astype(F32)
    values = values_ref[...].astype(F32)
    offset = offset_ref[...]
    outs = []
    for step in range(4):
        table = probabilities(
            stack_heads(agent_rows(query, step)), agent_rows(keys, step), offset
        )
        table_ref[0, step] = table
        outs.append(attend(table, agent_rows(values, step)).reshape(16, 8, 128))
    out_ref[...] = jnp.concatenate(outs, 1).astype(BF)


def agent_specs():
    return [pl.BlockSpec((16, 32, 128), lambda i, k=k: (0, 4 * k + i, 0)) for k in range(3)]


def agent_forward(arrived, offset):
    return pl.pallas_call(
        agent_forward_kernel,
        grid=(4,),
        in_specs=agent_specs() + [fixed((1, 128))],
        out_specs=[
            pl.BlockSpec((16, 32, 128), lambda i: (0, i, 0)),
            pl.BlockSpec((1, 4, 256, 128), lambda i: (i, 0, 0, 0)),
        ],
        out_shape=[
            jax.ShapeDtypeStruct((16, 128, 128), BF),
            pltpu.HBM((4, 4, 256, 128), F32),
        ],
        compiler_params=params(),
        cost_estimate=cost(3e9, 4 * MIB),
        name="agent_forward",
    )(arrived, arrived, arrived, offset)


def agent_backward_kernel(
    query_ref, keys_ref, values_ref, upstream_ref, table_ref, query_out, keys_out, values_out
):
    query = query_ref[...].astype(F32)
    keys = keys_ref[...].astype(F32)
    values = values_ref[...].astype(F32)
    upstream = upstream_ref[...].astype(F32)
    outs = [[], [], []]
    for step in range(4):
        grads = attention_back(
            table_ref[0, step],
            stack_heads(agent_rows(query, step)),
            agent_rows(keys, step),
            agent_rows(values, step),
            agent_rows(upstream, step),
        )
        for kept, grad in zip(outs, grads):
            kept.append(grad.reshape(16, 8, 128))
    for ref, kept in zip((query_out, keys_out, values_out), outs):
        ref[...] = jnp.concatenate(kept, 1).astype(BF)


def agent_backward_all_kernel(q, k, v, g, table_ref, *rest):
    out_ref = rest[-1]
    agent_backward_kernel(
        q,
        k,
        v,
        g,
        table_ref,
        out_ref.at[:, 0],
        out_ref.at[:, 1],
        out_ref.at[:, 2],
    )


def agent_backward(arrived, upstream, tables, waits=()):
    return pl.pallas_call(
        agent_backward_all_kernel,
        grid=(4,),
        in_specs=agent_specs()
        + [
            pl.BlockSpec((16, 32, 128), lambda i: (0, i, 0)),
            pl.BlockSpec((1, 4, 256, 128), lambda i: (i, 0, 0, 0)),
        ]
        + [unused] * len(waits),
        out_specs=pl.BlockSpec((16, 3, 32, 128), lambda i: (0, 0, i, 0)),
        out_shape=jax.ShapeDtypeStruct((16, 3, 128, 128), BF),
        compiler_params=params(),
        cost_estimate=cost(6e9, 6 * MIB),
        name="agent_backward",
    )(arrived, arrived, arrived, upstream, tables, *map(pinned, waits))


def middle_kernel(
    tokens_ref, mixed_ref, cotangent_ref, weights_ref, *rest
):
    send_ref, after_ref, hidden_out_ref, cotangent_out_ref, hidden_ref = rest[-7:-2]
    step = pl.program_id(0)
    ready = fetch((3, 4, 5, 6, 7), weights_ref, *rest[-2:])
    matrix = ready()

    @pl.when(step == 0)
    def _():
        mixed = jnp.concatenate([mixed_ref[pair] for pair in range(8)], 1)
        after = (
            tokens_ref[...].astype(F32)
            + jnp.dot(mixed, matrix, preferred_element_type=F32)
        ).astype(BF)
        after = reorder(after, "a", "m")
        after_ref[...] = after
        wide = after.astype(F32)
        hidden = (wide * factor_of(wide)).astype(BF)
        hidden_ref[...] = hidden
        for block in range(8):
            hidden_out_ref[block] = hidden[:, 128 * block : 128 * block + 128]
        cotangent_out_ref[...] = reorder(cotangent_ref[...], "o", "m")

    def send(result):
        result = result.astype(BF)
        for pair in range(8):
            send_ref[pair, 0] = result[:, 128 * pair : 128 * pair + 128]

    @pl.when((step > 0) & (step < 4))
    def _():
        send(jnp.dot(hidden_ref[...], matrix, preferred_element_type=F32))

    @pl.when(step == 4)
    def _():
        send(dot_nt(cotangent_out_ref[...], matrix))


def middle(tokens, mixed, cotangent, weights, waits=()):
    return pl.pallas_call(
        middle_kernel,
        grid=(5,),
        in_specs=[
            fixed((ROWS, D)),
            fixed((8, ROWS, 128)),
            fixed((ROWS, D)),
            unused,
        ]
        + [unused] * len(waits),
        out_specs=[
            pl.BlockSpec((8, 1, ROWS, 128), lambda i: (0, jnp.maximum(i - 1, 0), 0, 0)),
            fixed((ROWS, D)),
            fixed((8, ROWS, 128)),
            fixed((ROWS, D)),
        ],
        out_shape=[
            jax.ShapeDtypeStruct((8, 4, ROWS, 128), BF),
            pltpu.HBM((ROWS, D), BF),
            pltpu.HBM((8, ROWS, 128), BF),
            pltpu.HBM((ROWS, D), BF),
        ],
        scratch_shapes=[pltpu.VMEM((ROWS, D), BF)] + held(5),
        compiler_params=params(45),
        cost_estimate=cost(5 * 2 * ROWS * D * D, 13 * MIB),
        name="middle",
    )(tokens, mixed, cotangent, pinned(weights), *map(pinned, waits))


def mode_kernel(arrived_ref, *rest):
    out_ref = rest[-1]
    rows = lax.broadcasted_iota(jnp.int32, (256, 128), 0)
    columns = lax.broadcasted_iota(jnp.int32, (256, 128), 1)
    same = ((rows >> 6) & 1) == (columns >> 6)
    offset = jnp.where(same, 0.0, -1e30).astype(F32)
    for pair in range(4):

        def take(which):
            block = arrived_ref[:, which, 16 * pair : 16 * pair + 16, :].astype(F32)
            parts = [block[:, 8 * n : 8 * n + 8, :].reshape(64, 128) for n in range(2)]
            return jnp.concatenate(parts, 0).astype(BF)

        query, keys, values, upstream = (take(which) for which in range(4))
        query_stack = stack_heads(query)
        table = probabilities(query_stack, keys, offset)
        results = (attend(table, values),) + attention_back(
            table, query_stack, keys, values, upstream
        )
        for which, result in enumerate(results):
            parts = [result[64 * n : 64 * n + 64].reshape(8, 8, 128) for n in range(2)]
            out_ref[:, which, 16 * pair : 16 * pair + 16, :] = jnp.concatenate(parts, 1).astype(BF)


def mode_attention(arrived, after=()):
    spec = pl.BlockSpec((8, 4, 64, 128), lambda i: (0, 0, i, 0))
    return pl.pallas_call(
        mode_kernel,
        grid=(4,),
        in_specs=[spec] + [unused] * len(after),
        out_specs=spec,
        out_shape=pltpu.HBM((8, 4, ROWS, 128), BF),
        compiler_params=params(),
        cost_estimate=cost(8e9, 4 * MIB),
        name="mode_attention",
    )(arrived, *map(pinned, after))


def turn_kernel(returned_ref, cotangent_ref, after_ref, weights_ref, *rest):
    send_ref, grad_after_ref, total_ref = rest[-5:-2]
    step = pl.program_id(0)
    ready = fetch((4, 5, 6, 3), weights_ref, *rest[-2:])
    matrix = ready()

    @pl.when(step < 3)
    def _():
        grads = jnp.concatenate([returned_ref[pair, 0] for pair in range(8)], 1)
        product = dot_nt(grads, matrix)

        @pl.when(step == 0)
        def _():
            total_ref[...] = product

        @pl.when(step > 0)
        def _():
            total_ref[...] += product

    @pl.when(step == 3)
    def _():
        grad_after = (
            cotangent_ref[...].astype(F32) + normalize_back(after_ref[...], total_ref[...])
        ).astype(BF)
        grad_after = reorder(grad_after, "m", "a")
        grad_after_ref[...] = grad_after
        result = dot_nt(grad_after, matrix).astype(BF)
        for pair in range(8):
            for half in range(2):
                send_ref[2 * pair + half] = result[
                    128 * half : 128 * half + 128, 128 * pair : 128 * pair + 128
                ]


def turn(returned, cotangent, after, weights, waits=()):
    return pl.pallas_call(
        turn_kernel,
        grid=(4,),
        in_specs=[
            pl.BlockSpec((8, 1, ROWS, 128), lambda i: (0, jnp.minimum(i + 1, 3), 0, 0)),
            fixed((ROWS, D)),
            fixed((ROWS, D)),
            unused,
        ]
        + [unused] * len(waits),
        out_specs=[fixed((16, 128, 128)), fixed((ROWS, D))],
        out_shape=[
            pltpu.HBM((16, 128, 128), BF),
            pltpu.HBM((ROWS, D), BF),
        ],
        scratch_shapes=[pltpu.VMEM((ROWS, D), F32)] + held(4),
        compiler_params=params(45),
        cost_estimate=cost(4 * 2 * ROWS * D * D, 12 * MIB),
        name="turn",
    )(returned, cotangent, after, pinned(weights), *map(pinned, waits))


def whole_rows(ref):
    return jnp.concatenate([ref[:, 0].reshape(8, ROWS, 128)[pair] for pair in range(8)], 1)


def leave_kernel(returned_ref, tokens_ref, grad_after_ref, weights_ref, *rest):
    out_ref, total_ref = rest[-4:-2]
    step = pl.program_id(0)
    ready = fetch((0, 1, 2), weights_ref, *rest[-2:])
    product = dot_nt(whole_rows(returned_ref), ready())

    @pl.when(step == 0)
    def _():
        total_ref[...] = product

    @pl.when(step > 0)
    def _():
        total_ref[...] += product

    @pl.when(step == 2)
    def _():
        grads = (
            grad_after_ref[...].astype(F32) + normalize_back(tokens_ref[...], total_ref[...])
        ).astype(BF)
        out_ref[...] = reorder(grads, "a", "o")


def leave(returned, tokens, grad_after, weights, waits=()):
    return pl.pallas_call(
        leave_kernel,
        grid=(3,),
        in_specs=[
            pl.BlockSpec((16, 1, 128, 128), lambda i: (0, i, 0, 0)),
            fixed((ROWS, D)),
            fixed((ROWS, D)),
            unused,
        ]
        + [unused] * len(waits),
        out_specs=fixed((ROWS, D)),
        out_shape=jax.ShapeDtypeStruct((ROWS, D), BF),
        scratch_shapes=[pltpu.VMEM((ROWS, D), F32)] + held(3),
        compiler_params=params(45),
        cost_estimate=cost(3 * 2 * ROWS * D * D, 9 * MIB),
        name="leave",
    )(returned, tokens, grad_after, pinned(weights), *map(pinned, waits))


CORE, MODE, CHIP, Z, YLO, X, YHI = range(7)


def swap(values, axis, bits):
    size = lax.axis_size(axis)
    return lax.ppermute(values, axis, [(n, n ^ bits) for n in range(size)])


def swap_all(parts, axis, bit):
    return [parts[0]] + [swap(parts[o], axis, o * bit) for o in range(1, 4)]


def prefetched(kernel, ids, operands, in_specs, out_specs, out_shape, name, grid=(), scratch=()):
    return pl.pallas_call(
        kernel,
        grid_spec=pltpu.PrefetchScalarGridSpec(
            num_scalar_prefetch=1,
            grid=grid,
            in_specs=in_specs,
            out_specs=out_specs,
            scratch_shapes=list(scratch),
        ),
        out_shape=out_shape,
        compiler_params=params(),
        cost_estimate=cost(1e9, 5 * MIB),
        name=name,
    )(ids, *operands)


def rows_of(values, start, count):
    return values[pl.ds(pl.multiple_of(start, count), count), :]


def early_kernel(add, ids_ref, hidden_ref, mixed_ref, grads_ref, last_ref, *rest):
    step = pl.program_id(0)

    def finish(first, second, right):
        product = dot_tn(jnp.concatenate([first, second], 1), right)
        if add:
            arrived_ref, total_ref = rest[0], rest[-1]
            total_ref[...] = product + arrived_ref[0].astype(F32)
            for columns in range(2):
                for give in range(2):
                    out_ref = rest[2 * columns + give - 5]
                    near, far = ((0, 3), (1, 2))[give] if columns == 0 else ((0, 1), (3, 2))[give]
                    for place, partner in enumerate((near, far)):
                        rows = rows_of(total_ref, (ids_ref[Z] ^ partner) * 64, 64)
                        out_ref[0, 64 * place : 64 * place + 64] = rows[
                            :, 512 * columns : 512 * columns + 512
                        ].astype(BF)
        else:
            rest[-1][0] = product.astype(BF)

    @pl.when(step < 6)
    def _():
        right = jnp.concatenate([grads_ref[pair, 0] for pair in range(8)], 1)
        finish(hidden_ref[0], hidden_ref[1], right)

    @pl.when(step >= 6)
    def _():
        finish(mixed_ref[0, 0], mixed_ref[1, 0], last_ref[...])


def early_products(ids, hidden, returned, last, arrived=None, waits=()):
    def feature(i, ids_ref):
        return 2 * (i % 2) + ids_ref[CORE]

    in_specs = [
        pl.BlockSpec((2, ROWS, 128), lambda i, c: (feature(i, c), 0, 0)),
        pl.BlockSpec((2, 1, ROWS, 128), lambda i, c: (feature(i, c), 0, 0, 0)),
        pl.BlockSpec((8, 1, ROWS, 128), lambda i, c: (0, jnp.minimum(i // 2, 2) + 1, 0, 0)),
        pl.BlockSpec((ROWS, D), lambda i, c: (0, 0)),
    ]
    operands = [hidden, returned, returned, last]
    if arrived is None:
        return prefetched(
            functools.partial(early_kernel, False), ids, operands + [pinned(wait) for wait in waits],
            in_specs + [unused] * len(waits),
            pl.BlockSpec((1, ROWS, D), lambda i, c: (i, 0, 0)),
            jax.ShapeDtypeStruct((8, ROWS, D), BF), "early_first", (8,),
        )
    return prefetched(
        functools.partial(early_kernel, True), ids, operands + [arrived, *map(pinned, waits)],
        in_specs + [pl.BlockSpec((1, ROWS, D), lambda i, c: (i, 0, 0))] + [unused] * len(waits),
        [pl.BlockSpec((1, 128, 512), lambda i, c: (i, 0, 0))] * 4,
        [pltpu.HBM((8, 128, 512), BF), jax.ShapeDtypeStruct((8, 128, 512), BF)] * 2, "early_add", (8,),
        [pltpu.VMEM((ROWS, D), F32)],
    )


def sum_split_kernel(split, count, inputs, ids_ref, *refs):
    total_ref = refs[-1]
    total = refs[0][0].astype(F32)
    for ref in refs[1:inputs]:
        total += ref[0].astype(F32)
    total_ref[...] = total
    share = total_ref.shape[0] // count
    for partner, out_ref in enumerate(refs[-1 - count : -1]):
        out_ref[0] = rows_of(total_ref, (ids_ref[split] ^ partner) * share, share).astype(BF)


def sum_split(ids, parts, split, count, name, waits=()):
    blocks, rows, columns = parts[0].shape
    return prefetched(
        functools.partial(sum_split_kernel, split, count, len(parts)), ids, [*parts, *map(pinned, waits)],
        [pl.BlockSpec((1, rows, columns), lambda i, c: (i, 0, 0))] * len(parts)
        + [unused] * len(waits),
        [pl.BlockSpec((1, rows // count, columns), lambda i, c: (i, 0, 0))] * count,
        [jax.ShapeDtypeStruct((blocks, rows // count, columns), BF)] * count, name, (blocks,),
        [pltpu.VMEM((rows, columns), F32)],
    )


def early_half_kernel(ids_ref, left_ref, left_in, right_ref, right_in, own_ref, *outs):
    for columns, (ref, arrived) in enumerate(((left_ref, left_in), (right_ref, right_in))):
        total = (ref[...].astype(F32) + arrived[...].astype(F32)).astype(BF)
        own_ref[:, :, 512 * columns : 512 * columns + 512] = total[:, :64]
        outs[columns][...] = total[:, 64:]


def early_half(ids, parts):
    left, left_give, right, right_give = parts
    operands = [left, swap(left_give, "mode", 2), right, swap(right_give, "mode", 6)]
    narrow = pl.BlockSpec((2, 64, 512), lambda i, c: (i, 0, 0))
    return prefetched(
        early_half_kernel, ids, operands,
        [pl.BlockSpec((2, 128, 512), lambda i, c: (i, 0, 0))] * 4,
        [pl.BlockSpec((2, 64, D), lambda i, c: (i, 0, 0)), narrow, narrow],
        [pltpu.HBM((8, 64, D), BF)] + [jax.ShapeDtypeStruct((8, 64, 512), BF)] * 2,
        "early_half", (4,),
    )


def early_z_kernel(ids_ref, own_ref, left_ref, right_ref, keep_ref, give_ref):
    for other, out_ref in enumerate((keep_ref, give_ref)):
        first = pl.multiple_of((ids_ref[YLO] ^ other) * 32, 32)
        for columns, ref in enumerate((left_ref, right_ref)):
            lanes = slice(512 * columns, 512 * columns + 512)
            out_ref[:, :, lanes] = (
                own_ref[:, pl.ds(first, 32), lanes].astype(F32)
                + ref[:, pl.ds(first, 32), :].astype(F32)
            ).astype(BF)


def early_sums(ids, own, left, right):
    narrow = pl.BlockSpec((2, 64, 512), lambda i, c: (i, 0, 0))
    keep, give = prefetched(
        early_z_kernel, ids, [own, left, right],
        [pl.BlockSpec((2, 64, D), lambda i, c: (i, 0, 0)), narrow, narrow],
        [pl.BlockSpec((2, 32, D), lambda i, c: (i, 0, 0))] * 2,
        [pltpu.HBM((8, 32, D), BF), jax.ShapeDtypeStruct((8, 32, D), BF)], "early_z", (4,),
    )
    return keep, swap(give, "mode", 1)


WIDE = 384 + D


def gather_hidden(keep, give):
    chip = jnp.concatenate([keep, swap(give, "agent", 1)], 0)
    here = jnp.stack([chip, swap(chip, "agent", 2)])
    return here


def late_kernel(ids_ref, *refs):
    hiddens, first_ref, second_ref, mixed_ref, after_ref, mine_ref, *theirs_refs, total_ref = (
        refs[:4],
        *refs[4:8],
        *refs[-4:],
    )
    step = pl.program_id(0)
    core = ids_ref[CORE]

    @pl.when(step == 0)
    def _():
        total_ref[...] = jnp.zeros_like(total_ref)

    for partner, ref in enumerate(hiddens):

        @pl.when(step // 2 == partner)
        def _(ref=ref):
            right = jnp.concatenate(
                [
                    jnp.concatenate([source[0, slot] for slot in range(3)], 1)
                    for source in (first_ref, second_ref)
                ],
                0,
            )
            total_ref[...] += dot_tn(right, ref[0])

    for block in range(4):

        @pl.when(step == 8 + block)
        def _(block=block):
            rows = total_ref[:, 256 * block : 256 * block + 256].T.astype(BF)
            left = jnp.concatenate([mixed_ref[0], mixed_ref[1]], 1)
            other = dot_tn(left, after_ref[...]).astype(BF)

            @pl.when(core == block % 2)
            def _():
                mine_ref[block // 2, :, :384] = rows
                mine_ref[block // 2, :, 384:] = other

            @pl.when(core != block % 2)
            def _():
                theirs_refs[block // 2][:, :384] = rows
                theirs_refs[block // 2][:, 384:] = other


def late_products(ids, hiddens, grads, mixed, grad_after, waits):
    def source(i, c, other):
        chip = (c[X] ^ jnp.minimum(i // 2, 3)) * 2 + (c[YHI] ^ (i % 2))
        return 2 * chip + (c[CORE] ^ other)

    in_specs = [
        pl.BlockSpec((1, ROWS, D), lambda i, c, o=o: (jnp.clip(i - 2 * o, 0, 1), 0, 0))
        for o in range(4)
    ]
    in_specs += [
        pl.BlockSpec((1, 3, 128, 128), lambda i, c, o=o: (source(i, c, o), 0, 0, 0))
        for o in range(2)
    ]
    in_specs += [
        pl.BlockSpec((2, ROWS, 128), lambda i, c: (jnp.clip(i - 8, 0, 3), 0, 0)),
        pl.BlockSpec((ROWS, D), lambda i, c: (0, 0)),
    ]
    return prefetched(
        late_kernel, ids, list(hiddens) + [grads, grads, mixed, grad_after, *map(pinned, waits)],
        in_specs + [unused] * len(waits),
        [pl.BlockSpec((2, ROWS, WIDE), lambda i, c: (0, 0, 0))]
        + [pl.BlockSpec((ROWS, WIDE), lambda i, c: (0, 0))] * 2,
        [jax.ShapeDtypeStruct((2, ROWS, WIDE), BF)]
        + [jax.ShapeDtypeStruct((ROWS, WIDE), BF)] * 2, "late_products", (12,),
        [pltpu.VMEM((384, D), F32)],
    )


def chips_kernel(ids_ref, early_ref, early_in, late_ref, late_in, *rest):
    outs, total_ref = rest[:-1], rest[-1]
    total_ref[...] = late_ref[...].astype(F32) + late_in[...].astype(F32)
    for partner, out_ref in enumerate(outs):
        chip_x = ids_ref[X] ^ partner
        lanes = pl.ds(pl.multiple_of(jnp.minimum(chip_x, 2) * 128, 128), 128)
        for n in range(2):
            block = chip_x * 2 + n
            out_ref[n, :, :D] = (early_ref[block].astype(F32) + early_in[block].astype(F32)).astype(
                BF
            )
        out_ref[:, :, D : D + 128] = total_ref[:, :, lanes].astype(BF)
        out_ref[:, :, D + 128 :] = total_ref[:, :, 384:].astype(BF)


def cross_kernel(ids_ref, *refs):
    for other, out_ref in enumerate(refs[4:]):
        row = ids_ref[YHI] ^ other
        for source, target in ((0, 0), (D + 128, 384)):
            total = refs[0][row, :, source : source + D].astype(F32)
            for ref in refs[1:4]:
                total += ref[row, :, source : source + D].astype(F32)
            for place in range(4):
                out_ref[place, :, target : target + 256] = total[
                    :, 256 * place : 256 * place + 256
                ].astype(BF)
        for partner, ref in enumerate(refs[:4]):
            out_ref[partner, :, 256:384] = ref[row, :, D : D + 128]


def last_kernel(ids_ref, keep_ref, arrived_ref, agent_ref, mode_ref):
    for place in range(4):
        lanes = slice(256 * place, 256 * place + 256)
        mode_ref[:, lanes] = keep_ref[place, :, :256].astype(F32) + arrived_ref[
            place, :, :256
        ].astype(F32)

    @pl.when(ids_ref[X] < 3)
    def _():
        for other, ref in enumerate((keep_ref, arrived_ref)):
            for partner in range(4):
                pair = (ids_ref[X] ^ partner) * 2 + (ids_ref[YHI] ^ other)
                lanes = pl.ds(pl.multiple_of(pair * 128, 128), 128)
                agent_ref[:, lanes] = ref[partner, :, 256:384].astype(F32)

    @pl.when(ids_ref[X] == 3)
    def _():
        for place in range(4):
            lanes = slice(256 * place, 256 * place + 256)
            agent_ref[:, lanes] = keep_ref[place, :, 384:].astype(F32) + arrived_ref[
                place, :, 384:
            ].astype(F32)


def chip_sums(ids, early, late):
    parts = prefetched(
        chips_kernel, ids, [*early, *late],
        [fixed((8, 32, D))] * 2 + [fixed((2, 32, WIDE))] * 2, [fixed((2, 32, 128 + 2 * D))] * 4,
        [jax.ShapeDtypeStruct((2, 32, 128 + 2 * D), BF)] * 4, "chips", (1,),
        [pltpu.VMEM((2, 32, WIDE), F32)],
    )
    keep, give = prefetched(
        cross_kernel, ids, swap_all(parts, "agent", 4),
        [fixed((2, 32, 128 + 2 * D))] * 4, [fixed((4, 32, 640))] * 2,
        [jax.ShapeDtypeStruct((4, 32, 640), BF)] * 2, "cross", (1,),
    )
    return prefetched(
        last_kernel, ids, [keep, swap(give, "agent", 2)],
        [fixed((4, 32, 640))] * 2, [fixed((32, D))] * 2,
        [jax.ShapeDtypeStruct((32, D), F32)] * 2, "last", (1,),
    )


def late_add_kernel(ids_ref, mine_ref, first_ref, second_ref, *rest):
    total_ref = rest[-1]
    for block, ref in enumerate((first_ref, second_ref)):
        total_ref[...] = mine_ref[block].astype(F32) + ref[...].astype(F32)
        for partner, out_ref in enumerate(rest[-5:-1]):
            out_ref[block] = rows_of(total_ref, (ids_ref[Z] ^ partner) * 64, 64).astype(BF)


def late_sums(ids, mine, first, second, waits):
    parts = prefetched(
        late_add_kernel, ids,
        [mine, swap(first, "agent", 1), swap(second, "agent", 1)],
        [fixed((2, ROWS, WIDE))] + [fixed((ROWS, WIDE))] * 2,
        [fixed((2, 64, WIDE))] * 4,
        [pltpu.HBM((2, 64, WIDE), BF)] + [jax.ShapeDtypeStruct((2, 64, WIDE), BF)] * 3, "late_add", (1,),
        [pltpu.VMEM((ROWS, WIDE), F32)],
    )
    keep, give = sum_split(ids, swap_all(parts, "mode", 2), YLO, 2, "late_z", waits)
    return keep, swap(give, "mode", 1)


def exchange(values, axis):
    return lax.all_to_all(values, axis, split_axis=0, concat_axis=0, tiled=True)


def local(tokens, cotangent, weights, agent_mask):
    agent, mode = lax.axis_index("agent"), lax.axis_index("mode")
    ids = jnp.stack(
        [agent & 1, mode, agent >> 1, mode >> 1, mode & 1, agent >> 2, (agent >> 1) & 1]
    ).astype(jnp.int32)
    other_ids = ids.at[CORE].set(1 - ids[CORE])
    token_rows = tokens.reshape(ROWS, D)
    grad_rows = cotangent.reshape(ROWS, D)
    offset = jnp.where(agent_mask == 1, 0.0, masked_score).astype(F32).reshape(1, 128)

    outgoing, tokens_a, hidden_keep, hidden_give = enter(ids, token_rows, weights)
    arrived_one = exchange(outgoing, "agent")
    hidden_here = gather_hidden(hidden_keep, hidden_give)
    mixed, tables = agent_forward(arrived_one, offset)
    mixed_one = exchange(mixed, "agent").reshape(8, ROWS, 128)
    outgoing, after, hidden_two, cotangent_m = middle(
        tokens_a, mixed_one, grad_rows, weights, [hidden_here]
    )
    arrived_two = exchange(outgoing.reshape(8, 1024, 128), "mode").reshape(8, 4, ROWS, 128)
    hiddens = [hidden_here] + [swap(hidden_here, "agent", 4 * o) for o in range(1, 4)]
    returning = mode_attention(arrived_two, hiddens[1::2])
    returned_two = exchange(returning.reshape(8, 1024, 128), "mode").reshape(8, 4, ROWS, 128)
    early = (hidden_two, returned_two, cotangent_m)
    theirs = early_products(other_ids, *early, None, hiddens[2:3])
    parts = early_products(ids, *early, swap(theirs, "agent", 1))
    outgoing, grad_after = turn(returned_two, cotangent_m, after, weights, parts[:1])
    upstream = exchange(outgoing, "agent")
    own, left, right = early_half(ids, parts)
    returning = agent_backward(arrived_one, upstream, tables, [own])
    left, right = swap(left, "mode", 6), swap(right, "mode", 2)
    returned_one = exchange(returning.reshape(16, 384, 128), "agent").reshape(16, 3, 128, 128)
    late_parts = late_products(
        ids, hiddens, returning, mixed_one, grad_after, [left, right]
    )
    token_grads = leave(returned_one, tokens_a, grad_after, weights)
    late = late_sums(ids, *late_parts, [token_grads])
    early = early_sums(ids, own, left, right)
    agent_weight_grads, mode_weight_grads = chip_sums(ids, early, late)
    return (token_grads.reshape(tokens.shape), agent_weight_grads, mode_weight_grads)


def solution(mesh):
    placed = (P("agent", "mode", None, None), P("agent", "mode", None, None), P(), P())
    return jax.shard_map(
        local,
        mesh=mesh,
        in_specs=placed,
        out_specs=(
            P("agent", "mode", None, None),
            P(("agent", "mode"), None),
            P(("agent", "mode"), None),
        ),
        check_vma=False,
    )
```

```python
import functools

import jax
import jax.numpy as jnp
from jax import lax
from jax.experimental import pallas as pl
from jax.experimental.pallas import tpu as pltpu
from jax.sharding import PartitionSpec as P

epsilon = 1e-06
masked_score = -1000000000.0

BF = jnp.bfloat16
F32 = jnp.float32
D = 1024
ROWS = 256
SCALE = 0.125
MIB = 1024 * 1024


def decode(row, order):
    if order == "o":
        return row >> 5, (row >> 2) & 7, row & 3
    if order == "a":
        return row & 7, row >> 5, (row >> 3) & 3
    return (row >> 3) & 7, row & 7, row >> 6


def encode(agent, mode, step, order):
    if order == "o":
        return agent * 32 + mode * 4 + step
    if order == "a":
        return mode * 32 + step * 8 + agent
    return step * 64 + agent * 8 + mode


def reorder(values, source, target):
    rows = lax.broadcasted_iota(jnp.int32, (ROWS, ROWS), 0)
    columns = lax.broadcasted_iota(jnp.int32, (ROWS, ROWS), 1)
    chosen = encode(*decode(rows, target), source)
    table = (chosen == columns).astype(F32).astype(BF)
    return jnp.dot(table, values, preferred_element_type=F32).astype(BF)


def dot_nt(left, right):
    return lax.dot_general(left, right, (((1,), (1,)), ((), ())), preferred_element_type=F32)


def dot_tn(left, right):
    return lax.dot_general(left, right, (((0,), (0,)), ((), ())), preferred_element_type=F32)


def factor_of(wide):
    return lax.rsqrt(jnp.mean(wide * wide, -1, keepdims=True) + epsilon)


def normalize_back(values, upstream):
    wide = values.astype(F32)
    factor = factor_of(wide)
    normed = wide * factor
    return factor * (upstream - normed * jnp.mean(upstream * normed, -1, keepdims=True))


def fetch(slots, weights_ref, held_ref, sems_ref):
    copies = [
        pltpu.make_async_copy(weights_ref.at[slot], held_ref.at[n], sems_ref.at[n])
        for n, slot in enumerate(slots)
    ]
    step = pl.program_id(0)

    @pl.when(step == 0)
    def _():
        for copy in copies:
            copy.start()

    def ready():
        for n, copy in enumerate(copies):

            @pl.when(step == n)
            def _(copy=copy):
                copy.wait()

        return held_ref[step]

    return ready


def pinned(operand):
    return pltpu.with_memory_space_constraint(operand, pltpu.HBM)


def held(count):
    return [pltpu.VMEM((count, D, D), BF), pltpu.SemaphoreType.DMA((count,))]


def params(limit=32):
    return pltpu.CompilerParams(vmem_limit_bytes=limit * MIB)


def cost(flops, read):
    return pl.CostEstimate(flops=int(flops), bytes_accessed=int(read), transcendentals=0)


unused = pl.BlockSpec(memory_space=pl.ANY)


def fixed(shape):
    return pl.BlockSpec(shape, lambda *i: (0,) * len(shape))


def stack_heads(values):
    lanes = lax.broadcasted_iota(jnp.int32, (1, 128), 1)
    first = (lanes < 64).astype(F32).astype(BF)
    second = (lanes >= 64).astype(F32).astype(BF)
    return jnp.concatenate([values * first, values * second], 0)


def beside(table):
    return jnp.concatenate([table[:128], table[128:]], 1)


def probabilities(query_stack, keys, offset):
    scores = dot_nt(query_stack, keys) * SCALE + offset
    raised = jnp.exp(scores - jnp.max(scores, -1, keepdims=True))
    return raised / jnp.sum(raised, -1, keepdims=True)


def attend(table, values):
    return jnp.dot(beside(table.astype(BF)), stack_heads(values), preferred_element_type=F32)


def attention_back(table, query_stack, keys, values, upstream):
    upstream_stack = stack_heads(upstream)
    through = dot_nt(upstream_stack, values)
    value_grad = dot_tn(table.astype(BF), upstream_stack)
    centre = jnp.sum(through * table, -1, keepdims=True)
    score_grad = (table * (through - centre) * SCALE).astype(BF)
    query_grad = jnp.dot(beside(score_grad), stack_heads(keys), preferred_element_type=F32)
    keys_grad = dot_tn(score_grad, query_stack)
    return query_grad, keys_grad, value_grad


def enter_kernel(
    ids_ref, tokens_ref, weights_ref,
    send_ref, tokens_out_ref, keep_ref, give_ref, hidden_ref, held_ref, sems_ref,
):
    step = pl.program_id(0)
    ready = fetch((0, 1, 2), weights_ref, held_ref, sems_ref)

    @pl.when(step == 0)
    def _():
        rows = reorder(tokens_ref[...], "o", "a")
        tokens_out_ref[...] = rows
        wide = rows.astype(F32)
        hidden = (wide * factor_of(wide)).astype(BF)
        hidden_ref[...] = hidden
        core = ids_ref[0]

        @pl.when(core == 0)
        def _():
            keep_ref[...] = hidden[:128]
            give_ref[...] = hidden[128:]

        @pl.when(core == 1)
        def _():
            keep_ref[...] = hidden[128:]
            give_ref[...] = hidden[:128]

    result = jnp.dot(hidden_ref[...], ready(), preferred_element_type=F32).astype(BF)
    for pair in range(8):
        for half in range(2):
            send_ref[2 * pair + half] = result[
                128 * half : 128 * half + 128, 128 * pair : 128 * pair + 128
            ]


def enter(ids, tokens, weights):
    return pl.pallas_call(
        enter_kernel,
        grid_spec=pltpu.PrefetchScalarGridSpec(
            num_scalar_prefetch=1,
            grid=(3,),
            in_specs=[fixed((ROWS, D)), unused],
            out_specs=[
                pl.BlockSpec((16, 128, 128), lambda i, c: (0, i, 0)),
                fixed((ROWS, D)),
                fixed((128, D)),
                fixed((128, D)),
            ],
            scratch_shapes=[pltpu.VMEM((ROWS, D), BF)] + held(3),
        ),
        out_shape=[
            jax.ShapeDtypeStruct((16, 384, 128), BF),
            pltpu.HBM((ROWS, D), BF),
            pltpu.HBM((128, D), BF),
            jax.ShapeDtypeStruct((128, D), BF),
        ],
        compiler_params=params(45),
        cost_estimate=cost(3 * 2 * ROWS * D * D, 8 * MIB),
        name="enter",
    )(ids, tokens, pinned(weights))


def agent_rows(block, step):
    return block[:, 8 * step : 8 * step + 8, :].reshape(128, 128).astype(BF)


def agent_forward_kernel(query_ref, keys_ref, values_ref, offset_ref, out_ref, table_ref):
    query = query_ref[...].astype(F32)
    keys = keys_ref[...].astype(F32)
    values = values_ref[...].astype(F32)
    offset = offset_ref[...]
    outs = []
    for step in range(4):
        table = probabilities(
            stack_heads(agent_rows(query, step)), agent_rows(keys, step), offset
        )
        table_ref[0, step] = table
        outs.append(attend(table, agent_rows(values, step)).reshape(16, 8, 128))
    out_ref[...] = jnp.concatenate(outs, 1).astype(BF)


def agent_specs():
    return [pl.BlockSpec((16, 32, 128), lambda i, k=k: (0, 4 * k + i, 0)) for k in range(3)]


def agent_forward(arrived, offset):
    return pl.pallas_call(
        agent_forward_kernel,
        grid=(4,),
        in_specs=agent_specs() + [fixed((1, 128))],
        out_specs=[
            pl.BlockSpec((16, 32, 128), lambda i: (0, i, 0)),
            pl.BlockSpec((1, 4, 256, 128), lambda i: (i, 0, 0, 0)),
        ],
        out_shape=[
            jax.ShapeDtypeStruct((16, 128, 128), BF),
            pltpu.HBM((4, 4, 256, 128), F32),
        ],
        compiler_params=params(),
        cost_estimate=cost(3e9, 4 * MIB),
        name="agent_forward",
    )(arrived, arrived, arrived, offset)


def agent_backward_kernel(
    query_ref, keys_ref, values_ref, upstream_ref, table_ref, query_out, keys_out, values_out
):
    query = query_ref[...].astype(F32)
    keys = keys_ref[...].astype(F32)
    values = values_ref[...].astype(F32)
    upstream = upstream_ref[...].astype(F32)
    outs = [[], [], []]
    for step in range(4):
        grads = attention_back(
            table_ref[0, step],
            stack_heads(agent_rows(query, step)),
            agent_rows(keys, step),
            agent_rows(values, step),
            agent_rows(upstream, step),
        )
        for kept, grad in zip(outs, grads):
            kept.append(grad.reshape(16, 8, 128))
    for ref, kept in zip((query_out, keys_out, values_out), outs):
        ref[...] = jnp.concatenate(kept, 1).astype(BF)


def agent_backward_all_kernel(q, k, v, g, table_ref, *rest):
    out_ref = rest[-1]
    agent_backward_kernel(
        q,
        k,
        v,
        g,
        table_ref,
        out_ref.at[:, 0],
        out_ref.at[:, 1],
        out_ref.at[:, 2],
    )


def agent_backward(arrived, upstream, tables, waits=()):
    return pl.pallas_call(
        agent_backward_all_kernel,
        grid=(4,),
        in_specs=agent_specs()
        + [
            pl.BlockSpec((16, 32, 128), lambda i: (0, i, 0)),
            pl.BlockSpec((1, 4, 256, 128), lambda i: (i, 0, 0, 0)),
        ]
        + [unused] * len(waits),
        out_specs=pl.BlockSpec((16, 3, 32, 128), lambda i: (0, 0, i, 0)),
        out_shape=jax.ShapeDtypeStruct((16, 3, 128, 128), BF),
        compiler_params=params(),
        cost_estimate=cost(6e9, 6 * MIB),
        name="agent_backward",
    )(arrived, arrived, arrived, upstream, tables, *map(pinned, waits))


def middle_kernel(
    tokens_ref, mixed_ref, cotangent_ref, weights_ref, *rest
):
    send_ref, after_ref, hidden_out_ref, cotangent_out_ref, hidden_ref = rest[-7:-2]
    step = pl.program_id(0)
    ready = fetch((3, 4, 5, 6, 7), weights_ref, *rest[-2:])
    matrix = ready()

    @pl.when(step == 0)
    def _():
        mixed = jnp.concatenate([mixed_ref[pair] for pair in range(8)], 1)
        after = (
            tokens_ref[...].astype(F32)
            + jnp.dot(mixed, matrix, preferred_element_type=F32)
        ).astype(BF)
        after = reorder(after, "a", "m")
        after_ref[...] = after
        wide = after.astype(F32)
        hidden = (wide * factor_of(wide)).astype(BF)
        hidden_ref[...] = hidden
        for block in range(8):
            hidden_out_ref[block] = hidden[:, 128 * block : 128 * block + 128]
        cotangent_out_ref[...] = reorder(cotangent_ref[...], "o", "m")

    def send(result):
        result = result.astype(BF)
        for pair in range(8):
            send_ref[pair, 0] = result[:, 128 * pair : 128 * pair + 128]

    @pl.when((step > 0) & (step < 4))
    def _():
        send(jnp.dot(hidden_ref[...], matrix, preferred_element_type=F32))

    @pl.when(step == 4)
    def _():
        send(dot_nt(cotangent_out_ref[...], matrix))


def middle(tokens, mixed, cotangent, weights, waits=()):
    return pl.pallas_call(
        middle_kernel,
        grid=(5,),
        in_specs=[
            fixed((ROWS, D)),
            fixed((8, ROWS, 128)),
            fixed((ROWS, D)),
            unused,
        ]
        + [unused] * len(waits),
        out_specs=[
            pl.BlockSpec((8, 1, ROWS, 128), lambda i: (0, jnp.maximum(i - 1, 0), 0, 0)),
            fixed((ROWS, D)),
            fixed((8, ROWS, 128)),
            fixed((ROWS, D)),
        ],
        out_shape=[
            jax.ShapeDtypeStruct((8, 4, ROWS, 128), BF),
            pltpu.HBM((ROWS, D), BF),
            pltpu.HBM((8, ROWS, 128), BF),
            pltpu.HBM((ROWS, D), BF),
        ],
        scratch_shapes=[pltpu.VMEM((ROWS, D), BF)] + held(5),
        compiler_params=params(45),
        cost_estimate=cost(5 * 2 * ROWS * D * D, 13 * MIB),
        name="middle",
    )(tokens, mixed, cotangent, pinned(weights), *map(pinned, waits))


def mode_kernel(arrived_ref, *rest):
    out_ref = rest[-1]
    rows = lax.broadcasted_iota(jnp.int32, (256, 128), 0)
    columns = lax.broadcasted_iota(jnp.int32, (256, 128), 1)
    same = ((rows >> 6) & 1) == (columns >> 6)
    offset = jnp.where(same, 0.0, -1e30).astype(F32)
    for pair in range(4):

        def take(which):
            block = arrived_ref[:, which, 16 * pair : 16 * pair + 16, :].astype(F32)
            parts = [block[:, 8 * n : 8 * n + 8, :].reshape(64, 128) for n in range(2)]
            return jnp.concatenate(parts, 0).astype(BF)

        query, keys, values, upstream = (take(which) for which in range(4))
        query_stack = stack_heads(query)
        table = probabilities(query_stack, keys, offset)
        results = (attend(table, values),) + attention_back(
            table, query_stack, keys, values, upstream
        )
        for which, result in enumerate(results):
            parts = [result[64 * n : 64 * n + 64].reshape(8, 8, 128) for n in range(2)]
            out_ref[:, which, 16 * pair : 16 * pair + 16, :] = jnp.concatenate(parts, 1).astype(BF)


def mode_attention(arrived, after=()):
    spec = pl.BlockSpec((8, 4, 64, 128), lambda i: (0, 0, i, 0))
    return pl.pallas_call(
        mode_kernel,
        grid=(4,),
        in_specs=[spec] + [unused] * len(after),
        out_specs=spec,
        out_shape=pltpu.HBM((8, 4, ROWS, 128), BF),
        compiler_params=params(),
        cost_estimate=cost(8e9, 4 * MIB),
        name="mode_attention",
    )(arrived, *map(pinned, after))


def turn_kernel(returned_ref, cotangent_ref, after_ref, weights_ref, *rest):
    send_ref, grad_after_ref, total_ref = rest[-5:-2]
    step = pl.program_id(0)
    ready = fetch((4, 5, 6, 3), weights_ref, *rest[-2:])
    matrix = ready()

    @pl.when(step < 3)
    def _():
        grads = jnp.concatenate([returned_ref[pair, 0] for pair in range(8)], 1)
        product = dot_nt(grads, matrix)

        @pl.when(step == 0)
        def _():
            total_ref[...] = product

        @pl.when(step > 0)
        def _():
            total_ref[...] += product

    @pl.when(step == 3)
    def _():
        grad_after = (
            cotangent_ref[...].astype(F32) + normalize_back(after_ref[...], total_ref[...])
        ).astype(BF)
        grad_after = reorder(grad_after, "m", "a")
        grad_after_ref[...] = grad_after
        result = dot_nt(grad_after, matrix).astype(BF)
        for pair in range(8):
            for half in range(2):
                send_ref[2 * pair + half] = result[
                    128 * half : 128 * half + 128, 128 * pair : 128 * pair + 128
                ]


def turn(returned, cotangent, after, weights, waits=()):
    return pl.pallas_call(
        turn_kernel,
        grid=(4,),
        in_specs=[
            pl.BlockSpec((8, 1, ROWS, 128), lambda i: (0, jnp.minimum(i + 1, 3), 0, 0)),
            fixed((ROWS, D)),
            fixed((ROWS, D)),
            unused,
        ]
        + [unused] * len(waits),
        out_specs=[fixed((16, 128, 128)), fixed((ROWS, D))],
        out_shape=[
            pltpu.HBM((16, 128, 128), BF),
            pltpu.HBM((ROWS, D), BF),
        ],
        scratch_shapes=[pltpu.VMEM((ROWS, D), F32)] + held(4),
        compiler_params=params(45),
        cost_estimate=cost(4 * 2 * ROWS * D * D, 12 * MIB),
        name="turn",
    )(returned, cotangent, after, pinned(weights), *map(pinned, waits))


def whole_rows(ref):
    return jnp.concatenate([ref[:, 0].reshape(8, ROWS, 128)[pair] for pair in range(8)], 1)


def leave_kernel(returned_ref, tokens_ref, grad_after_ref, weights_ref, *rest):
    out_ref, total_ref = rest[-4:-2]
    step = pl.program_id(0)
    ready = fetch((0, 1, 2), weights_ref, *rest[-2:])
    product = dot_nt(whole_rows(returned_ref), ready())

    @pl.when(step == 0)
    def _():
        total_ref[...] = product

    @pl.when(step > 0)
    def _():
        total_ref[...] += product

    @pl.when(step == 2)
    def _():
        grads = (
            grad_after_ref[...].astype(F32) + normalize_back(tokens_ref[...], total_ref[...])
        ).astype(BF)
        out_ref[...] = reorder(grads, "a", "o")


def leave(returned, tokens, grad_after, weights, waits=()):
    return pl.pallas_call(
        leave_kernel,
        grid=(3,),
        in_specs=[
            pl.BlockSpec((16, 1, 128, 128), lambda i: (0, i, 0, 0)),
            fixed((ROWS, D)),
            fixed((ROWS, D)),
            unused,
        ]
        + [unused] * len(waits),
        out_specs=fixed((ROWS, D)),
        out_shape=jax.ShapeDtypeStruct((ROWS, D), BF),
        scratch_shapes=[pltpu.VMEM((ROWS, D), F32)] + held(3),
        compiler_params=params(45),
        cost_estimate=cost(3 * 2 * ROWS * D * D, 9 * MIB),
        name="leave",
    )(returned, tokens, grad_after, pinned(weights), *map(pinned, waits))


CORE, MODE, CHIP, Z, YLO, X, YHI = range(7)


def swap(values, axis, bits):
    size = lax.axis_size(axis)
    return lax.ppermute(values, axis, [(n, n ^ bits) for n in range(size)])


def swap_all(parts, axis, bit):
    return [parts[0]] + [swap(parts[o], axis, o * bit) for o in range(1, 4)]


def prefetched(kernel, ids, operands, in_specs, out_specs, out_shape, name, grid=(), scratch=()):
    return pl.pallas_call(
        kernel,
        grid_spec=pltpu.PrefetchScalarGridSpec(
            num_scalar_prefetch=1,
            grid=grid,
            in_specs=in_specs,
            out_specs=out_specs,
            scratch_shapes=list(scratch),
        ),
        out_shape=out_shape,
        compiler_params=params(),
        cost_estimate=cost(1e9, 5 * MIB),
        name=name,
    )(ids, *operands)


def rows_of(values, start, count):
    return values[pl.ds(pl.multiple_of(start, count), count), :]


def early_kernel(add, ids_ref, hidden_ref, mixed_ref, grads_ref, last_ref, *rest):
    step = pl.program_id(0)

    def finish(first, second, right):
        product = dot_tn(jnp.concatenate([first, second], 1), right)
        if add:
            arrived_ref, total_ref = rest[0], rest[-1]
            total_ref[...] = product + arrived_ref[0].astype(F32)
            for columns in range(2):
                for give in range(2):
                    out_ref = rest[2 * columns + give - 5]
                    near, far = ((0, 3), (1, 2))[give] if columns == 0 else ((0, 1), (3, 2))[give]
                    for place, partner in enumerate((near, far)):
                        rows = rows_of(total_ref, (ids_ref[Z] ^ partner) * 64, 64)
                        out_ref[0, 64 * place : 64 * place + 64] = rows[
                            :, 512 * columns : 512 * columns + 512
                        ].astype(BF)
        else:
            rest[-1][0] = product.astype(BF)

    @pl.when(step < 6)
    def _():
        right = jnp.concatenate([grads_ref[pair, 0] for pair in range(8)], 1)
        finish(hidden_ref[0], hidden_ref[1], right)

    @pl.when(step >= 6)
    def _():
        finish(mixed_ref[0, 0], mixed_ref[1, 0], last_ref[...])


def early_products(ids, hidden, returned, last, arrived=None, waits=()):
    def feature(i, ids_ref):
        return 2 * (i % 2) + ids_ref[CORE]

    in_specs = [
        pl.BlockSpec((2, ROWS, 128), lambda i, c: (feature(i, c), 0, 0)),
        pl.BlockSpec((2, 1, ROWS, 128), lambda i, c: (feature(i, c), 0, 0, 0)),
        pl.BlockSpec((8, 1, ROWS, 128), lambda i, c: (0, jnp.minimum(i // 2, 2) + 1, 0, 0)),
        pl.BlockSpec((ROWS, D), lambda i, c: (0, 0)),
    ]
    operands = [hidden, returned, returned, last]
    if arrived is None:
        return prefetched(
            functools.partial(early_kernel, False), ids, operands + [pinned(wait) for wait in waits],
            in_specs + [unused] * len(waits),
            pl.BlockSpec((1, ROWS, D), lambda i, c: (i, 0, 0)),
            jax.ShapeDtypeStruct((8, ROWS, D), BF), "early_first", (8,),
        )
    return prefetched(
        functools.partial(early_kernel, True), ids, operands + [arrived, *map(pinned, waits)],
        in_specs + [pl.BlockSpec((1, ROWS, D), lambda i, c: (i, 0, 0))] + [unused] * len(waits),
        [pl.BlockSpec((1, 128, 512), lambda i, c: (i, 0, 0))] * 4,
        [pltpu.HBM((8, 128, 512), BF), jax.ShapeDtypeStruct((8, 128, 512), BF)] * 2, "early_add", (8,),
        [pltpu.VMEM((ROWS, D), F32)],
    )


def sum_split_kernel(split, count, inputs, ids_ref, *refs):
    total_ref = refs[-1]
    total = refs[0][0].astype(F32)
    for ref in refs[1:inputs]:
        total += ref[0].astype(F32)
    total_ref[...] = total
    share = total_ref.shape[0] // count
    for partner, out_ref in enumerate(refs[-1 - count : -1]):
        out_ref[0] = rows_of(total_ref, (ids_ref[split] ^ partner) * share, share).astype(BF)


def sum_split(ids, parts, split, count, name, waits=()):
    blocks, rows, columns = parts[0].shape
    return prefetched(
        functools.partial(sum_split_kernel, split, count, len(parts)), ids, [*parts, *map(pinned, waits)],
        [pl.BlockSpec((1, rows, columns), lambda i, c: (i, 0, 0))] * len(parts)
        + [unused] * len(waits),
        [pl.BlockSpec((1, rows // count, columns), lambda i, c: (i, 0, 0))] * count,
        [jax.ShapeDtypeStruct((blocks, rows // count, columns), BF)] * count, name, (blocks,),
        [pltpu.VMEM((rows, columns), F32)],
    )


def early_half_kernel(ids_ref, left_ref, left_in, right_ref, right_in, own_ref, *outs):
    for columns, (ref, arrived) in enumerate(((left_ref, left_in), (right_ref, right_in))):
        total = (ref[...].astype(F32) + arrived[...].astype(F32)).astype(BF)
        own_ref[:, :, 512 * columns : 512 * columns + 512] = total[:, :64]
        outs[columns][...] = total[:, 64:]


def early_half(ids, parts):
    narrow = pl.BlockSpec((2, 64, 512), lambda i, c: (i, 0, 0))
    return prefetched(
        early_half_kernel, ids, parts,
        [pl.BlockSpec((2, 128, 512), lambda i, c: (i, 0, 0))] * 4,
        [pl.BlockSpec((2, 64, D), lambda i, c: (i, 0, 0)), narrow, narrow],
        [pltpu.HBM((8, 64, D), BF)] + [jax.ShapeDtypeStruct((8, 64, 512), BF)] * 2,
        "early_half", (4,),
    )


def early_z_kernel(ids_ref, own_ref, left_ref, right_ref, keep_ref, give_ref):
    for other, out_ref in enumerate((keep_ref, give_ref)):
        first = pl.multiple_of((ids_ref[YLO] ^ other) * 32, 32)
        for columns, ref in enumerate((left_ref, right_ref)):
            lanes = slice(512 * columns, 512 * columns + 512)
            out_ref[:, :, lanes] = (
                own_ref[:, pl.ds(first, 32), lanes].astype(F32)
                + ref[:, pl.ds(first, 32), :].astype(F32)
            ).astype(BF)


def early_sums(ids, own, left, right):
    narrow = pl.BlockSpec((2, 64, 512), lambda i, c: (i, 0, 0))
    keep, give = prefetched(
        early_z_kernel, ids, [own, left, right],
        [pl.BlockSpec((2, 64, D), lambda i, c: (i, 0, 0)), narrow, narrow],
        [pl.BlockSpec((2, 32, D), lambda i, c: (i, 0, 0))] * 2,
        [pltpu.HBM((8, 32, D), BF), jax.ShapeDtypeStruct((8, 32, D), BF)], "early_z", (4,),
    )
    return keep, swap(give, "mode", 1)


WIDE = 384 + D


def gather_hidden(keep, give):
    chip = jnp.concatenate([keep, swap(give, "agent", 1)], 0)
    here = jnp.stack([chip, swap(chip, "agent", 2)])
    return here


def late_kernel(ids_ref, *refs):
    hiddens, first_ref, second_ref, mixed_ref, after_ref, mine_ref, *theirs_refs, total_ref = (
        refs[:4],
        *refs[4:8],
        *refs[-4:],
    )
    step = pl.program_id(0)
    core = ids_ref[CORE]

    @pl.when(step == 0)
    def _():
        total_ref[...] = jnp.zeros_like(total_ref)

    for partner, ref in enumerate(hiddens):

        @pl.when(step // 2 == partner)
        def _(ref=ref):
            right = jnp.concatenate(
                [
                    jnp.concatenate([source[0, slot] for slot in range(3)], 1)
                    for source in (first_ref, second_ref)
                ],
                0,
            )
            total_ref[...] += dot_tn(right, ref[0])

    for block in range(4):

        @pl.when(step == 8 + block)
        def _(block=block):
            rows = total_ref[:, 256 * block : 256 * block + 256].T.astype(BF)
            left = jnp.concatenate([mixed_ref[0], mixed_ref[1]], 1)
            other = dot_tn(left, after_ref[...]).astype(BF)

            @pl.when(core == block % 2)
            def _():
                mine_ref[block // 2, :, :384] = rows
                mine_ref[block // 2, :, 384:] = other

            @pl.when(core != block % 2)
            def _():
                theirs_refs[block // 2][:, :384] = rows
                theirs_refs[block // 2][:, 384:] = other


def late_products(ids, hiddens, grads, mixed, grad_after, waits):
    def source(i, c, other):
        chip = (c[X] ^ jnp.minimum(i // 2, 3)) * 2 + (c[YHI] ^ (i % 2))
        return 2 * chip + (c[CORE] ^ other)

    in_specs = [
        pl.BlockSpec((1, ROWS, D), lambda i, c, o=o: (jnp.clip(i - 2 * o, 0, 1), 0, 0))
        for o in range(4)
    ]
    in_specs += [
        pl.BlockSpec((1, 3, 128, 128), lambda i, c, o=o: (source(i, c, o), 0, 0, 0))
        for o in range(2)
    ]
    in_specs += [
        pl.BlockSpec((2, ROWS, 128), lambda i, c: (jnp.clip(i - 8, 0, 3), 0, 0)),
        pl.BlockSpec((ROWS, D), lambda i, c: (0, 0)),
    ]
    return prefetched(
        late_kernel, ids, list(hiddens) + [grads, grads, mixed, grad_after, *map(pinned, waits)],
        in_specs + [unused] * len(waits),
        [pl.BlockSpec((2, ROWS, WIDE), lambda i, c: (0, 0, 0))]
        + [pl.BlockSpec((ROWS, WIDE), lambda i, c: (0, 0))] * 2,
        [jax.ShapeDtypeStruct((2, ROWS, WIDE), BF)]
        + [jax.ShapeDtypeStruct((ROWS, WIDE), BF)] * 2, "late_products", (12,),
        [pltpu.VMEM((384, D), F32)],
    )


def chips_kernel(ids_ref, early_ref, early_in, late_ref, late_in, *rest):
    outs, total_ref = rest[:-1], rest[-1]
    total_ref[...] = late_ref[...].astype(F32) + late_in[...].astype(F32)
    for partner, out_ref in enumerate(outs):
        chip_x = ids_ref[X] ^ partner
        lanes = pl.ds(pl.multiple_of(jnp.minimum(chip_x, 2) * 128, 128), 128)
        for n in range(2):
            block = chip_x * 2 + n
            out_ref[n, :, :D] = (early_ref[block].astype(F32) + early_in[block].astype(F32)).astype(
                BF
            )
        out_ref[:, :, D : D + 128] = total_ref[:, :, lanes].astype(BF)
        out_ref[:, :, D + 128 :] = total_ref[:, :, 384:].astype(BF)


def cross_kernel(ids_ref, *refs):
    for other, out_ref in enumerate(refs[4:]):
        row = ids_ref[YHI] ^ other
        for source, target in ((0, 0), (D + 128, 384)):
            total = refs[0][row, :, source : source + D].astype(F32)
            for ref in refs[1:4]:
                total += ref[row, :, source : source + D].astype(F32)
            for place in range(4):
                out_ref[place, :, target : target + 256] = total[
                    :, 256 * place : 256 * place + 256
                ].astype(BF)
        for partner, ref in enumerate(refs[:4]):
            out_ref[partner, :, 256:384] = ref[row, :, D : D + 128]


def last_kernel(ids_ref, keep_ref, arrived_ref, agent_ref, mode_ref):
    for place in range(4):
        lanes = slice(256 * place, 256 * place + 256)
        mode_ref[:, lanes] = keep_ref[place, :, :256].astype(F32) + arrived_ref[
            place, :, :256
        ].astype(F32)

    @pl.when(ids_ref[X] < 3)
    def _():
        for other, ref in enumerate((keep_ref, arrived_ref)):
            for partner in range(4):
                pair = (ids_ref[X] ^ partner) * 2 + (ids_ref[YHI] ^ other)
                lanes = pl.ds(pl.multiple_of(pair * 128, 128), 128)
                agent_ref[:, lanes] = ref[partner, :, 256:384].astype(F32)

    @pl.when(ids_ref[X] == 3)
    def _():
        for place in range(4):
            lanes = slice(256 * place, 256 * place + 256)
            agent_ref[:, lanes] = keep_ref[place, :, 384:].astype(F32) + arrived_ref[
                place, :, 384:
            ].astype(F32)


def chip_sums(ids, early, late):
    parts = prefetched(
        chips_kernel, ids, [*early, *late],
        [fixed((8, 32, D))] * 2 + [fixed((2, 32, WIDE))] * 2, [fixed((2, 32, 128 + 2 * D))] * 4,
        [jax.ShapeDtypeStruct((2, 32, 128 + 2 * D), BF)] * 4, "chips", (1,),
        [pltpu.VMEM((2, 32, WIDE), F32)],
    )
    keep, give = prefetched(
        cross_kernel, ids, swap_all(parts, "agent", 4),
        [fixed((2, 32, 128 + 2 * D))] * 4, [fixed((4, 32, 640))] * 2,
        [jax.ShapeDtypeStruct((4, 32, 640), BF)] * 2, "cross", (1,),
    )
    return prefetched(
        last_kernel, ids, [keep, swap(give, "agent", 2)],
        [fixed((4, 32, 640))] * 2, [fixed((32, D))] * 2,
        [jax.ShapeDtypeStruct((32, D), F32)] * 2, "last", (1,),
    )


def late_add_kernel(ids_ref, mine_ref, first_ref, second_ref, *rest):
    total_ref = rest[-1]
    for block, ref in enumerate((first_ref, second_ref)):
        total_ref[...] = mine_ref[block].astype(F32) + ref[...].astype(F32)
        for partner, out_ref in enumerate(rest[-5:-1]):
            out_ref[block] = rows_of(total_ref, (ids_ref[Z] ^ partner) * 64, 64).astype(BF)


def late_sums(ids, mine, first, second, waits):
    parts = prefetched(
        late_add_kernel, ids,
        [mine, swap(first, "agent", 1), swap(second, "agent", 1)],
        [fixed((2, ROWS, WIDE))] + [fixed((ROWS, WIDE))] * 2,
        [fixed((2, 64, WIDE))] * 4,
        [pltpu.HBM((2, 64, WIDE), BF)] + [jax.ShapeDtypeStruct((2, 64, WIDE), BF)] * 3, "late_add", (1,),
        [pltpu.VMEM((ROWS, WIDE), F32)],
    )
    keep, give = sum_split(ids, swap_all(parts, "mode", 2), YLO, 2, "late_z", waits)
    return keep, swap(give, "mode", 1)


def exchange(values, axis):
    return lax.all_to_all(values, axis, split_axis=0, concat_axis=0, tiled=True)


def local(tokens, cotangent, weights, agent_mask):
    agent, mode = lax.axis_index("agent"), lax.axis_index("mode")
    ids = jnp.stack(
        [agent & 1, mode, agent >> 1, mode >> 1, mode & 1, agent >> 2, (agent >> 1) & 1]
    ).astype(jnp.int32)
    other_ids = ids.at[CORE].set(1 - ids[CORE])
    token_rows = tokens.reshape(ROWS, D)
    grad_rows = cotangent.reshape(ROWS, D)
    offset = jnp.where(agent_mask == 1, 0.0, masked_score).astype(F32).reshape(1, 128)

    outgoing, tokens_a, hidden_keep, hidden_give = enter(ids, token_rows, weights)
    arrived_one = exchange(outgoing, "agent")
    hidden_here = gather_hidden(hidden_keep, hidden_give)
    mixed, tables = agent_forward(arrived_one, offset)
    mixed_one = exchange(mixed, "agent").reshape(8, ROWS, 128)
    outgoing, after, hidden_two, cotangent_m = middle(
        tokens_a, mixed_one, grad_rows, weights, [hidden_here]
    )
    arrived_two = exchange(outgoing.reshape(8, 1024, 128), "mode").reshape(8, 4, ROWS, 128)
    hiddens = [hidden_here] + [swap(hidden_here, "agent", 4 * o) for o in range(1, 4)]
    returning = mode_attention(arrived_two, hiddens[1::2])
    returned_two = exchange(returning.reshape(8, 1024, 128), "mode").reshape(8, 4, ROWS, 128)
    early = (hidden_two, returned_two, cotangent_m)
    theirs = early_products(other_ids, *early, None, hiddens[2:3])
    outgoing, grad_after = turn(returned_two, cotangent_m, after, weights, [theirs])
    upstream = exchange(outgoing, "agent")
    parts = early_products(ids, *early, swap(theirs, "agent", 1), [grad_after])
    arrived_half = swap(parts[1], "mode", 2)
    returning = agent_backward(arrived_one, upstream, tables, [])
    own, left, right = early_half(ids, [parts[0], arrived_half, parts[2], swap(parts[3], "mode", 6)])
    left, right = swap(left, "mode", 6), swap(right, "mode", 2)
    returned_one = exchange(returning.reshape(16, 384, 128), "agent").reshape(16, 3, 128, 128)
    late_parts = late_products(ids, hiddens, returning, mixed_one, grad_after, [])
    token_grads = leave(returned_one, tokens_a, grad_after, weights)
    late = late_sums(ids, *late_parts, [token_grads])
    early = early_sums(ids, own, left, right)
    agent_weight_grads, mode_weight_grads = chip_sums(ids, early, late)
    return (token_grads.reshape(tokens.shape), agent_weight_grads, mode_weight_grads)


def solution(mesh):
    placed = (P("agent", "mode", None, None), P("agent", "mode", None, None), P(), P())
    return jax.shard_map(
        local,
        mesh=mesh,
        in_specs=placed,
        out_specs=(
            P("agent", "mode", None, None),
            P(("agent", "mode"), None),
            P(("agent", "mode"), None),
        ),
        check_vma=False,
    )
```

```python
import functools

import jax
import jax.numpy as jnp
from jax import lax
from jax.experimental import pallas as pl
from jax.experimental.pallas import tpu as pltpu
from jax.sharding import PartitionSpec as P

epsilon = 1e-06
masked_score = -1000000000.0

BF = jnp.bfloat16
F32 = jnp.float32
D = 1024
ROWS = 256
SCALE = 0.125
MIB = 1024 * 1024


def decode(row, order):
    if order == "o":
        return row >> 5, (row >> 2) & 7, row & 3
    if order == "a":
        return row & 7, row >> 5, (row >> 3) & 3
    return (row >> 3) & 7, row & 7, row >> 6


def encode(agent, mode, step, order):
    if order == "o":
        return agent * 32 + mode * 4 + step
    if order == "a":
        return mode * 32 + step * 8 + agent
    return step * 64 + agent * 8 + mode


def reorder(values, source, target):
    rows = lax.broadcasted_iota(jnp.int32, (ROWS, ROWS), 0)
    columns = lax.broadcasted_iota(jnp.int32, (ROWS, ROWS), 1)
    chosen = encode(*decode(rows, target), source)
    table = (chosen == columns).astype(F32).astype(BF)
    return jnp.dot(table, values, preferred_element_type=F32).astype(BF)


def dot_nt(left, right):
    return lax.dot_general(left, right, (((1,), (1,)), ((), ())), preferred_element_type=F32)


def dot_tn(left, right):
    return lax.dot_general(left, right, (((0,), (0,)), ((), ())), preferred_element_type=F32)


def factor_of(wide):
    return lax.rsqrt(jnp.mean(wide * wide, -1, keepdims=True) + epsilon)


def normalize_back(values, upstream):
    wide = values.astype(F32)
    factor = factor_of(wide)
    normed = wide * factor
    return factor * (upstream - normed * jnp.mean(upstream * normed, -1, keepdims=True))


def fetch(slots, weights_ref, held_ref, sems_ref):
    copies = [
        pltpu.make_async_copy(weights_ref.at[slot], held_ref.at[n], sems_ref.at[n])
        for n, slot in enumerate(slots)
    ]
    step = pl.program_id(0)

    @pl.when(step == 0)
    def _():
        for copy in copies:
            copy.start()

    def ready():
        for n, copy in enumerate(copies):

            @pl.when(step == n)
            def _(copy=copy):
                copy.wait()

        return held_ref[step]

    return ready


def pinned(operand):
    return pltpu.with_memory_space_constraint(operand, pltpu.HBM)


def held(count):
    return [pltpu.VMEM((count, D, D), BF), pltpu.SemaphoreType.DMA((count,))]


def params(limit=32):
    return pltpu.CompilerParams(vmem_limit_bytes=limit * MIB)


def cost(flops, read):
    return pl.CostEstimate(flops=int(flops), bytes_accessed=int(read), transcendentals=0)


unused = pl.BlockSpec(memory_space=pl.ANY)


def fixed(shape):
    return pl.BlockSpec(shape, lambda *i: (0,) * len(shape))


def stack_heads(values):
    lanes = lax.broadcasted_iota(jnp.int32, (1, 128), 1)
    first = (lanes < 64).astype(F32).astype(BF)
    second = (lanes >= 64).astype(F32).astype(BF)
    return jnp.concatenate([values * first, values * second], 0)


def beside(table):
    return jnp.concatenate([table[:128], table[128:]], 1)


def probabilities(query_stack, keys, offset):
    scores = dot_nt(query_stack, keys) * SCALE + offset
    raised = jnp.exp(scores - jnp.max(scores, -1, keepdims=True))
    return raised / jnp.sum(raised, -1, keepdims=True)


def attend(table, values):
    return jnp.dot(beside(table.astype(BF)), stack_heads(values), preferred_element_type=F32)


def attention_back(table, query_stack, keys, values, upstream):
    upstream_stack = stack_heads(upstream)
    through = dot_nt(upstream_stack, values)
    value_grad = dot_tn(table.astype(BF), upstream_stack)
    centre = jnp.sum(through * table, -1, keepdims=True)
    score_grad = (table * (through - centre) * SCALE).astype(BF)
    query_grad = jnp.dot(beside(score_grad), stack_heads(keys), preferred_element_type=F32)
    keys_grad = dot_tn(score_grad, query_stack)
    return query_grad, keys_grad, value_grad


def enter_kernel(
    ids_ref, tokens_ref, weights_ref,
    send_ref, tokens_out_ref, keep_ref, give_ref, hidden_ref, held_ref, sems_ref,
):
    step = pl.program_id(0)
    ready = fetch((0, 1, 2), weights_ref, held_ref, sems_ref)

    @pl.when(step == 0)
    def _():
        rows = reorder(tokens_ref[...], "o", "a")
        tokens_out_ref[...] = rows
        wide = rows.astype(F32)
        hidden = (wide * factor_of(wide)).astype(BF)
        hidden_ref[...] = hidden
        core = ids_ref[0]

        @pl.when(core == 0)
        def _():
            keep_ref[...] = hidden[:128]
            give_ref[...] = hidden[128:]

        @pl.when(core == 1)
        def _():
            keep_ref[...] = hidden[128:]
            give_ref[...] = hidden[:128]

    result = jnp.dot(hidden_ref[...], ready(), preferred_element_type=F32).astype(BF)
    for pair in range(8):
        for half in range(2):
            send_ref[2 * pair + half] = result[
                128 * half : 128 * half + 128, 128 * pair : 128 * pair + 128
            ]


def enter(ids, tokens, weights):
    return pl.pallas_call(
        enter_kernel,
        grid_spec=pltpu.PrefetchScalarGridSpec(
            num_scalar_prefetch=1,
            grid=(3,),
            in_specs=[fixed((ROWS, D)), unused],
            out_specs=[
                pl.BlockSpec((16, 128, 128), lambda i, c: (0, i, 0)),
                fixed((ROWS, D)),
                fixed((128, D)),
                fixed((128, D)),
            ],
            scratch_shapes=[pltpu.VMEM((ROWS, D), BF)] + held(3),
        ),
        out_shape=[
            jax.ShapeDtypeStruct((16, 384, 128), BF),
            pltpu.HBM((ROWS, D), BF),
            pltpu.HBM((128, D), BF),
            jax.ShapeDtypeStruct((128, D), BF),
        ],
        compiler_params=params(45),
        cost_estimate=cost(3 * 2 * ROWS * D * D, 8 * MIB),
        name="enter",
    )(ids, tokens, pinned(weights))


def agent_rows(block, step):
    return block[:, 8 * step : 8 * step + 8, :].reshape(128, 128).astype(BF)


def agent_forward_kernel(query_ref, keys_ref, values_ref, offset_ref, out_ref, table_ref):
    query = query_ref[...].astype(F32)
    keys = keys_ref[...].astype(F32)
    values = values_ref[...].astype(F32)
    offset = offset_ref[...]
    outs = []
    for step in range(4):
        table = probabilities(
            stack_heads(agent_rows(query, step)), agent_rows(keys, step), offset
        )
        table_ref[0, step] = table
        outs.append(attend(table, agent_rows(values, step)).reshape(16, 8, 128))
    out_ref[...] = jnp.concatenate(outs, 1).astype(BF)


def agent_specs():
    return [pl.BlockSpec((16, 32, 128), lambda i, k=k: (0, 4 * k + i, 0)) for k in range(3)]


def agent_forward(arrived, offset):
    return pl.pallas_call(
        agent_forward_kernel,
        grid=(4,),
        in_specs=agent_specs() + [fixed((1, 128))],
        out_specs=[
            pl.BlockSpec((16, 32, 128), lambda i: (0, i, 0)),
            pl.BlockSpec((1, 4, 256, 128), lambda i: (i, 0, 0, 0)),
        ],
        out_shape=[
            jax.ShapeDtypeStruct((16, 128, 128), BF),
            pltpu.HBM((4, 4, 256, 128), F32),
        ],
        compiler_params=params(),
        cost_estimate=cost(3e9, 4 * MIB),
        name="agent_forward",
    )(arrived, arrived, arrived, offset)


def agent_backward_kernel(
    query_ref, keys_ref, values_ref, upstream_ref, table_ref, query_out, keys_out, values_out
):
    query = query_ref[...].astype(F32)
    keys = keys_ref[...].astype(F32)
    values = values_ref[...].astype(F32)
    upstream = upstream_ref[...].astype(F32)
    outs = [[], [], []]
    for step in range(4):
        grads = attention_back(
            table_ref[0, step],
            stack_heads(agent_rows(query, step)),
            agent_rows(keys, step),
            agent_rows(values, step),
            agent_rows(upstream, step),
        )
        for kept, grad in zip(outs, grads):
            kept.append(grad.reshape(16, 8, 128))
    for ref, kept in zip((query_out, keys_out, values_out), outs):
        ref[...] = jnp.concatenate(kept, 1).astype(BF)


def agent_backward_all_kernel(q, k, v, g, table_ref, *rest):
    out_ref = rest[-1]
    agent_backward_kernel(
        q,
        k,
        v,
        g,
        table_ref,
        out_ref.at[:, 0],
        out_ref.at[:, 1],
        out_ref.at[:, 2],
    )


def agent_backward(arrived, upstream, tables, waits=()):
    return pl.pallas_call(
        agent_backward_all_kernel,
        grid=(4,),
        in_specs=agent_specs()
        + [
            pl.BlockSpec((16, 32, 128), lambda i: (0, i, 0)),
            pl.BlockSpec((1, 4, 256, 128), lambda i: (i, 0, 0, 0)),
        ]
        + [unused] * len(waits),
        out_specs=pl.BlockSpec((16, 3, 32, 128), lambda i: (0, 0, i, 0)),
        out_shape=jax.ShapeDtypeStruct((16, 3, 128, 128), BF),
        compiler_params=params(),
        cost_estimate=cost(6e9, 6 * MIB),
        name="agent_backward",
    )(*[pinned(arrived)] * 3, upstream, pinned(tables), *map(pinned, waits))


def middle_kernel(
    tokens_ref, mixed_ref, cotangent_ref, weights_ref, *rest
):
    send_ref, after_ref, hidden_out_ref, cotangent_out_ref, hidden_ref = rest[-7:-2]
    step = pl.program_id(0)
    ready = fetch((3, 4, 5, 6, 7), weights_ref, *rest[-2:])
    matrix = ready()

    @pl.when(step == 0)
    def _():
        mixed = jnp.concatenate([mixed_ref[pair] for pair in range(8)], 1)
        after = (
            tokens_ref[...].astype(F32)
            + jnp.dot(mixed, matrix, preferred_element_type=F32)
        ).astype(BF)
        after = reorder(after, "a", "m")
        after_ref[...] = after
        wide = after.astype(F32)
        hidden = (wide * factor_of(wide)).astype(BF)
        hidden_ref[...] = hidden
        for block in range(8):
            hidden_out_ref[block] = hidden[:, 128 * block : 128 * block + 128]
        cotangent_out_ref[...] = reorder(cotangent_ref[...], "o", "m")

    def send(result):
        result = result.astype(BF)
        for pair in range(8):
            send_ref[pair, 0] = result[:, 128 * pair : 128 * pair + 128]

    @pl.when((step > 0) & (step < 4))
    def _():
        send(jnp.dot(hidden_ref[...], matrix, preferred_element_type=F32))

    @pl.when(step == 4)
    def _():
        send(dot_nt(cotangent_out_ref[...], matrix))


def middle(tokens, mixed, cotangent, weights, waits=()):
    return pl.pallas_call(
        middle_kernel,
        grid=(5,),
        in_specs=[
            fixed((ROWS, D)),
            fixed((8, ROWS, 128)),
            fixed((ROWS, D)),
            unused,
        ]
        + [unused] * len(waits),
        out_specs=[
            pl.BlockSpec((8, 1, ROWS, 128), lambda i: (0, jnp.maximum(i - 1, 0), 0, 0)),
            fixed((ROWS, D)),
            fixed((8, ROWS, 128)),
            fixed((ROWS, D)),
        ],
        out_shape=[
            pltpu.HBM((8, 4, ROWS, 128), BF),
            pltpu.HBM((ROWS, D), BF),
            pltpu.HBM((8, ROWS, 128), BF),
            pltpu.HBM((ROWS, D), BF),
        ],
        scratch_shapes=[pltpu.VMEM((ROWS, D), BF)] + held(5),
        compiler_params=params(45),
        cost_estimate=cost(5 * 2 * ROWS * D * D, 13 * MIB),
        name="middle",
    )(tokens, mixed, cotangent, pinned(weights), *map(pinned, waits))


def mode_kernel(arrived_ref, *rest):
    out_ref = rest[-1]
    rows = lax.broadcasted_iota(jnp.int32, (256, 128), 0)
    columns = lax.broadcasted_iota(jnp.int32, (256, 128), 1)
    same = ((rows >> 6) & 1) == (columns >> 6)
    offset = jnp.where(same, 0.0, -1e30).astype(F32)
    for pair in range(4):

        def take(which):
            block = arrived_ref[:, which, 16 * pair : 16 * pair + 16, :].astype(F32)
            parts = [block[:, 8 * n : 8 * n + 8, :].reshape(64, 128) for n in range(2)]
            return jnp.concatenate(parts, 0).astype(BF)

        query, keys, values, upstream = (take(which) for which in range(4))
        query_stack = stack_heads(query)
        table = probabilities(query_stack, keys, offset)
        results = (attend(table, values),) + attention_back(
            table, query_stack, keys, values, upstream
        )
        for which, result in enumerate(results):
            parts = [result[64 * n : 64 * n + 64].reshape(8, 8, 128) for n in range(2)]
            out_ref[:, which, 16 * pair : 16 * pair + 16, :] = jnp.concatenate(parts, 1).astype(BF)


def mode_attention(arrived, after=()):
    spec = pl.BlockSpec((8, 4, 64, 128), lambda i: (0, 0, i, 0))
    return pl.pallas_call(
        mode_kernel,
        grid=(4,),
        in_specs=[spec] + [unused] * len(after),
        out_specs=spec,
        out_shape=pltpu.HBM((8, 4, ROWS, 128), BF),
        compiler_params=params(),
        cost_estimate=cost(8e9, 4 * MIB),
        name="mode_attention",
    )(arrived, *map(pinned, after))


def turn_kernel(returned_ref, cotangent_ref, after_ref, weights_ref, *rest):
    send_ref, grad_after_ref, total_ref = rest[-5:-2]
    step = pl.program_id(0)
    ready = fetch((4, 5, 6, 3), weights_ref, *rest[-2:])
    matrix = ready()

    @pl.when(step < 3)
    def _():
        grads = jnp.concatenate([returned_ref[pair, 0] for pair in range(8)], 1)
        product = dot_nt(grads, matrix)

        @pl.when(step == 0)
        def _():
            total_ref[...] = product

        @pl.when(step > 0)
        def _():
            total_ref[...] += product

    @pl.when(step == 3)
    def _():
        grad_after = (
            cotangent_ref[...].astype(F32) + normalize_back(after_ref[...], total_ref[...])
        ).astype(BF)
        grad_after = reorder(grad_after, "m", "a")
        grad_after_ref[...] = grad_after
        result = dot_nt(grad_after, matrix).astype(BF)
        for pair in range(8):
            for half in range(2):
                send_ref[2 * pair + half] = result[
                    128 * half : 128 * half + 128, 128 * pair : 128 * pair + 128
                ]


def turn(returned, cotangent, after, weights, waits=()):
    return pl.pallas_call(
        turn_kernel,
        grid=(4,),
        in_specs=[
            pl.BlockSpec((8, 1, ROWS, 128), lambda i: (0, jnp.minimum(i + 1, 3), 0, 0)),
            fixed((ROWS, D)),
            fixed((ROWS, D)),
            unused,
        ]
        + [unused] * len(waits),
        out_specs=[fixed((16, 128, 128)), fixed((ROWS, D))],
        out_shape=[
            pltpu.HBM((16, 128, 128), BF),
            pltpu.HBM((ROWS, D), BF),
        ],
        scratch_shapes=[pltpu.VMEM((ROWS, D), F32)] + held(4),
        compiler_params=params(45),
        cost_estimate=cost(4 * 2 * ROWS * D * D, 12 * MIB),
        name="turn",
    )(returned, cotangent, after, pinned(weights), *waits)


def whole_rows(ref):
    return jnp.concatenate([ref[:, 0].reshape(8, ROWS, 128)[pair] for pair in range(8)], 1)


def leave_kernel(returned_ref, tokens_ref, grad_after_ref, weights_ref, *rest):
    out_ref, total_ref = rest[-4:-2]
    step = pl.program_id(0)
    ready = fetch((0, 1, 2), weights_ref, *rest[-2:])
    product = dot_nt(whole_rows(returned_ref), ready())

    @pl.when(step == 0)
    def _():
        total_ref[...] = product

    @pl.when(step > 0)
    def _():
        total_ref[...] += product

    @pl.when(step == 2)
    def _():
        grads = (
            grad_after_ref[...].astype(F32) + normalize_back(tokens_ref[...], total_ref[...])
        ).astype(BF)
        out_ref[...] = reorder(grads, "a", "o")


def leave(returned, tokens, grad_after, weights, waits=()):
    return pl.pallas_call(
        leave_kernel,
        grid=(3,),
        in_specs=[
            pl.BlockSpec((16, 1, 128, 128), lambda i: (0, i, 0, 0)),
            fixed((ROWS, D)),
            fixed((ROWS, D)),
            unused,
        ]
        + [unused] * len(waits),
        out_specs=fixed((ROWS, D)),
        out_shape=jax.ShapeDtypeStruct((ROWS, D), BF),
        scratch_shapes=[pltpu.VMEM((ROWS, D), F32)] + held(3),
        compiler_params=params(45),
        cost_estimate=cost(3 * 2 * ROWS * D * D, 9 * MIB),
        name="leave",
    )(returned, tokens, grad_after, pinned(weights), *map(pinned, waits))


CORE, MODE, CHIP, Z, YLO, X, YHI = range(7)


def swap(values, axis, bits):
    size = lax.axis_size(axis)
    return lax.ppermute(values, axis, [(n, n ^ bits) for n in range(size)])


def swap_all(parts, axis, bit):
    return [parts[0]] + [swap(parts[o], axis, o * bit) for o in range(1, 4)]


def prefetched(kernel, ids, operands, in_specs, out_specs, out_shape, name, grid=(), scratch=()):
    return pl.pallas_call(
        kernel,
        grid_spec=pltpu.PrefetchScalarGridSpec(
            num_scalar_prefetch=1,
            grid=grid,
            in_specs=in_specs,
            out_specs=out_specs,
            scratch_shapes=list(scratch),
        ),
        out_shape=out_shape,
        compiler_params=params(),
        cost_estimate=cost(1e9, 5 * MIB),
        name=name,
    )(ids, *operands)


def rows_of(values, start, count):
    return values[pl.ds(pl.multiple_of(start, count), count), :]


def early_kernel(add, ids_ref, hidden_ref, mixed_ref, grads_ref, last_ref, *rest):
    step = pl.program_id(0)

    def finish(first, second, right):
        product = dot_tn(jnp.concatenate([first, second], 1), right)
        if add:
            arrived_ref, total_ref = rest[0], rest[-1]
            total_ref[...] = product + arrived_ref[0].astype(F32)
            for columns in range(2):
                for give in range(2):
                    out_ref = rest[2 * columns + give - 5]
                    near, far = ((0, 3), (1, 2))[give] if columns == 0 else ((0, 1), (3, 2))[give]
                    for place, partner in enumerate((near, far)):
                        rows = rows_of(total_ref, (ids_ref[Z] ^ partner) * 64, 64)
                        out_ref[0, 64 * place : 64 * place + 64] = rows[
                            :, 512 * columns : 512 * columns + 512
                        ].astype(BF)
        else:
            rest[-1][0] = product.astype(BF)

    @pl.when(step < 6)
    def _():
        right = jnp.concatenate([grads_ref[pair, 0] for pair in range(8)], 1)
        finish(hidden_ref[0], hidden_ref[1], right)

    @pl.when(step >= 6)
    def _():
        finish(mixed_ref[0, 0], mixed_ref[1, 0], last_ref[...])


def early_products(ids, hidden, returned, last, arrived=None, waits=()):
    def feature(i, ids_ref):
        return 2 * (i % 2) + ids_ref[CORE]

    in_specs = [
        pl.BlockSpec((2, ROWS, 128), lambda i, c: (feature(i, c), 0, 0)),
        pl.BlockSpec((2, 1, ROWS, 128), lambda i, c: (feature(i, c), 0, 0, 0)),
        pl.BlockSpec((8, 1, ROWS, 128), lambda i, c: (0, jnp.minimum(i // 2, 2) + 1, 0, 0)),
        pl.BlockSpec((ROWS, D), lambda i, c: (0, 0)),
    ]
    operands = [pinned(hidden), returned, returned, pinned(last)]
    if arrived is None:
        return prefetched(
            functools.partial(early_kernel, False), ids, operands + [pinned(wait) for wait in waits],
            in_specs + [unused] * len(waits),
            pl.BlockSpec((1, ROWS, D), lambda i, c: (i, 0, 0)),
            jax.ShapeDtypeStruct((8, ROWS, D), BF), "early_first", (8,),
        )
    return prefetched(
        functools.partial(early_kernel, True), ids, operands + [arrived, *map(pinned, waits)],
        in_specs + [pl.BlockSpec((1, ROWS, D), lambda i, c: (i, 0, 0))] + [unused] * len(waits),
        [pl.BlockSpec((1, 128, 512), lambda i, c: (i, 0, 0))] * 4,
        [pltpu.HBM((8, 128, 512), BF), jax.ShapeDtypeStruct((8, 128, 512), BF)] * 2, "early_add", (8,),
        [pltpu.VMEM((ROWS, D), F32)],
    )


def sum_split_kernel(split, count, inputs, ids_ref, *refs):
    total_ref = refs[-1]
    total = refs[0][0].astype(F32)
    for ref in refs[1:inputs]:
        total += ref[0].astype(F32)
    total_ref[...] = total
    share = total_ref.shape[0] // count
    for partner, out_ref in enumerate(refs[-1 - count : -1]):
        out_ref[0] = rows_of(total_ref, (ids_ref[split] ^ partner) * share, share).astype(BF)


def sum_split(ids, parts, split, count, name, waits=()):
    blocks, rows, columns = parts[0].shape
    return prefetched(
        functools.partial(sum_split_kernel, split, count, len(parts)), ids, [*parts, *map(pinned, waits)],
        [pl.BlockSpec((1, rows, columns), lambda i, c: (i, 0, 0))] * len(parts)
        + [unused] * len(waits),
        [pl.BlockSpec((1, rows // count, columns), lambda i, c: (i, 0, 0))] * count,
        [jax.ShapeDtypeStruct((blocks, rows // count, columns), BF)] * count, name, (blocks,),
        [pltpu.VMEM((rows, columns), F32)],
    )


def early_half_kernel(ids_ref, left_ref, left_in, right_ref, right_in, own_ref, *outs):
    for columns, (ref, arrived) in enumerate(((left_ref, left_in), (right_ref, right_in))):
        total = (ref[...].astype(F32) + arrived[...].astype(F32)).astype(BF)
        own_ref[:, :, 512 * columns : 512 * columns + 512] = total[:, :64]
        outs[columns][...] = total[:, 64:]


def early_half(ids, parts):
    narrow = pl.BlockSpec((2, 64, 512), lambda i, c: (i, 0, 0))
    return prefetched(
        early_half_kernel, ids, parts,
        [pl.BlockSpec((2, 128, 512), lambda i, c: (i, 0, 0))] * 4,
        [pl.BlockSpec((2, 64, D), lambda i, c: (i, 0, 0)), narrow, narrow],
        [pltpu.HBM((8, 64, D), BF)] + [jax.ShapeDtypeStruct((8, 64, 512), BF)] * 2,
        "early_half", (4,),
    )


def early_z_kernel(ids_ref, own_ref, left_ref, right_ref, keep_ref, give_ref):
    for other, out_ref in enumerate((keep_ref, give_ref)):
        first = pl.multiple_of((ids_ref[YLO] ^ other) * 32, 32)
        for columns, ref in enumerate((left_ref, right_ref)):
            lanes = slice(512 * columns, 512 * columns + 512)
            out_ref[:, :, lanes] = (
                own_ref[:, pl.ds(first, 32), lanes].astype(F32)
                + ref[:, pl.ds(first, 32), :].astype(F32)
            ).astype(BF)


def early_sums(ids, own, left, right):
    narrow = pl.BlockSpec((2, 64, 512), lambda i, c: (i, 0, 0))
    keep, give = prefetched(
        early_z_kernel, ids, [own, left, right],
        [pl.BlockSpec((2, 64, D), lambda i, c: (i, 0, 0)), narrow, narrow],
        [pl.BlockSpec((2, 32, D), lambda i, c: (i, 0, 0))] * 2,
        [pltpu.HBM((8, 32, D), BF), jax.ShapeDtypeStruct((8, 32, D), BF)], "early_z", (4,),
    )
    return keep, swap(give, "mode", 1)


WIDE = 384 + D


def gather_hidden(keep, give):
    chip = jnp.concatenate([keep, swap(give, "agent", 1)], 0)
    here = jnp.stack([chip, swap(chip, "agent", 2)])
    return here


def late_kernel(ids_ref, *refs):
    hiddens, first_ref, second_ref, mixed_ref, after_ref, mine_ref, *theirs_refs, total_ref = (
        refs[:4],
        *refs[4:8],
        *refs[-4:],
    )
    step = pl.program_id(0)
    core = ids_ref[CORE]

    @pl.when(step == 0)
    def _():
        total_ref[...] = jnp.zeros_like(total_ref)

    for partner, ref in enumerate(hiddens):

        @pl.when(step // 2 == partner)
        def _(ref=ref):
            right = jnp.concatenate(
                [
                    jnp.concatenate([source[0, slot] for slot in range(3)], 1)
                    for source in (first_ref, second_ref)
                ],
                0,
            )
            total_ref[...] += dot_tn(right, ref[0])

    for block in range(4):

        @pl.when(step == 8 + block)
        def _(block=block):
            rows = total_ref[:, 256 * block : 256 * block + 256].T.astype(BF)
            left = jnp.concatenate([mixed_ref[0], mixed_ref[1]], 1)
            other = dot_tn(left, after_ref[...]).astype(BF)

            @pl.when(core == block % 2)
            def _():
                mine_ref[block // 2, :, :384] = rows
                mine_ref[block // 2, :, 384:] = other

            @pl.when(core != block % 2)
            def _():
                theirs_refs[block // 2][:, :384] = rows
                theirs_refs[block // 2][:, 384:] = other


def late_products(ids, hiddens, grads, mixed, grad_after, waits):
    def source(i, c, other):
        chip = (c[X] ^ jnp.minimum(i // 2, 3)) * 2 + (c[YHI] ^ (i % 2))
        return 2 * chip + (c[CORE] ^ other)

    in_specs = [
        pl.BlockSpec((1, ROWS, D), lambda i, c, o=o: (jnp.clip(i - 2 * o, 0, 1), 0, 0))
        for o in range(4)
    ]
    in_specs += [
        pl.BlockSpec((1, 3, 128, 128), lambda i, c, o=o: (source(i, c, o), 0, 0, 0))
        for o in range(2)
    ]
    in_specs += [
        pl.BlockSpec((2, ROWS, 128), lambda i, c: (jnp.clip(i - 8, 0, 3), 0, 0)),
        pl.BlockSpec((ROWS, D), lambda i, c: (0, 0)),
    ]
    return prefetched(
        late_kernel, ids, list(map(pinned, hiddens)) + [grads, grads, pinned(mixed), grad_after, *map(pinned, waits)],
        in_specs + [unused] * len(waits),
        [pl.BlockSpec((2, ROWS, WIDE), lambda i, c: (0, 0, 0))]
        + [pl.BlockSpec((ROWS, WIDE), lambda i, c: (0, 0))] * 2,
        [jax.ShapeDtypeStruct((2, ROWS, WIDE), BF)]
        + [jax.ShapeDtypeStruct((ROWS, WIDE), BF)] * 2, "late_products", (12,),
        [pltpu.VMEM((384, D), F32)],
    )


def chips_kernel(ids_ref, early_ref, early_in, late_ref, late_in, *rest):
    outs, total_ref = rest[:-1], rest[-1]
    total_ref[...] = late_ref[...].astype(F32) + late_in[...].astype(F32)
    for partner, out_ref in enumerate(outs):
        chip_x = ids_ref[X] ^ partner
        lanes = pl.ds(pl.multiple_of(jnp.minimum(chip_x, 2) * 128, 128), 128)
        for n in range(2):
            block = chip_x * 2 + n
            out_ref[n, :, :D] = (early_ref[block].astype(F32) + early_in[block].astype(F32)).astype(
                BF
            )
        out_ref[:, :, D : D + 128] = total_ref[:, :, lanes].astype(BF)
        out_ref[:, :, D + 128 :] = total_ref[:, :, 384:].astype(BF)


def cross_kernel(ids_ref, *refs):
    for other, out_ref in enumerate(refs[4:]):
        row = ids_ref[YHI] ^ other
        for source, target in ((0, 0), (D + 128, 384)):
            total = refs[0][row, :, source : source + D].astype(F32)
            for ref in refs[1:4]:
                total += ref[row, :, source : source + D].astype(F32)
            for place in range(4):
                out_ref[place, :, target : target + 256] = total[
                    :, 256 * place : 256 * place + 256
                ].astype(BF)
        for partner, ref in enumerate(refs[:4]):
            out_ref[partner, :, 256:384] = ref[row, :, D : D + 128]


def last_kernel(ids_ref, keep_ref, arrived_ref, agent_ref, mode_ref):
    for place in range(4):
        lanes = slice(256 * place, 256 * place + 256)
        mode_ref[:, lanes] = keep_ref[place, :, :256].astype(F32) + arrived_ref[
            place, :, :256
        ].astype(F32)

    @pl.when(ids_ref[X] < 3)
    def _():
        for other, ref in enumerate((keep_ref, arrived_ref)):
            for partner in range(4):
                pair = (ids_ref[X] ^ partner) * 2 + (ids_ref[YHI] ^ other)
                lanes = pl.ds(pl.multiple_of(pair * 128, 128), 128)
                agent_ref[:, lanes] = ref[partner, :, 256:384].astype(F32)

    @pl.when(ids_ref[X] == 3)
    def _():
        for place in range(4):
            lanes = slice(256 * place, 256 * place + 256)
            agent_ref[:, lanes] = keep_ref[place, :, 384:].astype(F32) + arrived_ref[
                place, :, 384:
            ].astype(F32)


def chip_sums(ids, early, late):
    parts = prefetched(
        chips_kernel, ids, [*early, *late],
        [fixed((8, 32, D))] * 2 + [fixed((2, 32, WIDE))] * 2, [fixed((2, 32, 128 + 2 * D))] * 4,
        [jax.ShapeDtypeStruct((2, 32, 128 + 2 * D), BF)] * 4, "chips", (1,),
        [pltpu.VMEM((2, 32, WIDE), F32)],
    )
    keep, give = prefetched(
        cross_kernel, ids, swap_all(parts, "agent", 4),
        [fixed((2, 32, 128 + 2 * D))] * 4, [fixed((4, 32, 640))] * 2,
        [jax.ShapeDtypeStruct((4, 32, 640), BF)] * 2, "cross", (1,),
    )
    return prefetched(
        last_kernel, ids, [keep, swap(give, "agent", 2)],
        [fixed((4, 32, 640))] * 2, [fixed((32, D))] * 2,
        [jax.ShapeDtypeStruct((32, D), F32)] * 2, "last", (1,),
    )


def late_add_kernel(ids_ref, mine_ref, first_ref, second_ref, *rest):
    total_ref = rest[-1]
    for block, ref in enumerate((first_ref, second_ref)):
        total_ref[...] = mine_ref[block].astype(F32) + ref[...].astype(F32)
        for partner, out_ref in enumerate(rest[-5:-1]):
            out_ref[block] = rows_of(total_ref, (ids_ref[Z] ^ partner) * 64, 64).astype(BF)


def late_sums(ids, mine, first, second, waits):
    parts = prefetched(
        late_add_kernel, ids,
        [mine, swap(first, "agent", 1), swap(second, "agent", 1)],
        [fixed((2, ROWS, WIDE))] + [fixed((ROWS, WIDE))] * 2,
        [fixed((2, 64, WIDE))] * 4,
        [pltpu.HBM((2, 64, WIDE), BF)] + [jax.ShapeDtypeStruct((2, 64, WIDE), BF)] * 3, "late_add", (1,),
        [pltpu.VMEM((ROWS, WIDE), F32)],
    )
    keep, give = sum_split(ids, swap_all(parts, "mode", 2), YLO, 2, "late_z", waits)
    return keep, swap(give, "mode", 1)


def exchange(values, axis):
    return lax.all_to_all(values, axis, split_axis=0, concat_axis=0, tiled=True)


def local(tokens, cotangent, weights, agent_mask):
    agent, mode = lax.axis_index("agent"), lax.axis_index("mode")
    ids = jnp.stack(
        [agent & 1, mode, agent >> 1, mode >> 1, mode & 1, agent >> 2, (agent >> 1) & 1]
    ).astype(jnp.int32)
    other_ids = ids.at[CORE].set(1 - ids[CORE])
    token_rows = tokens.reshape(ROWS, D)
    grad_rows = cotangent.reshape(ROWS, D)
    offset = jnp.where(agent_mask == 1, 0.0, masked_score).astype(F32).reshape(1, 128)

    outgoing, tokens_a, hidden_keep, hidden_give = enter(ids, token_rows, weights)
    arrived_one = exchange(outgoing, "agent")
    hidden_here = gather_hidden(hidden_keep, hidden_give)
    mixed, tables = agent_forward(arrived_one, offset)
    mixed_one = exchange(mixed, "agent").reshape(8, ROWS, 128)
    outgoing, after, hidden_two, cotangent_m = middle(
        tokens_a, mixed_one, grad_rows, weights, [hidden_here]
    )
    arrived_two = exchange(outgoing.reshape(8, 1024, 128), "mode").reshape(8, 4, ROWS, 128)
    hiddens = [hidden_here] + [swap(hidden_here, "agent", 4 * o) for o in range(1, 4)]
    returning = mode_attention(arrived_two, hiddens[1::2])
    returned_two = exchange(returning.reshape(8, 1024, 128), "mode").reshape(8, 4, ROWS, 128)
    early = (hidden_two, returned_two, cotangent_m)
    theirs = early_products(other_ids, *early, None, hiddens[2:3])
    outgoing, grad_after = turn(returned_two, cotangent_m, after, weights, [theirs])
    upstream = exchange(outgoing, "agent")
    parts = early_products(ids, *early, swap(theirs, "agent", 1), [grad_after])
    arrived_half = swap(parts[1], "mode", 2)
    returning = agent_backward(arrived_one, upstream, tables, [])
    own, left, right = early_half(ids, [parts[0], arrived_half, parts[2], swap(parts[3], "mode", 6)])
    left, right = swap(left, "mode", 6), swap(right, "mode", 2)
    returned_one = exchange(returning.reshape(16, 384, 128), "agent").reshape(16, 3, 128, 128)
    late_parts = late_products(ids, hiddens, returning, mixed_one, grad_after, [])
    token_grads = leave(returned_one, tokens_a, grad_after, weights)
    late = late_sums(ids, *late_parts, [token_grads])
    early = early_sums(ids, own, left, right)
    agent_weight_grads, mode_weight_grads = chip_sums(ids, early, late)
    return (token_grads.reshape(tokens.shape), agent_weight_grads, mode_weight_grads)


def solution(mesh):
    placed = (P("agent", "mode", None, None), P("agent", "mode", None, None), P(), P())
    return jax.shard_map(
        local,
        mesh=mesh,
        in_specs=placed,
        out_specs=(
            P("agent", "mode", None, None),
            P(("agent", "mode"), None),
            P(("agent", "mode"), None),
        ),
        check_vma=False,
    )
```

```python
import functools

import jax
import jax.numpy as jnp
from jax import lax
from jax.experimental import pallas as pl
from jax.experimental.pallas import tpu as pltpu
from jax.sharding import PartitionSpec as P

epsilon = 1e-06
masked_score = -1000000000.0

BF = jnp.bfloat16
F32 = jnp.float32
D = 1024
ROWS = 256
SCALE = 0.125
MIB = 1024 * 1024


def decode(row, order):
    if order == "o":
        return row >> 5, (row >> 2) & 7, row & 3
    if order == "a":
        return row & 7, row >> 5, (row >> 3) & 3
    return (row >> 3) & 7, row & 7, row >> 6


def encode(agent, mode, step, order):
    if order == "o":
        return agent * 32 + mode * 4 + step
    if order == "a":
        return mode * 32 + step * 8 + agent
    return step * 64 + agent * 8 + mode


def reorder(values, source, target):
    rows = lax.broadcasted_iota(jnp.int32, (ROWS, ROWS), 0)
    columns = lax.broadcasted_iota(jnp.int32, (ROWS, ROWS), 1)
    chosen = encode(*decode(rows, target), source)
    table = (chosen == columns).astype(F32).astype(BF)
    return jnp.dot(table, values, preferred_element_type=F32).astype(BF)


def dot_nt(left, right):
    return lax.dot_general(left, right, (((1,), (1,)), ((), ())), preferred_element_type=F32)


def dot_tn(left, right):
    return lax.dot_general(left, right, (((0,), (0,)), ((), ())), preferred_element_type=F32)


def factor_of(wide):
    return lax.rsqrt(jnp.mean(wide * wide, -1, keepdims=True) + epsilon)


def normalize_back(values, upstream):
    wide = values.astype(F32)
    factor = factor_of(wide)
    normed = wide * factor
    return factor * (upstream - normed * jnp.mean(upstream * normed, -1, keepdims=True))


def fetch(slots, weights_ref, held_ref, sems_ref):
    copies = [
        pltpu.make_async_copy(weights_ref.at[slot], held_ref.at[n], sems_ref.at[n])
        for n, slot in enumerate(slots)
    ]
    step = pl.program_id(0)

    @pl.when(step == 0)
    def _():
        for copy in copies:
            copy.start()

    def ready():
        for n, copy in enumerate(copies):

            @pl.when(step == n)
            def _(copy=copy):
                copy.wait()

        return held_ref[step]

    return ready


def pinned(operand):
    return pltpu.with_memory_space_constraint(operand, pltpu.HBM)


def held(count):
    return [pltpu.VMEM((count, D, D), BF), pltpu.SemaphoreType.DMA((count,))]


def params(limit=32):
    return pltpu.CompilerParams(vmem_limit_bytes=limit * MIB)


def cost(flops, read):
    return pl.CostEstimate(flops=int(flops), bytes_accessed=int(read), transcendentals=0)


unused = pl.BlockSpec(memory_space=pl.ANY)


def fixed(shape):
    return pl.BlockSpec(shape, lambda *i: (0,) * len(shape))


def stack_heads(values):
    lanes = lax.broadcasted_iota(jnp.int32, (1, 128), 1)
    first = (lanes < 64).astype(F32).astype(BF)
    second = (lanes >= 64).astype(F32).astype(BF)
    return jnp.concatenate([values * first, values * second], 0)


def beside(table):
    return jnp.concatenate([table[:128], table[128:]], 1)


def probabilities(query_stack, keys, offset):
    scores = dot_nt(query_stack, keys) * SCALE + offset
    raised = jnp.exp(scores - jnp.max(scores, -1, keepdims=True))
    return raised / jnp.sum(raised, -1, keepdims=True)


def attend(table, values):
    return jnp.dot(beside(table.astype(BF)), stack_heads(values), preferred_element_type=F32)


def attention_back(table, query_stack, keys, values, upstream):
    upstream_stack = stack_heads(upstream)
    through = dot_nt(upstream_stack, values)
    value_grad = dot_tn(table.astype(BF), upstream_stack)
    centre = jnp.sum(through * table, -1, keepdims=True)
    score_grad = (table * (through - centre) * SCALE).astype(BF)
    query_grad = jnp.dot(beside(score_grad), stack_heads(keys), preferred_element_type=F32)
    keys_grad = dot_tn(score_grad, query_stack)
    return query_grad, keys_grad, value_grad


def enter_kernel(
    ids_ref, tokens_ref, weights_ref,
    send_ref, tokens_out_ref, keep_ref, give_ref, hidden_ref, held_ref, sems_ref,
):
    step = pl.program_id(0)
    ready = fetch((0, 1, 2), weights_ref, held_ref, sems_ref)

    @pl.when(step == 0)
    def _():
        rows = reorder(tokens_ref[...], "o", "a")
        tokens_out_ref[...] = rows
        wide = rows.astype(F32)
        hidden = (wide * factor_of(wide)).astype(BF)
        hidden_ref[...] = hidden
        core = ids_ref[0]

        @pl.when(core == 0)
        def _():
            keep_ref[...] = hidden[:128]
            give_ref[...] = hidden[128:]

        @pl.when(core == 1)
        def _():
            keep_ref[...] = hidden[128:]
            give_ref[...] = hidden[:128]

    result = jnp.dot(hidden_ref[...], ready(), preferred_element_type=F32).astype(BF)
    for pair in range(8):
        for half in range(2):
            send_ref[2 * pair + half] = result[
                128 * half : 128 * half + 128, 128 * pair : 128 * pair + 128
            ]


def enter(ids, tokens, weights):
    return pl.pallas_call(
        enter_kernel,
        grid_spec=pltpu.PrefetchScalarGridSpec(
            num_scalar_prefetch=1,
            grid=(3,),
            in_specs=[fixed((ROWS, D)), unused],
            out_specs=[
                pl.BlockSpec((16, 128, 128), lambda i, c: (0, i, 0)),
                fixed((ROWS, D)),
                fixed((128, D)),
                fixed((128, D)),
            ],
            scratch_shapes=[pltpu.VMEM((ROWS, D), BF)] + held(3),
        ),
        out_shape=[
            jax.ShapeDtypeStruct((16, 384, 128), BF),
            pltpu.HBM((ROWS, D), BF),
            pltpu.HBM((128, D), BF),
            jax.ShapeDtypeStruct((128, D), BF),
        ],
        compiler_params=params(45),
        cost_estimate=cost(3 * 2 * ROWS * D * D, 8 * MIB),
        name="enter",
    )(ids, tokens, pinned(weights))


def agent_rows(block, step):
    return block[:, 8 * step : 8 * step + 8, :].reshape(128, 128).astype(BF)


def agent_forward_kernel(query_ref, keys_ref, values_ref, offset_ref, out_ref, table_ref):
    query = query_ref[...].astype(F32)
    keys = keys_ref[...].astype(F32)
    values = values_ref[...].astype(F32)
    offset = offset_ref[...]
    outs = []
    for step in range(4):
        table = probabilities(
            stack_heads(agent_rows(query, step)), agent_rows(keys, step), offset
        )
        table_ref[0, step] = table
        outs.append(attend(table, agent_rows(values, step)).reshape(16, 8, 128))
    out_ref[...] = jnp.concatenate(outs, 1).astype(BF)


def agent_specs():
    return [pl.BlockSpec((16, 32, 128), lambda i, k=k: (0, 4 * k + i, 0)) for k in range(3)]


def agent_forward(arrived, offset):
    return pl.pallas_call(
        agent_forward_kernel,
        grid=(4,),
        in_specs=agent_specs() + [fixed((1, 128))],
        out_specs=[
            pl.BlockSpec((16, 32, 128), lambda i: (0, i, 0)),
            pl.BlockSpec((1, 4, 256, 128), lambda i: (i, 0, 0, 0)),
        ],
        out_shape=[
            jax.ShapeDtypeStruct((16, 128, 128), BF),
            pltpu.HBM((4, 4, 256, 128), F32),
        ],
        compiler_params=params(),
        cost_estimate=cost(3e9, 4 * MIB),
        name="agent_forward",
    )(arrived, arrived, arrived, offset)


def agent_backward_kernel(
    query_ref, keys_ref, values_ref, upstream_ref, table_ref, query_out, keys_out, values_out
):
    query = query_ref[...].astype(F32)
    keys = keys_ref[...].astype(F32)
    values = values_ref[...].astype(F32)
    upstream = upstream_ref[...].astype(F32)
    outs = [[], [], []]
    for step in range(4):
        grads = attention_back(
            table_ref[0, step],
            stack_heads(agent_rows(query, step)),
            agent_rows(keys, step),
            agent_rows(values, step),
            agent_rows(upstream, step),
        )
        for kept, grad in zip(outs, grads):
            kept.append(grad.reshape(16, 8, 128))
    for ref, kept in zip((query_out, keys_out, values_out), outs):
        ref[...] = jnp.concatenate(kept, 1).astype(BF)


def agent_backward_all_kernel(q, k, v, g, table_ref, *rest):
    out_ref = rest[-1]
    agent_backward_kernel(
        q,
        k,
        v,
        g,
        table_ref,
        out_ref.at[:, 0],
        out_ref.at[:, 1],
        out_ref.at[:, 2],
    )


def agent_backward(arrived, upstream, tables, waits=()):
    return pl.pallas_call(
        agent_backward_all_kernel,
        grid=(4,),
        in_specs=agent_specs()
        + [
            pl.BlockSpec((16, 32, 128), lambda i: (0, i, 0)),
            pl.BlockSpec((1, 4, 256, 128), lambda i: (i, 0, 0, 0)),
        ]
        + [unused] * len(waits),
        out_specs=pl.BlockSpec((16, 3, 32, 128), lambda i: (0, 0, i, 0)),
        out_shape=jax.ShapeDtypeStruct((16, 3, 128, 128), BF),
        compiler_params=params(),
        cost_estimate=cost(6e9, 6 * MIB),
        name="agent_backward",
    )(*[pinned(arrived)] * 3, upstream, pinned(tables), *map(pinned, waits))


def middle_kernel(
    tokens_ref, mixed_ref, cotangent_ref, weights_ref, *rest
):
    send_ref, after_ref, hidden_out_ref, cotangent_out_ref, hidden_ref = rest[-7:-2]
    step = pl.program_id(0)
    ready = fetch((3, 4, 5, 6, 7), weights_ref, *rest[-2:])
    matrix = ready()

    @pl.when(step == 0)
    def _():
        mixed = jnp.concatenate([mixed_ref[pair] for pair in range(8)], 1)
        after = (
            tokens_ref[...].astype(F32)
            + jnp.dot(mixed, matrix, preferred_element_type=F32)
        ).astype(BF)
        after = reorder(after, "a", "m")
        after_ref[...] = after
        wide = after.astype(F32)
        hidden = (wide * factor_of(wide)).astype(BF)
        hidden_ref[...] = hidden
        for block in range(8):
            hidden_out_ref[block] = hidden[:, 128 * block : 128 * block + 128]
        cotangent_out_ref[...] = reorder(cotangent_ref[...], "o", "m")

    def send(result):
        result = result.astype(BF)
        for pair in range(8):
            send_ref[pair, 0] = result[:, 128 * pair : 128 * pair + 128]

    @pl.when((step > 0) & (step < 4))
    def _():
        send(jnp.dot(hidden_ref[...], matrix, preferred_element_type=F32))

    @pl.when(step == 4)
    def _():
        send(dot_nt(cotangent_out_ref[...], matrix))


def middle(tokens, mixed, cotangent, weights, waits=()):
    return pl.pallas_call(
        middle_kernel,
        grid=(5,),
        in_specs=[
            fixed((ROWS, D)),
            fixed((8, ROWS, 128)),
            fixed((ROWS, D)),
            unused,
        ]
        + [unused] * len(waits),
        out_specs=[
            pl.BlockSpec((8, 1, ROWS, 128), lambda i: (0, jnp.maximum(i - 1, 0), 0, 0)),
            fixed((ROWS, D)),
            fixed((8, ROWS, 128)),
            fixed((ROWS, D)),
        ],
        out_shape=[
            pltpu.HBM((8, 4, ROWS, 128), BF),
            pltpu.HBM((ROWS, D), BF),
            pltpu.HBM((8, ROWS, 128), BF),
            pltpu.HBM((ROWS, D), BF),
        ],
        scratch_shapes=[pltpu.VMEM((ROWS, D), BF)] + held(5),
        compiler_params=params(45),
        cost_estimate=cost(5 * 2 * ROWS * D * D, 13 * MIB),
        name="middle",
    )(tokens, mixed, cotangent, pinned(weights), *map(pinned, waits))


def mode_kernel(arrived_ref, *rest):
    out_ref = rest[-1]
    rows = lax.broadcasted_iota(jnp.int32, (256, 128), 0)
    columns = lax.broadcasted_iota(jnp.int32, (256, 128), 1)
    same = ((rows >> 6) & 1) == (columns >> 6)
    offset = jnp.where(same, 0.0, -1e30).astype(F32)
    for pair in range(4):

        def take(which):
            block = arrived_ref[:, which, 16 * pair : 16 * pair + 16, :].astype(F32)
            parts = [block[:, 8 * n : 8 * n + 8, :].reshape(64, 128) for n in range(2)]
            return jnp.concatenate(parts, 0).astype(BF)

        query, keys, values, upstream = (take(which) for which in range(4))
        query_stack = stack_heads(query)
        table = probabilities(query_stack, keys, offset)
        results = (attend(table, values),) + attention_back(
            table, query_stack, keys, values, upstream
        )
        for which, result in enumerate(results):
            parts = [result[64 * n : 64 * n + 64].reshape(8, 8, 128) for n in range(2)]
            out_ref[:, which, 16 * pair : 16 * pair + 16, :] = jnp.concatenate(parts, 1).astype(BF)


def mode_attention(arrived, after=()):
    spec = pl.BlockSpec((8, 4, 64, 128), lambda i: (0, 0, i, 0))
    return pl.pallas_call(
        mode_kernel,
        grid=(4,),
        in_specs=[spec] + [unused] * len(after),
        out_specs=spec,
        out_shape=pltpu.HBM((8, 4, ROWS, 128), BF),
        compiler_params=params(),
        cost_estimate=cost(8e9, 4 * MIB),
        name="mode_attention",
    )(arrived, *map(pinned, after))


def turn_kernel(returned_ref, cotangent_ref, after_ref, weights_ref, *rest):
    send_ref, grad_after_ref, total_ref = rest[-5:-2]
    step = pl.program_id(0)
    ready = fetch((4, 5, 6, 3), weights_ref, *rest[-2:])
    matrix = ready()

    @pl.when(step < 3)
    def _():
        grads = jnp.concatenate([returned_ref[pair, 0] for pair in range(8)], 1)
        product = dot_nt(grads, matrix)

        @pl.when(step == 0)
        def _():
            total_ref[...] = product

        @pl.when(step > 0)
        def _():
            total_ref[...] += product

    @pl.when(step == 3)
    def _():
        grad_after = (
            cotangent_ref[...].astype(F32) + normalize_back(after_ref[...], total_ref[...])
        ).astype(BF)
        grad_after = reorder(grad_after, "m", "a")
        grad_after_ref[...] = grad_after
        result = dot_nt(grad_after, matrix).astype(BF)
        for pair in range(8):
            for half in range(2):
                send_ref[2 * pair + half] = result[
                    128 * half : 128 * half + 128, 128 * pair : 128 * pair + 128
                ]


def turn(returned, cotangent, after, weights, waits=()):
    return pl.pallas_call(
        turn_kernel,
        grid=(4,),
        in_specs=[
            pl.BlockSpec((8, 1, ROWS, 128), lambda i: (0, jnp.minimum(i + 1, 3), 0, 0)),
            fixed((ROWS, D)),
            fixed((ROWS, D)),
            unused,
        ]
        + [unused] * len(waits),
        out_specs=[fixed((16, 128, 128)), fixed((ROWS, D))],
        out_shape=[
            pltpu.HBM((16, 128, 128), BF),
            pltpu.HBM((ROWS, D), BF),
        ],
        scratch_shapes=[pltpu.VMEM((ROWS, D), F32)] + held(4),
        compiler_params=params(45),
        cost_estimate=cost(4 * 2 * ROWS * D * D, 12 * MIB),
        name="turn",
    )(returned, cotangent, after, pinned(weights), *waits)


def whole_rows(ref):
    return jnp.concatenate([ref[:, 0].reshape(8, ROWS, 128)[pair] for pair in range(8)], 1)


def leave_kernel(returned_ref, tokens_ref, grad_after_ref, weights_ref, *rest):
    out_ref, total_ref = rest[-4:-2]
    step = pl.program_id(0)
    ready = fetch((0, 1, 2), weights_ref, *rest[-2:])
    product = dot_nt(whole_rows(returned_ref), ready())

    @pl.when(step == 0)
    def _():
        total_ref[...] = product

    @pl.when(step > 0)
    def _():
        total_ref[...] += product

    @pl.when(step == 2)
    def _():
        grads = (
            grad_after_ref[...].astype(F32) + normalize_back(tokens_ref[...], total_ref[...])
        ).astype(BF)
        out_ref[...] = reorder(grads, "a", "o")


def leave(returned, tokens, grad_after, weights, waits=()):
    return pl.pallas_call(
        leave_kernel,
        grid=(3,),
        in_specs=[
            pl.BlockSpec((16, 1, 128, 128), lambda i: (0, i, 0, 0)),
            fixed((ROWS, D)),
            fixed((ROWS, D)),
            unused,
        ]
        + [unused] * len(waits),
        out_specs=fixed((ROWS, D)),
        out_shape=jax.ShapeDtypeStruct((ROWS, D), BF),
        scratch_shapes=[pltpu.VMEM((ROWS, D), F32)] + held(3),
        compiler_params=params(45),
        cost_estimate=cost(3 * 2 * ROWS * D * D, 9 * MIB),
        name="leave",
    )(returned, tokens, grad_after, pinned(weights), *map(pinned, waits))


CORE, MODE, CHIP, Z, YLO, X, YHI = range(7)


def swap(values, axis, bits):
    size = lax.axis_size(axis)
    return lax.ppermute(values, axis, [(n, n ^ bits) for n in range(size)])


def swap_all(parts, axis, bit):
    return [parts[0]] + [swap(parts[o], axis, o * bit) for o in range(1, 4)]


def prefetched(kernel, ids, operands, in_specs, out_specs, out_shape, name, grid=(), scratch=()):
    return pl.pallas_call(
        kernel,
        grid_spec=pltpu.PrefetchScalarGridSpec(
            num_scalar_prefetch=1,
            grid=grid,
            in_specs=in_specs,
            out_specs=out_specs,
            scratch_shapes=list(scratch),
        ),
        out_shape=out_shape,
        compiler_params=params(),
        cost_estimate=cost(1e9, 5 * MIB),
        name=name,
    )(ids, *operands)


def rows_of(values, start, count):
    return values[pl.ds(pl.multiple_of(start, count), count), :]


def early_kernel(add, ids_ref, hidden_ref, mixed_ref, grads_ref, last_ref, *rest):
    step = pl.program_id(0)

    def finish(first, second, right):
        product = dot_tn(jnp.concatenate([first, second], 1), right)
        if add:
            arrived_ref, total_ref = rest[0], rest[-1]
            total_ref[...] = product + arrived_ref[0].astype(F32)
            for columns in range(2):
                for give in range(2):
                    out_ref = rest[2 * columns + give - 5]
                    near, far = ((0, 3), (1, 2))[give] if columns == 0 else ((0, 1), (3, 2))[give]
                    for place, partner in enumerate((near, far)):
                        rows = rows_of(total_ref, (ids_ref[Z] ^ partner) * 64, 64)
                        out_ref[0, 64 * place : 64 * place + 64] = rows[
                            :, 512 * columns : 512 * columns + 512
                        ].astype(BF)
        else:
            rest[-1][0] = product.astype(BF)

    @pl.when(step < 6)
    def _():
        right = jnp.concatenate([grads_ref[pair, 0] for pair in range(8)], 1)
        finish(hidden_ref[0], hidden_ref[1], right)

    @pl.when(step >= 6)
    def _():
        finish(mixed_ref[0, 0], mixed_ref[1, 0], last_ref[...])


def early_products(ids, hidden, returned, last, arrived=None, waits=()):
    def feature(i, ids_ref):
        return 2 * (i % 2) + ids_ref[CORE]

    in_specs = [
        pl.BlockSpec((2, ROWS, 128), lambda i, c: (feature(i, c), 0, 0)),
        pl.BlockSpec((2, 1, ROWS, 128), lambda i, c: (feature(i, c), 0, 0, 0)),
        pl.BlockSpec((8, 1, ROWS, 128), lambda i, c: (0, jnp.minimum(i // 2, 2) + 1, 0, 0)),
        pl.BlockSpec((ROWS, D), lambda i, c: (0, 0)),
    ]
    operands = [pinned(hidden), returned, returned, pinned(last)]
    if arrived is None:
        return prefetched(
            functools.partial(early_kernel, False), ids, operands + [pinned(wait) for wait in waits],
            in_specs + [unused] * len(waits),
            pl.BlockSpec((1, ROWS, D), lambda i, c: (i, 0, 0)),
            jax.ShapeDtypeStruct((8, ROWS, D), BF), "early_first", (8,),
        )
    return prefetched(
        functools.partial(early_kernel, True), ids, operands + [arrived, *map(pinned, waits)],
        in_specs + [pl.BlockSpec((1, ROWS, D), lambda i, c: (i, 0, 0))] + [unused] * len(waits),
        [pl.BlockSpec((1, 128, 512), lambda i, c: (i, 0, 0))] * 4,
        [pltpu.HBM((8, 128, 512), BF), jax.ShapeDtypeStruct((8, 128, 512), BF)] * 2, "early_add", (8,),
        [pltpu.VMEM((ROWS, D), F32)],
    )


def sum_split_kernel(split, count, inputs, ids_ref, *refs):
    total_ref = refs[-1]
    total = refs[0][0].astype(F32)
    for ref in refs[1:inputs]:
        total += ref[0].astype(F32)
    total_ref[...] = total
    share = total_ref.shape[0] // count
    for partner, out_ref in enumerate(refs[-1 - count : -1]):
        out_ref[0] = rows_of(total_ref, (ids_ref[split] ^ partner) * share, share).astype(BF)


def sum_split(ids, parts, split, count, name, waits=()):
    blocks, rows, columns = parts[0].shape
    return prefetched(
        functools.partial(sum_split_kernel, split, count, len(parts)), ids, [*parts, *map(pinned, waits)],
        [pl.BlockSpec((1, rows, columns), lambda i, c: (i, 0, 0))] * len(parts)
        + [unused] * len(waits),
        [pl.BlockSpec((1, rows // count, columns), lambda i, c: (i, 0, 0))] * count,
        [jax.ShapeDtypeStruct((blocks, rows // count, columns), BF)] * count, name, (blocks,),
        [pltpu.VMEM((rows, columns), F32)],
    )


def early_half_kernel(ids_ref, left_ref, left_in, right_ref, right_in, own_ref, *outs):
    for columns, (ref, arrived) in enumerate(((left_ref, left_in), (right_ref, right_in))):
        total = (ref[...].astype(F32) + arrived[...].astype(F32)).astype(BF)
        own_ref[:, :, 512 * columns : 512 * columns + 512] = total[:, :64]
        outs[columns][...] = total[:, 64:]


def early_half(ids, parts):
    narrow = pl.BlockSpec((2, 64, 512), lambda i, c: (i, 0, 0))
    return prefetched(
        early_half_kernel, ids, parts,
        [pl.BlockSpec((2, 128, 512), lambda i, c: (i, 0, 0))] * 4,
        [pl.BlockSpec((2, 64, D), lambda i, c: (i, 0, 0)), narrow, narrow],
        [pltpu.HBM((8, 64, D), BF)] + [jax.ShapeDtypeStruct((8, 64, 512), BF)] * 2,
        "early_half", (4,),
    )


def early_z_kernel(ids_ref, own_ref, left_ref, right_ref, *rest):
    for other, out_ref in enumerate(rest[-2:]):
        first = pl.multiple_of((ids_ref[YLO] ^ other) * 32, 32)
        for columns, ref in enumerate((left_ref, right_ref)):
            lanes = slice(512 * columns, 512 * columns + 512)
            out_ref[:, :, lanes] = (
                own_ref[:, pl.ds(first, 32), lanes].astype(F32)
                + ref[:, pl.ds(first, 32), :].astype(F32)
            ).astype(BF)


def early_sums(ids, own, left, right, waits):
    narrow = pl.BlockSpec((2, 64, 512), lambda i, c: (i, 0, 0))
    keep, give = prefetched(
        early_z_kernel, ids, [own, left, right, *map(pinned, waits)],
        [pl.BlockSpec((2, 64, D), lambda i, c: (i, 0, 0)), narrow, narrow] + [unused] * len(waits),
        [pl.BlockSpec((2, 32, D), lambda i, c: (i, 0, 0))] * 2,
        [pltpu.HBM((8, 32, D), BF), jax.ShapeDtypeStruct((8, 32, D), BF)], "early_z", (4,),
    )
    return keep, swap(give, "mode", 1)


WIDE = 384 + D


def gather_hidden(keep, give):
    chip = jnp.concatenate([keep, swap(give, "agent", 1)], 0)
    here = jnp.stack([chip, swap(chip, "agent", 2)])
    return here


def late_kernel(ids_ref, *refs):
    hiddens, first_ref, second_ref, mixed_ref, after_ref, mine_ref, *theirs_refs, total_ref = (
        refs[:4],
        *refs[4:8],
        *refs[-4:],
    )
    step = pl.program_id(0)
    core = ids_ref[CORE]

    @pl.when(step == 0)
    def _():
        total_ref[...] = jnp.zeros_like(total_ref)

    for partner, ref in enumerate(hiddens):

        @pl.when(step // 2 == partner)
        def _(ref=ref):
            right = jnp.concatenate(
                [
                    jnp.concatenate([source[0, slot] for slot in range(3)], 1)
                    for source in (first_ref, second_ref)
                ],
                0,
            )
            total_ref[...] += dot_tn(right, ref[0])

    for block in range(4):

        @pl.when(step == 8 + block)
        def _(block=block):
            rows = total_ref[:, 256 * block : 256 * block + 256].T.astype(BF)
            left = jnp.concatenate([mixed_ref[0], mixed_ref[1]], 1)
            other = dot_tn(left, after_ref[...]).astype(BF)

            @pl.when(core == block % 2)
            def _():
                mine_ref[block // 2, :, :384] = rows
                mine_ref[block // 2, :, 384:] = other

            @pl.when(core != block % 2)
            def _():
                theirs_refs[block // 2][:, :384] = rows
                theirs_refs[block // 2][:, 384:] = other


def late_products(ids, hiddens, grads, mixed, grad_after, waits):
    def source(i, c, other):
        chip = (c[X] ^ jnp.minimum(i // 2, 3)) * 2 + (c[YHI] ^ (i % 2))
        return 2 * chip + (c[CORE] ^ other)

    in_specs = [
        pl.BlockSpec((1, ROWS, D), lambda i, c, o=o: (jnp.clip(i - 2 * o, 0, 1), 0, 0))
        for o in range(4)
    ]
    in_specs += [
        pl.BlockSpec((1, 3, 128, 128), lambda i, c, o=o: (source(i, c, o), 0, 0, 0))
        for o in range(2)
    ]
    in_specs += [
        pl.BlockSpec((2, ROWS, 128), lambda i, c: (jnp.clip(i - 8, 0, 3), 0, 0)),
        pl.BlockSpec((ROWS, D), lambda i, c: (0, 0)),
    ]
    return prefetched(
        late_kernel, ids, list(map(pinned, hiddens)) + [grads, grads, pinned(mixed), grad_after, *map(pinned, waits)],
        in_specs + [unused] * len(waits),
        [pl.BlockSpec((2, ROWS, WIDE), lambda i, c: (0, 0, 0))]
        + [pl.BlockSpec((ROWS, WIDE), lambda i, c: (0, 0))] * 2,
        [jax.ShapeDtypeStruct((2, ROWS, WIDE), BF)]
        + [jax.ShapeDtypeStruct((ROWS, WIDE), BF)] * 2, "late_products", (12,),
        [pltpu.VMEM((384, D), F32)],
    )


def chips_kernel(ids_ref, early_ref, early_in, *rest):
    late, outs, total_ref = rest[:4], rest[4:-1], rest[-1]
    total_ref[...] = late[0][...].astype(F32)
    for ref in late[1:]:
        total_ref[...] += ref[...].astype(F32)
    for partner, out_ref in enumerate(outs):
        chip_x = ids_ref[X] ^ partner
        lanes = pl.ds(pl.multiple_of(jnp.minimum(chip_x, 2) * 128, 128), 128)
        for n in range(2):
            block = chip_x * 2 + n
            out_ref[n, :, :D] = (early_ref[block].astype(F32) + early_in[block].astype(F32)).astype(
                BF
            )
        out_ref[:, :, D : D + 128] = total_ref[:, :, lanes].astype(BF)
        out_ref[:, :, D + 128 :] = total_ref[:, :, 384:].astype(BF)


def cross_kernel(ids_ref, *refs):
    for other, out_ref in enumerate(refs[4:]):
        row = ids_ref[YHI] ^ other
        for source, target in ((0, 0), (D + 128, 384)):
            total = refs[0][row, :, source : source + D].astype(F32)
            for ref in refs[1:4]:
                total += ref[row, :, source : source + D].astype(F32)
            for place in range(4):
                out_ref[place, :, target : target + 256] = total[
                    :, 256 * place : 256 * place + 256
                ].astype(BF)
        for partner, ref in enumerate(refs[:4]):
            out_ref[partner, :, 256:384] = ref[row, :, D : D + 128]


def last_kernel(ids_ref, keep_ref, arrived_ref, agent_ref, mode_ref):
    for place in range(4):
        lanes = slice(256 * place, 256 * place + 256)
        mode_ref[:, lanes] = keep_ref[place, :, :256].astype(F32) + arrived_ref[
            place, :, :256
        ].astype(F32)

    @pl.when(ids_ref[X] < 3)
    def _():
        for other, ref in enumerate((keep_ref, arrived_ref)):
            for partner in range(4):
                pair = (ids_ref[X] ^ partner) * 2 + (ids_ref[YHI] ^ other)
                lanes = pl.ds(pl.multiple_of(pair * 128, 128), 128)
                agent_ref[:, lanes] = ref[partner, :, 256:384].astype(F32)

    @pl.when(ids_ref[X] == 3)
    def _():
        for place in range(4):
            lanes = slice(256 * place, 256 * place + 256)
            agent_ref[:, lanes] = keep_ref[place, :, 384:].astype(F32) + arrived_ref[
                place, :, 384:
            ].astype(F32)


def chip_sums(ids, early, late):
    parts = prefetched(
        chips_kernel, ids, [*early, *late],
        [fixed((8, 32, D))] * 2 + [fixed((2, 32, WIDE))] * 4, [fixed((2, 32, 128 + 2 * D))] * 4,
        [jax.ShapeDtypeStruct((2, 32, 128 + 2 * D), BF)] * 4, "chips", (1,),
        [pltpu.VMEM((2, 32, WIDE), F32)],
    )
    keep, give = prefetched(
        cross_kernel, ids, swap_all(parts, "agent", 4),
        [fixed((2, 32, 128 + 2 * D))] * 4, [fixed((4, 32, 640))] * 2,
        [jax.ShapeDtypeStruct((4, 32, 640), BF)] * 2, "cross", (1,),
    )
    return prefetched(
        last_kernel, ids, [keep, swap(give, "agent", 2)],
        [fixed((4, 32, 640))] * 2, [fixed((32, D))] * 2,
        [jax.ShapeDtypeStruct((32, D), F32)] * 2, "last", (1,),
    )


def late_add_kernel(ids_ref, mine_ref, first_ref, second_ref, *rest):
    total_ref = rest[-1]
    for block, ref in enumerate((first_ref, second_ref)):
        total_ref[...] = mine_ref[block].astype(F32) + ref[...].astype(F32)
        for partner, out_ref in enumerate(rest[-3:-1]):
            for z in range(4):
                first = z * 64 + (ids_ref[YLO] ^ partner) * 32
                out_ref[block, 32 * z : 32 * z + 32] = rows_of(total_ref, first, 32).astype(BF)


def late_sums(ids, mine, first, second, waits):
    keep, give = prefetched(
        late_add_kernel, ids,
        [mine, swap(first, "agent", 1), swap(second, "agent", 1)],
        [fixed((2, ROWS, WIDE))] + [fixed((ROWS, WIDE))] * 2,
        [fixed((2, 128, WIDE))] * 2,
        [pltpu.HBM((2, 128, WIDE), BF), jax.ShapeDtypeStruct((2, 128, WIDE), BF)],
        "late_add", (1,),
        [pltpu.VMEM((ROWS, WIDE), F32)],
    )
    parts = sum_split(ids, [keep, swap(give, "mode", 1)], Z, 4, "late_y", waits)
    return swap_all(parts, "mode", 2)


def exchange(values, axis):
    return lax.all_to_all(values, axis, split_axis=0, concat_axis=0, tiled=True)


def local(tokens, cotangent, weights, agent_mask):
    agent, mode = lax.axis_index("agent"), lax.axis_index("mode")
    ids = jnp.stack(
        [agent & 1, mode, agent >> 1, mode >> 1, mode & 1, agent >> 2, (agent >> 1) & 1]
    ).astype(jnp.int32)
    other_ids = ids.at[CORE].set(1 - ids[CORE])
    token_rows = tokens.reshape(ROWS, D)
    grad_rows = cotangent.reshape(ROWS, D)
    offset = jnp.where(agent_mask == 1, 0.0, masked_score).astype(F32).reshape(1, 128)

    outgoing, tokens_a, hidden_keep, hidden_give = enter(ids, token_rows, weights)
    arrived_one = exchange(outgoing, "agent")
    hidden_here = gather_hidden(hidden_keep, hidden_give)
    mixed, tables = agent_forward(arrived_one, offset)
    mixed_one = exchange(mixed, "agent").reshape(8, ROWS, 128)
    outgoing, after, hidden_two, cotangent_m = middle(
        tokens_a, mixed_one, grad_rows, weights, [hidden_here]
    )
    arrived_two = exchange(outgoing.reshape(8, 1024, 128), "mode").reshape(8, 4, ROWS, 128)
    hiddens = [hidden_here] + [swap(hidden_here, "agent", 4 * o) for o in range(1, 4)]
    returning = mode_attention(arrived_two, hiddens[1::2])
    returned_two = exchange(returning.reshape(8, 1024, 128), "mode").reshape(8, 4, ROWS, 128)
    early = (hidden_two, returned_two, cotangent_m)
    theirs = early_products(other_ids, *early, None, hiddens[2:3])
    outgoing, grad_after = turn(returned_two, cotangent_m, after, weights, [theirs])
    upstream = exchange(outgoing, "agent")
    parts = early_products(ids, *early, swap(theirs, "agent", 1), [grad_after])
    arrived_half = swap(parts[1], "mode", 2)
    returning = agent_backward(arrived_one, upstream, tables, [])
    own, left, right = early_half(ids, [parts[0], arrived_half, parts[2], swap(parts[3], "mode", 6)])
    left, right = swap(left, "mode", 6), swap(right, "mode", 2)
    returned_one = exchange(returning.reshape(16, 384, 128), "agent").reshape(16, 3, 128, 128)
    late_parts = late_products(ids, hiddens, returning, mixed_one, grad_after, [])
    token_grads = leave(returned_one, tokens_a, grad_after, weights)
    late = late_sums(ids, *late_parts, [])
    early = early_sums(ids, own, left, right, [token_grads])
    agent_weight_grads, mode_weight_grads = chip_sums(ids, early, late)
    return (token_grads.reshape(tokens.shape), agent_weight_grads, mode_weight_grads)


def solution(mesh):
    placed = (P("agent", "mode", None, None), P("agent", "mode", None, None), P(), P())
    return jax.shard_map(
        local,
        mesh=mesh,
        in_specs=placed,
        out_specs=(
            P("agent", "mode", None, None),
            P(("agent", "mode"), None),
            P(("agent", "mode"), None),
        ),
        check_vma=False,
    )
```

```python
import functools

import jax
import jax.numpy as jnp
from jax import lax
from jax.experimental import pallas as pl
from jax.experimental.pallas import tpu as pltpu
from jax.sharding import PartitionSpec as P

epsilon = 1e-06
masked_score = -1000000000.0

BF = jnp.bfloat16
F32 = jnp.float32
D = 1024
ROWS = 256
SCALE = 0.125
MIB = 1024 * 1024


def decode(row, order):
    if order == "o":
        return row >> 5, (row >> 2) & 7, row & 3
    if order == "a":
        return row & 7, row >> 5, (row >> 3) & 3
    return (row >> 3) & 7, row & 7, row >> 6


def encode(agent, mode, step, order):
    if order == "o":
        return agent * 32 + mode * 4 + step
    if order == "a":
        return mode * 32 + step * 8 + agent
    return step * 64 + agent * 8 + mode


def reorder(values, source, target):
    rows = lax.broadcasted_iota(jnp.int32, (ROWS, ROWS), 0)
    columns = lax.broadcasted_iota(jnp.int32, (ROWS, ROWS), 1)
    chosen = encode(*decode(rows, target), source)
    table = (chosen == columns).astype(F32).astype(BF)
    return jnp.dot(table, values, preferred_element_type=F32).astype(BF)


def dot_nt(left, right):
    return lax.dot_general(left, right, (((1,), (1,)), ((), ())), preferred_element_type=F32)


def dot_tn(left, right):
    return lax.dot_general(left, right, (((0,), (0,)), ((), ())), preferred_element_type=F32)


def factor_of(wide):
    return lax.rsqrt(jnp.mean(wide * wide, -1, keepdims=True) + epsilon)


def normalize_back(values, upstream):
    wide = values.astype(F32)
    factor = factor_of(wide)
    normed = wide * factor
    return factor * (upstream - normed * jnp.mean(upstream * normed, -1, keepdims=True))


def fetch(slots, weights_ref, held_ref, sems_ref):
    copies = [
        pltpu.make_async_copy(weights_ref.at[slot], held_ref.at[n], sems_ref.at[n])
        for n, slot in enumerate(slots)
    ]
    step = pl.program_id(0)

    @pl.when(step == 0)
    def _():
        for copy in copies:
            copy.start()

    def ready():
        for n, copy in enumerate(copies):

            @pl.when(step == n)
            def _(copy=copy):
                copy.wait()

        return held_ref[step]

    return ready


def pinned(operand):
    return pltpu.with_memory_space_constraint(operand, pltpu.HBM)


def held(count):
    return [pltpu.VMEM((count, D, D), BF), pltpu.SemaphoreType.DMA((count,))]


def params(limit=32):
    return pltpu.CompilerParams(vmem_limit_bytes=limit * MIB)


def cost(flops, read):
    return pl.CostEstimate(flops=int(flops), bytes_accessed=int(read), transcendentals=0)


unused = pl.BlockSpec(memory_space=pl.ANY)


def fixed(shape):
    return pl.BlockSpec(shape, lambda *i: (0,) * len(shape))


def stack_heads(values):
    lanes = lax.broadcasted_iota(jnp.int32, (1, 128), 1)
    first = (lanes < 64).astype(F32).astype(BF)
    second = (lanes >= 64).astype(F32).astype(BF)
    return jnp.concatenate([values * first, values * second], 0)


def beside(table):
    return jnp.concatenate([table[:128], table[128:]], 1)


def probabilities(query_stack, keys, offset):
    scores = dot_nt(query_stack, keys) * SCALE + offset
    raised = jnp.exp(scores - jnp.max(scores, -1, keepdims=True))
    return raised * (1.0 / jnp.sum(raised, -1, keepdims=True))


def attend(table, values):
    return jnp.dot(beside(table.astype(BF)), stack_heads(values), preferred_element_type=F32)


def attention_back(table, query_stack, keys, values, upstream):
    upstream_stack = stack_heads(upstream)
    through = dot_nt(upstream_stack, values)
    value_grad = dot_tn(table.astype(BF), upstream_stack)
    centre = jnp.sum(through * table, -1, keepdims=True)
    score_grad = (table * (through - centre) * SCALE).astype(BF)
    query_grad = jnp.dot(beside(score_grad), stack_heads(keys), preferred_element_type=F32)
    keys_grad = dot_tn(score_grad, query_stack)
    return query_grad, keys_grad, value_grad


def enter_kernel(
    ids_ref, tokens_ref, weights_ref,
    send_ref, tokens_out_ref, keep_ref, give_ref, hidden_ref, held_ref, sems_ref,
):
    step = pl.program_id(0)
    ready = fetch((0, 1, 2), weights_ref, held_ref, sems_ref)

    @pl.when(step == 0)
    def _():
        rows = reorder(tokens_ref[...], "o", "a")
        tokens_out_ref[...] = rows
        wide = rows.astype(F32)
        hidden = (wide * factor_of(wide)).astype(BF)
        hidden_ref[...] = hidden
        core = ids_ref[0]

        @pl.when(core == 0)
        def _():
            keep_ref[...] = hidden[:128]
            give_ref[...] = hidden[128:]

        @pl.when(core == 1)
        def _():
            keep_ref[...] = hidden[128:]
            give_ref[...] = hidden[:128]

    result = jnp.dot(hidden_ref[...], ready(), preferred_element_type=F32).astype(BF)
    for pair in range(8):
        for half in range(2):
            send_ref[2 * pair + half] = result[
                128 * half : 128 * half + 128, 128 * pair : 128 * pair + 128
            ]


def enter(ids, tokens, weights):
    return pl.pallas_call(
        enter_kernel,
        grid_spec=pltpu.PrefetchScalarGridSpec(
            num_scalar_prefetch=1,
            grid=(3,),
            in_specs=[fixed((ROWS, D)), unused],
            out_specs=[
                pl.BlockSpec((16, 128, 128), lambda i, c: (0, i, 0)),
                fixed((ROWS, D)),
                fixed((128, D)),
                fixed((128, D)),
            ],
            scratch_shapes=[pltpu.VMEM((ROWS, D), BF)] + held(3),
        ),
        out_shape=[
            jax.ShapeDtypeStruct((16, 384, 128), BF),
            pltpu.HBM((ROWS, D), BF),
            pltpu.HBM((128, D), BF),
            jax.ShapeDtypeStruct((128, D), BF),
        ],
        compiler_params=params(45),
        cost_estimate=cost(3 * 2 * ROWS * D * D, 8 * MIB),
        name="enter",
    )(ids, tokens, pinned(weights))


def agent_rows(block, step):
    return block[:, 8 * step : 8 * step + 8, :].reshape(128, 128).astype(BF)


def agent_forward_kernel(query_ref, keys_ref, values_ref, offset_ref, out_ref, table_ref):
    query = query_ref[...].astype(F32)
    keys = keys_ref[...].astype(F32)
    values = values_ref[...].astype(F32)
    offset = offset_ref[...]
    outs = []
    for step in range(4):
        table = probabilities(
            stack_heads(agent_rows(query, step)), agent_rows(keys, step), offset
        )
        table_ref[0, step] = table
        outs.append(attend(table, agent_rows(values, step)).reshape(16, 8, 128))
    out_ref[...] = jnp.concatenate(outs, 1).astype(BF)


def agent_specs():
    return [pl.BlockSpec((16, 32, 128), lambda i, k=k: (0, 4 * k + i, 0)) for k in range(3)]


def agent_forward(arrived, offset):
    return pl.pallas_call(
        agent_forward_kernel,
        grid=(4,),
        in_specs=agent_specs() + [fixed((1, 128))],
        out_specs=[
            pl.BlockSpec((16, 32, 128), lambda i: (0, i, 0)),
            pl.BlockSpec((1, 4, 256, 128), lambda i: (i, 0, 0, 0)),
        ],
        out_shape=[
            jax.ShapeDtypeStruct((16, 128, 128), BF),
            pltpu.HBM((4, 4, 256, 128), F32),
        ],
        compiler_params=params(),
        cost_estimate=cost(3e9, 4 * MIB),
        name="agent_forward",
    )(arrived, arrived, arrived, offset)


def agent_backward_kernel(
    query_ref, keys_ref, values_ref, upstream_ref, table_ref, query_out, keys_out, values_out
):
    query = query_ref[...].astype(F32)
    keys = keys_ref[...].astype(F32)
    values = values_ref[...].astype(F32)
    upstream = upstream_ref[...].astype(F32)
    outs = [[], [], []]
    for step in range(4):
        grads = attention_back(
            table_ref[0, step],
            stack_heads(agent_rows(query, step)),
            agent_rows(keys, step),
            agent_rows(values, step),
            agent_rows(upstream, step),
        )
        for kept, grad in zip(outs, grads):
            kept.append(grad.reshape(16, 8, 128))
    for ref, kept in zip((query_out, keys_out, values_out), outs):
        ref[...] = jnp.concatenate(kept, 1).astype(BF)


def agent_backward_all_kernel(q, k, v, g, table_ref, *rest):
    out_ref = rest[-1]
    agent_backward_kernel(
        q,
        k,
        v,
        g,
        table_ref,
        out_ref.at[:, 0],
        out_ref.at[:, 1],
        out_ref.at[:, 2],
    )


def agent_backward(arrived, upstream, tables, waits=()):
    return pl.pallas_call(
        agent_backward_all_kernel,
        grid=(4,),
        in_specs=agent_specs()
        + [
            pl.BlockSpec((16, 32, 128), lambda i: (0, i, 0)),
            pl.BlockSpec((1, 4, 256, 128), lambda i: (i, 0, 0, 0)),
        ]
        + [unused] * len(waits),
        out_specs=pl.BlockSpec((16, 3, 32, 128), lambda i: (0, 0, i, 0)),
        out_shape=jax.ShapeDtypeStruct((16, 3, 128, 128), BF),
        compiler_params=params(),
        cost_estimate=cost(6e9, 6 * MIB),
        name="agent_backward",
    )(*[pinned(arrived)] * 3, upstream, pinned(tables), *map(pinned, waits))


def middle_kernel(
    tokens_ref, mixed_ref, cotangent_ref, weights_ref, *rest
):
    send_ref, after_ref, hidden_out_ref, cotangent_out_ref, hidden_ref = rest[-7:-2]
    step = pl.program_id(0)
    ready = fetch((3, 4, 5, 6, 7), weights_ref, *rest[-2:])
    matrix = ready()

    @pl.when(step == 0)
    def _():
        mixed = jnp.concatenate([mixed_ref[pair] for pair in range(8)], 1)
        after = (
            tokens_ref[...].astype(F32)
            + jnp.dot(mixed, matrix, preferred_element_type=F32)
        ).astype(BF)
        after = reorder(after, "a", "m")
        after_ref[...] = after
        wide = after.astype(F32)
        hidden = (wide * factor_of(wide)).astype(BF)
        hidden_ref[...] = hidden
        for block in range(8):
            hidden_out_ref[block] = hidden[:, 128 * block : 128 * block + 128]
        cotangent_out_ref[...] = reorder(cotangent_ref[...], "o", "m")

    def send(result):
        result = result.astype(BF)
        for pair in range(8):
            send_ref[pair, 0] = result[:, 128 * pair : 128 * pair + 128]

    @pl.when((step > 0) & (step < 4))
    def _():
        send(jnp.dot(hidden_ref[...], matrix, preferred_element_type=F32))

    @pl.when(step == 4)
    def _():
        send(dot_nt(cotangent_out_ref[...], matrix))


def middle(tokens, mixed, cotangent, weights, waits=()):
    return pl.pallas_call(
        middle_kernel,
        grid=(5,),
        in_specs=[
            fixed((ROWS, D)),
            fixed((8, ROWS, 128)),
            fixed((ROWS, D)),
            unused,
        ]
        + [unused] * len(waits),
        out_specs=[
            pl.BlockSpec((8, 1, ROWS, 128), lambda i: (0, jnp.maximum(i - 1, 0), 0, 0)),
            fixed((ROWS, D)),
            fixed((8, ROWS, 128)),
            fixed((ROWS, D)),
        ],
        out_shape=[
            pltpu.HBM((8, 4, ROWS, 128), BF),
            pltpu.HBM((ROWS, D), BF),
            pltpu.HBM((8, ROWS, 128), BF),
            pltpu.HBM((ROWS, D), BF),
        ],
        scratch_shapes=[pltpu.VMEM((ROWS, D), BF)] + held(5),
        compiler_params=params(45),
        cost_estimate=cost(5 * 2 * ROWS * D * D, 13 * MIB),
        name="middle",
    )(tokens, mixed, cotangent, pinned(weights), *map(pinned, waits))


def mode_kernel(arrived_ref, *rest):
    out_ref = rest[-1]
    rows = lax.broadcasted_iota(jnp.int32, (256, 128), 0)
    columns = lax.broadcasted_iota(jnp.int32, (256, 128), 1)
    same = ((rows >> 6) & 1) == (columns >> 6)
    offset = jnp.where(same, 0.0, -1e30).astype(F32)
    for pair in range(4):

        def take(which):
            block = arrived_ref[:, which, 16 * pair : 16 * pair + 16, :].astype(F32)
            parts = [block[:, 8 * n : 8 * n + 8, :].reshape(64, 128) for n in range(2)]
            return jnp.concatenate(parts, 0).astype(BF)

        query, keys, values, upstream = (take(which) for which in range(4))
        query_stack = stack_heads(query)
        table = probabilities(query_stack, keys, offset)
        results = (attend(table, values),) + attention_back(
            table, query_stack, keys, values, upstream
        )
        for which, result in enumerate(results):
            parts = [result[64 * n : 64 * n + 64].reshape(8, 8, 128) for n in range(2)]
            out_ref[:, which, 16 * pair : 16 * pair + 16, :] = jnp.concatenate(parts, 1).astype(BF)


def mode_attention(arrived, after=()):
    spec = pl.BlockSpec((8, 4, 64, 128), lambda i: (0, 0, i, 0))
    return pl.pallas_call(
        mode_kernel,
        grid=(4,),
        in_specs=[spec] + [unused] * len(after),
        out_specs=spec,
        out_shape=pltpu.HBM((8, 4, ROWS, 128), BF),
        compiler_params=params(),
        cost_estimate=cost(8e9, 4 * MIB),
        name="mode_attention",
    )(arrived, *map(pinned, after))


def turn_kernel(returned_ref, cotangent_ref, after_ref, weights_ref, *rest):
    send_ref, grad_after_ref, total_ref = rest[-5:-2]
    step = pl.program_id(0)
    ready = fetch((4, 5, 6, 3), weights_ref, *rest[-2:])
    matrix = ready()

    @pl.when(step < 3)
    def _():
        grads = jnp.concatenate([returned_ref[pair, 0] for pair in range(8)], 1)
        product = dot_nt(grads, matrix)

        @pl.when(step == 0)
        def _():
            total_ref[...] = product

        @pl.when(step > 0)
        def _():
            total_ref[...] += product

    @pl.when(step == 3)
    def _():
        grad_after = (
            cotangent_ref[...].astype(F32) + normalize_back(after_ref[...], total_ref[...])
        ).astype(BF)
        grad_after = reorder(grad_after, "m", "a")
        grad_after_ref[...] = grad_after
        result = dot_nt(grad_after, matrix).astype(BF)
        for pair in range(8):
            for half in range(2):
                send_ref[2 * pair + half] = result[
                    128 * half : 128 * half + 128, 128 * pair : 128 * pair + 128
                ]


def turn(returned, cotangent, after, weights, waits=()):
    return pl.pallas_call(
        turn_kernel,
        grid=(4,),
        in_specs=[
            pl.BlockSpec((8, 1, ROWS, 128), lambda i: (0, jnp.minimum(i + 1, 3), 0, 0)),
            fixed((ROWS, D)),
            fixed((ROWS, D)),
            unused,
        ]
        + [unused] * len(waits),
        out_specs=[fixed((16, 128, 128)), fixed((ROWS, D))],
        out_shape=[
            pltpu.HBM((16, 128, 128), BF),
            pltpu.HBM((ROWS, D), BF),
        ],
        scratch_shapes=[pltpu.VMEM((ROWS, D), F32)] + held(4),
        compiler_params=params(45),
        cost_estimate=cost(4 * 2 * ROWS * D * D, 12 * MIB),
        name="turn",
    )(returned, cotangent, after, pinned(weights), *waits)


def whole_rows(ref):
    return jnp.concatenate([ref[:, 0].reshape(8, ROWS, 128)[pair] for pair in range(8)], 1)


def leave_kernel(returned_ref, tokens_ref, grad_after_ref, weights_ref, *rest):
    out_ref, total_ref = rest[-4:-2]
    step = pl.program_id(0)
    ready = fetch((0, 1, 2), weights_ref, *rest[-2:])
    product = dot_nt(whole_rows(returned_ref), ready())

    @pl.when(step == 0)
    def _():
        total_ref[...] = product

    @pl.when(step > 0)
    def _():
        total_ref[...] += product

    @pl.when(step == 2)
    def _():
        grads = (
            grad_after_ref[...].astype(F32) + normalize_back(tokens_ref[...], total_ref[...])
        ).astype(BF)
        out_ref[...] = reorder(grads, "a", "o")


def leave(returned, tokens, grad_after, weights, waits=()):
    return pl.pallas_call(
        leave_kernel,
        grid=(3,),
        in_specs=[
            pl.BlockSpec((16, 1, 128, 128), lambda i: (0, i, 0, 0)),
            fixed((ROWS, D)),
            fixed((ROWS, D)),
            unused,
        ]
        + [unused] * len(waits),
        out_specs=fixed((ROWS, D)),
        out_shape=jax.ShapeDtypeStruct((ROWS, D), BF),
        scratch_shapes=[pltpu.VMEM((ROWS, D), F32)] + held(3),
        compiler_params=params(45),
        cost_estimate=cost(3 * 2 * ROWS * D * D, 9 * MIB),
        name="leave",
    )(returned, tokens, grad_after, pinned(weights), *map(pinned, waits))


CORE, MODE, CHIP, Z, YLO, X, YHI = range(7)


def swap(values, axis, bits):
    size = lax.axis_size(axis)
    return lax.ppermute(values, axis, [(n, n ^ bits) for n in range(size)])


def swap_all(parts, axis, bit):
    return [parts[0]] + [swap(parts[o], axis, o * bit) for o in range(1, 4)]


def prefetched(kernel, ids, operands, in_specs, out_specs, out_shape, name, grid=(), scratch=()):
    return pl.pallas_call(
        kernel,
        grid_spec=pltpu.PrefetchScalarGridSpec(
            num_scalar_prefetch=1,
            grid=grid,
            in_specs=in_specs,
            out_specs=out_specs,
            scratch_shapes=list(scratch),
        ),
        out_shape=out_shape,
        compiler_params=params(),
        cost_estimate=cost(1e9, 5 * MIB),
        name=name,
    )(ids, *operands)


def rows_of(values, start, count):
    return values[pl.ds(pl.multiple_of(start, count), count), :]


def early_kernel(add, ids_ref, hidden_ref, mixed_ref, grads_ref, last_ref, *rest):
    step = pl.program_id(0)

    def finish(first, second, right):
        product = dot_tn(jnp.concatenate([first, second], 1), right)
        if add:
            arrived_ref, total_ref = rest[0], rest[-1]
            total_ref[...] = product + arrived_ref[0].astype(F32)
            for columns in range(2):
                for give in range(2):
                    out_ref = rest[2 * columns + give - 5]
                    near, far = ((0, 3), (1, 2))[give] if columns == 0 else ((0, 1), (3, 2))[give]
                    for place, partner in enumerate((near, far)):
                        rows = rows_of(total_ref, (ids_ref[Z] ^ partner) * 64, 64)
                        out_ref[0, 64 * place : 64 * place + 64] = rows[
                            :, 512 * columns : 512 * columns + 512
                        ].astype(BF)
        else:
            rest[-1][0] = product.astype(BF)

    @pl.when(step < 6)
    def _():
        right = jnp.concatenate([grads_ref[pair, 0] for pair in range(8)], 1)
        finish(hidden_ref[0], hidden_ref[1], right)

    @pl.when(step >= 6)
    def _():
        finish(mixed_ref[0, 0], mixed_ref[1, 0], last_ref[...])


def early_products(ids, hidden, returned, last, arrived=None, waits=()):
    def feature(i, ids_ref):
        return 2 * (i % 2) + ids_ref[CORE]

    in_specs = [
        pl.BlockSpec((2, ROWS, 128), lambda i, c: (feature(i, c), 0, 0)),
        pl.BlockSpec((2, 1, ROWS, 128), lambda i, c: (feature(i, c), 0, 0, 0)),
        pl.BlockSpec((8, 1, ROWS, 128), lambda i, c: (0, jnp.minimum(i // 2, 2) + 1, 0, 0)),
        pl.BlockSpec((ROWS, D), lambda i, c: (0, 0)),
    ]
    operands = [pinned(hidden), returned, returned, pinned(last)]
    if arrived is None:
        return prefetched(
            functools.partial(early_kernel, False), ids, operands + [pinned(wait) for wait in waits],
            in_specs + [unused] * len(waits),
            pl.BlockSpec((1, ROWS, D), lambda i, c: (i, 0, 0)),
            jax.ShapeDtypeStruct((8, ROWS, D), BF), "early_first", (8,),
        )
    return prefetched(
        functools.partial(early_kernel, True), ids, operands + [arrived, *map(pinned, waits)],
        in_specs + [pl.BlockSpec((1, ROWS, D), lambda i, c: (i, 0, 0))] + [unused] * len(waits),
        [pl.BlockSpec((1, 128, 512), lambda i, c: (i, 0, 0))] * 4,
        [pltpu.HBM((8, 128, 512), BF), jax.ShapeDtypeStruct((8, 128, 512), BF)] * 2, "early_add", (8,),
        [pltpu.VMEM((ROWS, D), F32)],
    )


def sum_split_kernel(split, count, inputs, ids_ref, *refs):
    total_ref = refs[-1]
    total = refs[0][0].astype(F32)
    for ref in refs[1:inputs]:
        total += ref[0].astype(F32)
    total_ref[...] = total
    share = total_ref.shape[0] // count
    for partner, out_ref in enumerate(refs[-1 - count : -1]):
        out_ref[0] = rows_of(total_ref, (ids_ref[split] ^ partner) * share, share).astype(BF)


def sum_split(ids, parts, split, count, name, waits=()):
    blocks, rows, columns = parts[0].shape
    return prefetched(
        functools.partial(sum_split_kernel, split, count, len(parts)), ids, [*parts, *map(pinned, waits)],
        [pl.BlockSpec((1, rows, columns), lambda i, c: (i, 0, 0))] * len(parts)
        + [unused] * len(waits),
        [pl.BlockSpec((1, rows // count, columns), lambda i, c: (i, 0, 0))] * count,
        [jax.ShapeDtypeStruct((blocks, rows // count, columns), BF)] * count, name, (blocks,),
        [pltpu.VMEM((rows, columns), F32)],
    )


def early_half_kernel(ids_ref, left_ref, left_in, right_ref, right_in, own_ref, *outs):
    for columns, (ref, arrived) in enumerate(((left_ref, left_in), (right_ref, right_in))):
        total = (ref[...].astype(F32) + arrived[...].astype(F32)).astype(BF)
        own_ref[:, :, 512 * columns : 512 * columns + 512] = total[:, :64]
        outs[columns][...] = total[:, 64:]


def early_half(ids, parts):
    narrow = pl.BlockSpec((2, 64, 512), lambda i, c: (i, 0, 0))
    return prefetched(
        early_half_kernel, ids, parts,
        [pl.BlockSpec((2, 128, 512), lambda i, c: (i, 0, 0))] * 4,
        [pl.BlockSpec((2, 64, D), lambda i, c: (i, 0, 0)), narrow, narrow],
        [pltpu.HBM((8, 64, D), BF)] + [jax.ShapeDtypeStruct((8, 64, 512), BF)] * 2,
        "early_half", (4,),
    )


def early_z_kernel(ids_ref, own_ref, left_ref, right_ref, *rest):
    for other, out_ref in enumerate(rest[-2:]):
        first = pl.multiple_of((ids_ref[YLO] ^ other) * 32, 32)
        for columns, ref in enumerate((left_ref, right_ref)):
            lanes = slice(512 * columns, 512 * columns + 512)
            out_ref[:, :, lanes] = (
                own_ref[:, pl.ds(first, 32), lanes].astype(F32)
                + ref[:, pl.ds(first, 32), :].astype(F32)
            ).astype(BF)


def early_sums(ids, own, left, right, waits):
    narrow = pl.BlockSpec((2, 64, 512), lambda i, c: (i, 0, 0))
    keep, give = prefetched(
        early_z_kernel, ids, [own, left, right, *map(pinned, waits)],
        [pl.BlockSpec((2, 64, D), lambda i, c: (i, 0, 0)), narrow, narrow] + [unused] * len(waits),
        [pl.BlockSpec((2, 32, D), lambda i, c: (i, 0, 0))] * 2,
        [pltpu.HBM((8, 32, D), BF), jax.ShapeDtypeStruct((8, 32, D), BF)], "early_z", (4,),
    )
    return keep, swap(give, "mode", 1)


WIDE = 384 + D


def gather_hidden(keep, give):
    chip = jnp.concatenate([keep, swap(give, "agent", 1)], 0)
    here = jnp.stack([chip, swap(chip, "agent", 2)])
    return here


def late_kernel(ids_ref, *refs):
    hiddens, first_ref, second_ref, mixed_ref, after_ref, mine_ref, *theirs_refs, total_ref = (
        refs[:4],
        *refs[4:8],
        *refs[-4:],
    )
    step = pl.program_id(0)
    core = ids_ref[CORE]

    @pl.when(step == 0)
    def _():
        total_ref[...] = jnp.zeros_like(total_ref)

    for partner, ref in enumerate(hiddens):

        @pl.when(step // 2 == partner)
        def _(ref=ref):
            right = jnp.concatenate(
                [
                    jnp.concatenate([source[0, slot] for slot in range(3)], 1)
                    for source in (first_ref, second_ref)
                ],
                0,
            )
            total_ref[...] += dot_tn(right, ref[0])

    for block in range(4):

        @pl.when(step == 8 + block)
        def _(block=block):
            rows = total_ref[:, 256 * block : 256 * block + 256].T.astype(BF)
            left = jnp.concatenate([mixed_ref[0], mixed_ref[1]], 1)
            other = dot_tn(left, after_ref[...]).astype(BF)

            @pl.when(core == block % 2)
            def _():
                mine_ref[block // 2, :, :384] = rows
                mine_ref[block // 2, :, 384:] = other

            @pl.when(core != block % 2)
            def _():
                theirs_refs[block // 2][:, :384] = rows
                theirs_refs[block // 2][:, 384:] = other


def late_products(ids, hiddens, grads, mixed, grad_after, waits):
    def source(i, c, other):
        chip = (c[X] ^ jnp.minimum(i // 2, 3)) * 2 + (c[YHI] ^ (i % 2))
        return 2 * chip + (c[CORE] ^ other)

    in_specs = [
        pl.BlockSpec((1, ROWS, D), lambda i, c, o=o: (jnp.clip(i - 2 * o, 0, 1), 0, 0))
        for o in range(4)
    ]
    in_specs += [
        pl.BlockSpec((1, 3, 128, 128), lambda i, c, o=o: (source(i, c, o), 0, 0, 0))
        for o in range(2)
    ]
    in_specs += [
        pl.BlockSpec((2, ROWS, 128), lambda i, c: (jnp.clip(i - 8, 0, 3), 0, 0)),
        pl.BlockSpec((ROWS, D), lambda i, c: (0, 0)),
    ]
    return prefetched(
        late_kernel, ids, list(map(pinned, hiddens)) + [grads, grads, pinned(mixed), grad_after, *map(pinned, waits)],
        in_specs + [unused] * len(waits),
        [pl.BlockSpec((2, ROWS, WIDE), lambda i, c: (0, 0, 0))]
        + [pl.BlockSpec((ROWS, WIDE), lambda i, c: (0, 0))] * 2,
        [jax.ShapeDtypeStruct((2, ROWS, WIDE), BF)]
        + [jax.ShapeDtypeStruct((ROWS, WIDE), BF)] * 2, "late_products", (12,),
        [pltpu.VMEM((384, D), F32)],
    )


def chips_kernel(ids_ref, early_ref, early_in, *rest):
    late, outs, total_ref = rest[:4], rest[4:-1], rest[-1]
    total_ref[...] = late[0][...].astype(F32)
    for ref in late[1:]:
        total_ref[...] += ref[...].astype(F32)
    for partner, out_ref in enumerate(outs):
        chip_x = ids_ref[X] ^ partner
        lanes = pl.ds(pl.multiple_of(jnp.minimum(chip_x, 2) * 128, 128), 128)
        for n in range(2):
            block = chip_x * 2 + n
            out_ref[n, :, :D] = (early_ref[block].astype(F32) + early_in[block].astype(F32)).astype(
                BF
            )
        out_ref[:, :, D : D + 128] = total_ref[:, :, lanes].astype(BF)
        out_ref[:, :, D + 128 :] = total_ref[:, :, 384:].astype(BF)


def cross_kernel(ids_ref, *refs):
    for other, out_ref in enumerate(refs[4:]):
        row = ids_ref[YHI] ^ other
        for source, target in ((0, 0), (D + 128, 384)):
            total = refs[0][row, :, source : source + D].astype(F32)
            for ref in refs[1:4]:
                total += ref[row, :, source : source + D].astype(F32)
            for place in range(4):
                out_ref[place, :, target : target + 256] = total[
                    :, 256 * place : 256 * place + 256
                ].astype(BF)
        for partner, ref in enumerate(refs[:4]):
            out_ref[partner, :, 256:384] = ref[row, :, D : D + 128]


def last_kernel(ids_ref, keep_ref, arrived_ref, agent_ref, mode_ref):
    for place in range(4):
        lanes = slice(256 * place, 256 * place + 256)
        mode_ref[:, lanes] = keep_ref[place, :, :256].astype(F32) + arrived_ref[
            place, :, :256
        ].astype(F32)

    @pl.when(ids_ref[X] < 3)
    def _():
        for other, ref in enumerate((keep_ref, arrived_ref)):
            for partner in range(4):
                pair = (ids_ref[X] ^ partner) * 2 + (ids_ref[YHI] ^ other)
                lanes = pl.ds(pl.multiple_of(pair * 128, 128), 128)
                agent_ref[:, lanes] = ref[partner, :, 256:384].astype(F32)

    @pl.when(ids_ref[X] == 3)
    def _():
        for place in range(4):
            lanes = slice(256 * place, 256 * place + 256)
            agent_ref[:, lanes] = keep_ref[place, :, 384:].astype(F32) + arrived_ref[
                place, :, 384:
            ].astype(F32)


def chip_sums(ids, early, late):
    parts = prefetched(
        chips_kernel, ids, [*early, *late],
        [fixed((8, 32, D))] * 2 + [fixed((2, 32, WIDE))] * 4, [fixed((2, 32, 128 + 2 * D))] * 4,
        [jax.ShapeDtypeStruct((2, 32, 128 + 2 * D), BF)] * 4, "chips", (1,),
        [pltpu.VMEM((2, 32, WIDE), F32)],
    )
    keep, give = prefetched(
        cross_kernel, ids, swap_all(parts, "agent", 4),
        [fixed((2, 32, 128 + 2 * D))] * 4, [fixed((4, 32, 640))] * 2,
        [jax.ShapeDtypeStruct((4, 32, 640), BF)] * 2, "cross", (1,),
    )
    return prefetched(
        last_kernel, ids, [keep, swap(give, "agent", 2)],
        [fixed((4, 32, 640))] * 2, [fixed((32, D))] * 2,
        [jax.ShapeDtypeStruct((32, D), F32)] * 2, "last", (1,),
    )


def late_add_kernel(ids_ref, mine_ref, first_ref, second_ref, *rest):
    total_ref = rest[-1]
    for block, ref in enumerate((first_ref, second_ref)):
        total_ref[...] = mine_ref[block].astype(F32) + ref[...].astype(F32)
        for partner, out_ref in enumerate(rest[-3:-1]):
            for z in range(4):
                first = z * 64 + (ids_ref[YLO] ^ partner) * 32
                out_ref[block, 32 * z : 32 * z + 32] = rows_of(total_ref, first, 32).astype(BF)


def late_sums(ids, mine, first, second, waits):
    keep, give = prefetched(
        late_add_kernel, ids,
        [mine, swap(first, "agent", 1), swap(second, "agent", 1)],
        [fixed((2, ROWS, WIDE))] + [fixed((ROWS, WIDE))] * 2,
        [fixed((2, 128, WIDE))] * 2,
        [pltpu.HBM((2, 128, WIDE), BF), jax.ShapeDtypeStruct((2, 128, WIDE), BF)],
        "late_add", (1,),
        [pltpu.VMEM((ROWS, WIDE), F32)],
    )
    parts = sum_split(ids, [keep, swap(give, "mode", 1)], Z, 4, "late_y", waits)
    return swap_all(parts, "mode", 2)


def exchange(values, axis):
    return lax.all_to_all(values, axis, split_axis=0, concat_axis=0, tiled=True)


def local(tokens, cotangent, weights, agent_mask):
    agent, mode = lax.axis_index("agent"), lax.axis_index("mode")
    ids = jnp.stack(
        [agent & 1, mode, agent >> 1, mode >> 1, mode & 1, agent >> 2, (agent >> 1) & 1]
    ).astype(jnp.int32)
    other_ids = ids.at[CORE].set(1 - ids[CORE])
    token_rows = tokens.reshape(ROWS, D)
    grad_rows = cotangent.reshape(ROWS, D)
    offset = jnp.where(agent_mask == 1, 0.0, masked_score).astype(F32).reshape(1, 128)

    outgoing, tokens_a, hidden_keep, hidden_give = enter(ids, token_rows, weights)
    arrived_one = exchange(outgoing, "agent")
    hidden_here = gather_hidden(hidden_keep, hidden_give)
    mixed, tables = agent_forward(arrived_one, offset)
    mixed_one = exchange(mixed, "agent").reshape(8, ROWS, 128)
    outgoing, after, hidden_two, cotangent_m = middle(
        tokens_a, mixed_one, grad_rows, weights, [hidden_here]
    )
    arrived_two = exchange(outgoing.reshape(8, 1024, 128), "mode").reshape(8, 4, ROWS, 128)
    hiddens = [hidden_here] + [swap(hidden_here, "agent", 4 * o) for o in range(1, 4)]
    returning = mode_attention(arrived_two, hiddens[1::2])
    returned_two = exchange(returning.reshape(8, 1024, 128), "mode").reshape(8, 4, ROWS, 128)
    early = (hidden_two, returned_two, cotangent_m)
    theirs = early_products(other_ids, *early, None, hiddens[2:3])
    outgoing, grad_after = turn(returned_two, cotangent_m, after, weights, [theirs])
    upstream = exchange(outgoing, "agent")
    parts = early_products(ids, *early, swap(theirs, "agent", 1), [grad_after])
    arrived_half = swap(parts[1], "mode", 2)
    returning = agent_backward(arrived_one, upstream, tables, [])
    own, left, right = early_half(ids, [parts[0], arrived_half, parts[2], swap(parts[3], "mode", 6)])
    left, right = swap(left, "mode", 6), swap(right, "mode", 2)
    returned_one = exchange(returning.reshape(16, 384, 128), "agent").reshape(16, 3, 128, 128)
    late_parts = late_products(ids, hiddens, returning, mixed_one, grad_after, [])
    token_grads = leave(returned_one, tokens_a, grad_after, weights)
    late = late_sums(ids, *late_parts, [])
    early = early_sums(ids, own, left, right, [token_grads])
    agent_weight_grads, mode_weight_grads = chip_sums(ids, early, late)
    return (token_grads.reshape(tokens.shape), agent_weight_grads, mode_weight_grads)


def solution(mesh):
    placed = (P("agent", "mode", None, None), P("agent", "mode", None, None), P(), P())
    return jax.shard_map(
        local,
        mesh=mesh,
        in_specs=placed,
        out_specs=(
            P("agent", "mode", None, None),
            P(("agent", "mode"), None),
            P(("agent", "mode"), None),
        ),
        check_vma=False,
    )
```

```python
import functools

import jax
import jax.numpy as jnp
from jax import lax
from jax.experimental import pallas as pl
from jax.experimental.pallas import tpu as pltpu
from jax.sharding import PartitionSpec as P

epsilon = 1e-06
masked_score = -1000000000.0

BF = jnp.bfloat16
F32 = jnp.float32
D = 1024
ROWS = 256
SCALE = 0.125
MIB = 1024 * 1024


def decode(row, order):
    if order == "o":
        return row >> 5, (row >> 2) & 7, row & 3
    if order == "a":
        return row & 7, row >> 5, (row >> 3) & 3
    return (row >> 3) & 7, row & 7, row >> 6


def encode(agent, mode, step, order):
    if order == "o":
        return agent * 32 + mode * 4 + step
    if order == "a":
        return mode * 32 + step * 8 + agent
    return step * 64 + agent * 8 + mode


def reorder(values, source, target):
    rows = lax.broadcasted_iota(jnp.int32, (ROWS, ROWS), 0)
    columns = lax.broadcasted_iota(jnp.int32, (ROWS, ROWS), 1)
    chosen = encode(*decode(rows, target), source)
    table = (chosen == columns).astype(F32).astype(BF)
    return jnp.dot(table, values, preferred_element_type=F32).astype(BF)


def dot_nt(left, right):
    return lax.dot_general(left, right, (((1,), (1,)), ((), ())), preferred_element_type=F32)


def dot_tn(left, right):
    return lax.dot_general(left, right, (((0,), (0,)), ((), ())), preferred_element_type=F32)


def factor_of(wide):
    return lax.rsqrt(jnp.mean(wide * wide, -1, keepdims=True) + epsilon)


def normalize_back(values, upstream):
    wide = values.astype(F32)
    factor = factor_of(wide)
    normed = wide * factor
    return factor * (upstream - normed * jnp.mean(upstream * normed, -1, keepdims=True))


def fetch(slots, weights_ref, held_ref, sems_ref):
    copies = [
        pltpu.make_async_copy(weights_ref.at[slot], held_ref.at[n], sems_ref.at[n])
        for n, slot in enumerate(slots)
    ]
    step = pl.program_id(0)

    @pl.when(step == 0)
    def _():
        for copy in copies:
            copy.start()

    def ready():
        for n, copy in enumerate(copies):

            @pl.when(step == n)
            def _(copy=copy):
                copy.wait()

        return held_ref[step]

    return ready


def pinned(operand):
    return pltpu.with_memory_space_constraint(operand, pltpu.HBM)


def held(count):
    return [pltpu.VMEM((count, D, D), BF), pltpu.SemaphoreType.DMA((count,))]


def params(limit=32):
    return pltpu.CompilerParams(vmem_limit_bytes=limit * MIB)


def cost(flops, read):
    return pl.CostEstimate(flops=int(flops), bytes_accessed=int(read), transcendentals=0)


unused = pl.BlockSpec(memory_space=pl.ANY)


def fixed(shape):
    return pl.BlockSpec(shape, lambda *i: (0,) * len(shape))


def stack_heads(values):
    lanes = lax.broadcasted_iota(jnp.int32, (1, 128), 1)
    first = (lanes < 64).astype(F32).astype(BF)
    second = (lanes >= 64).astype(F32).astype(BF)
    return jnp.concatenate([values * first, values * second], 0)


def beside(table):
    return jnp.concatenate([table[:128], table[128:]], 1)


def probabilities(query_stack, keys, offset):
    scores = dot_nt(query_stack, keys) * SCALE + offset
    raised = jnp.exp(scores - jnp.max(scores, -1, keepdims=True))
    return raised * (1.0 / jnp.sum(raised, -1, keepdims=True))


def attend(table, values):
    return jnp.dot(beside(table.astype(BF)), stack_heads(values), preferred_element_type=F32)


def attention_back(table, query_stack, keys, values, upstream):
    upstream_stack = stack_heads(upstream)
    through = dot_nt(upstream_stack, values)
    value_grad = dot_tn(table.astype(BF), upstream_stack)
    centre = jnp.sum(through * table, -1, keepdims=True)
    score_grad = (table * (through - centre) * SCALE).astype(BF)
    query_grad = jnp.dot(beside(score_grad), stack_heads(keys), preferred_element_type=F32)
    keys_grad = dot_tn(score_grad, query_stack)
    return query_grad, keys_grad, value_grad


def enter_kernel(
    ids_ref, tokens_ref, weights_ref,
    send_ref, tokens_out_ref, keep_ref, give_ref, hidden_ref, held_ref, sems_ref,
):
    step = pl.program_id(0)
    ready = fetch((0, 1, 2), weights_ref, held_ref, sems_ref)

    @pl.when(step == 0)
    def _():
        rows = reorder(tokens_ref[...], "o", "a")
        tokens_out_ref[...] = rows
        wide = rows.astype(F32)
        hidden = (wide * factor_of(wide)).astype(BF)
        hidden_ref[...] = hidden
        core = ids_ref[0]

        @pl.when(core == 0)
        def _():
            keep_ref[...] = hidden[:128]
            give_ref[...] = hidden[128:]

        @pl.when(core == 1)
        def _():
            keep_ref[...] = hidden[128:]
            give_ref[...] = hidden[:128]

    result = jnp.dot(hidden_ref[...], ready(), preferred_element_type=F32).astype(BF)
    for pair in range(8):
        for half in range(2):
            send_ref[2 * pair + half] = result[
                128 * half : 128 * half + 128, 128 * pair : 128 * pair + 128
            ]


def enter(ids, tokens, weights):
    return pl.pallas_call(
        enter_kernel,
        grid_spec=pltpu.PrefetchScalarGridSpec(
            num_scalar_prefetch=1,
            grid=(3,),
            in_specs=[fixed((ROWS, D)), unused],
            out_specs=[
                pl.BlockSpec((16, 128, 128), lambda i, c: (0, i, 0)),
                fixed((ROWS, D)),
                fixed((128, D)),
                fixed((128, D)),
            ],
            scratch_shapes=[pltpu.VMEM((ROWS, D), BF)] + held(3),
        ),
        out_shape=[
            jax.ShapeDtypeStruct((16, 384, 128), BF),
            pltpu.HBM((ROWS, D), BF),
            pltpu.HBM((128, D), BF),
            jax.ShapeDtypeStruct((128, D), BF),
        ],
        compiler_params=params(45),
        cost_estimate=cost(3 * 2 * ROWS * D * D, 8 * MIB),
        name="enter",
    )(ids, tokens, pinned(weights))


def agent_rows(block, step):
    return block[:, 8 * step : 8 * step + 8, :].reshape(128, 128).astype(BF)


def agent_forward_kernel(query_ref, keys_ref, values_ref, offset_ref, out_ref, table_ref):
    query = query_ref[...].astype(F32)
    keys = keys_ref[...].astype(F32)
    values = values_ref[...].astype(F32)
    offset = offset_ref[...]
    outs = []
    for step in range(4):
        table = probabilities(
            stack_heads(agent_rows(query, step)), agent_rows(keys, step), offset
        )
        table_ref[0, step] = table
        outs.append(attend(table, agent_rows(values, step)).reshape(16, 8, 128))
    out_ref[...] = jnp.concatenate(outs, 1).astype(BF)


def agent_specs():
    return [pl.BlockSpec((16, 32, 128), lambda i, k=k: (0, 4 * k + i, 0)) for k in range(3)]


def agent_forward(arrived, offset):
    return pl.pallas_call(
        agent_forward_kernel,
        grid=(4,),
        in_specs=agent_specs() + [fixed((1, 128))],
        out_specs=[
            pl.BlockSpec((16, 32, 128), lambda i: (0, i, 0)),
            pl.BlockSpec((1, 4, 256, 128), lambda i: (i, 0, 0, 0)),
        ],
        out_shape=[
            jax.ShapeDtypeStruct((16, 128, 128), BF),
            pltpu.HBM((4, 4, 256, 128), F32),
        ],
        compiler_params=params(),
        cost_estimate=cost(3e9, 4 * MIB),
        name="agent_forward",
    )(arrived, arrived, arrived, offset)


def agent_backward_kernel(
    query_ref, keys_ref, values_ref, upstream_ref, table_ref, query_out, keys_out, values_out
):
    query = query_ref[...].astype(F32)
    keys = keys_ref[...].astype(F32)
    values = values_ref[...].astype(F32)
    upstream = upstream_ref[...].astype(F32)
    outs = [[], [], []]
    for step in range(4):
        grads = attention_back(
            table_ref[0, step],
            stack_heads(agent_rows(query, step)),
            agent_rows(keys, step),
            agent_rows(values, step),
            agent_rows(upstream, step),
        )
        for kept, grad in zip(outs, grads):
            kept.append(grad.reshape(16, 8, 128))
    for ref, kept in zip((query_out, keys_out, values_out), outs):
        ref[...] = jnp.concatenate(kept, 1).astype(BF)


def agent_backward_all_kernel(q, k, v, g, table_ref, *rest):
    out_ref = rest[-1]
    agent_backward_kernel(
        q,
        k,
        v,
        g,
        table_ref,
        out_ref.at[:, 0],
        out_ref.at[:, 1],
        out_ref.at[:, 2],
    )


def agent_backward(arrived, upstream, tables, waits=()):
    return pl.pallas_call(
        agent_backward_all_kernel,
        grid=(4,),
        in_specs=agent_specs()
        + [
            pl.BlockSpec((16, 32, 128), lambda i: (0, i, 0)),
            pl.BlockSpec((1, 4, 256, 128), lambda i: (i, 0, 0, 0)),
        ]
        + [unused] * len(waits),
        out_specs=pl.BlockSpec((16, 3, 32, 128), lambda i: (0, 0, i, 0)),
        out_shape=jax.ShapeDtypeStruct((16, 3, 128, 128), BF),
        compiler_params=params(),
        cost_estimate=cost(6e9, 6 * MIB),
        name="agent_backward",
    )(*[pinned(arrived)] * 3, upstream, pinned(tables), *map(pinned, waits))


def middle_kernel(
    tokens_ref, mixed_ref, cotangent_ref, weights_ref, *rest
):
    send_ref, after_ref, hidden_out_ref, cotangent_out_ref, hidden_ref = rest[-7:-2]
    step = pl.program_id(0)
    ready = fetch((3, 4, 5, 6, 7), weights_ref, *rest[-2:])
    matrix = ready()

    @pl.when(step == 0)
    def _():
        mixed = jnp.concatenate([mixed_ref[pair] for pair in range(8)], 1)
        after = (
            tokens_ref[...].astype(F32)
            + jnp.dot(mixed, matrix, preferred_element_type=F32)
        ).astype(BF)
        after = reorder(after, "a", "m")
        after_ref[...] = after
        wide = after.astype(F32)
        hidden = (wide * factor_of(wide)).astype(BF)
        hidden_ref[...] = hidden
        for block in range(8):
            hidden_out_ref[block] = hidden[:, 128 * block : 128 * block + 128]
        cotangent_out_ref[...] = reorder(cotangent_ref[...], "o", "m")

    def send(result):
        result = result.astype(BF)
        for pair in range(8):
            send_ref[pair, 0] = result[:, 128 * pair : 128 * pair + 128]

    @pl.when((step > 0) & (step < 4))
    def _():
        send(jnp.dot(hidden_ref[...], matrix, preferred_element_type=F32))

    @pl.when(step == 4)
    def _():
        send(dot_nt(cotangent_out_ref[...], matrix))


def middle(tokens, mixed, cotangent, weights, waits=()):
    return pl.pallas_call(
        middle_kernel,
        grid=(5,),
        in_specs=[
            fixed((ROWS, D)),
            fixed((8, ROWS, 128)),
            fixed((ROWS, D)),
            unused,
        ]
        + [unused] * len(waits),
        out_specs=[
            pl.BlockSpec((8, 1, ROWS, 128), lambda i: (0, jnp.maximum(i - 1, 0), 0, 0)),
            fixed((ROWS, D)),
            fixed((8, ROWS, 128)),
            fixed((ROWS, D)),
        ],
        out_shape=[
            pltpu.HBM((8, 4, ROWS, 128), BF),
            pltpu.HBM((ROWS, D), BF),
            pltpu.HBM((8, ROWS, 128), BF),
            pltpu.HBM((ROWS, D), BF),
        ],
        scratch_shapes=[pltpu.VMEM((ROWS, D), BF)] + held(5),
        compiler_params=params(45),
        cost_estimate=cost(5 * 2 * ROWS * D * D, 13 * MIB),
        name="middle",
    )(tokens, mixed, cotangent, pinned(weights), *map(pinned, waits))


def mode_kernel(arrived_ref, *rest):
    out_ref = rest[-1]
    rows = lax.broadcasted_iota(jnp.int32, (256, 128), 0)
    columns = lax.broadcasted_iota(jnp.int32, (256, 128), 1)
    same = ((rows >> 6) & 1) == (columns >> 6)
    offset = jnp.where(same, 0.0, -1e30).astype(F32)
    for pair in range(4):

        def take(which):
            block = arrived_ref[:, which, 16 * pair : 16 * pair + 16, :].astype(F32)
            parts = [block[:, 8 * n : 8 * n + 8, :].reshape(64, 128) for n in range(2)]
            return jnp.concatenate(parts, 0).astype(BF)

        query, keys, values, upstream = (take(which) for which in range(4))
        query_stack = stack_heads(query)
        table = probabilities(query_stack, keys, offset)
        results = (attend(table, values),) + attention_back(
            table, query_stack, keys, values, upstream
        )
        for which, result in enumerate(results):
            parts = [result[64 * n : 64 * n + 64].reshape(8, 8, 128) for n in range(2)]
            out_ref[:, which, 16 * pair : 16 * pair + 16, :] = jnp.concatenate(parts, 1).astype(BF)


def mode_attention(arrived, after=()):
    spec = pl.BlockSpec((8, 4, 64, 128), lambda i: (0, 0, i, 0))
    return pl.pallas_call(
        mode_kernel,
        grid=(4,),
        in_specs=[spec] + [unused] * len(after),
        out_specs=spec,
        out_shape=pltpu.HBM((8, 4, ROWS, 128), BF),
        compiler_params=params(),
        cost_estimate=cost(8e9, 4 * MIB),
        name="mode_attention",
    )(arrived, *map(pinned, after))


def turn_kernel(returned_ref, cotangent_ref, after_ref, weights_ref, *rest):
    send_ref, grad_after_ref, total_ref = rest[-5:-2]
    step = pl.program_id(0)
    ready = fetch((4, 5, 6, 3), weights_ref, *rest[-2:])
    matrix = ready()

    @pl.when(step < 3)
    def _():
        grads = jnp.concatenate([returned_ref[pair, 0] for pair in range(8)], 1)
        product = dot_nt(grads, matrix)

        @pl.when(step == 0)
        def _():
            total_ref[...] = product

        @pl.when(step > 0)
        def _():
            total_ref[...] += product

    @pl.when(step == 3)
    def _():
        grad_after = (
            cotangent_ref[...].astype(F32) + normalize_back(after_ref[...], total_ref[...])
        ).astype(BF)
        grad_after = reorder(grad_after, "m", "a")
        grad_after_ref[...] = grad_after
        result = dot_nt(grad_after, matrix).astype(BF)
        for pair in range(8):
            for half in range(2):
                send_ref[2 * pair + half] = result[
                    128 * half : 128 * half + 128, 128 * pair : 128 * pair + 128
                ]


def turn(returned, cotangent, after, weights, waits=()):
    return pl.pallas_call(
        turn_kernel,
        grid=(4,),
        in_specs=[
            pl.BlockSpec((8, 1, ROWS, 128), lambda i: (0, jnp.minimum(i + 1, 3), 0, 0)),
            fixed((ROWS, D)),
            fixed((ROWS, D)),
            unused,
        ]
        + [unused] * len(waits),
        out_specs=[fixed((16, 128, 128)), fixed((ROWS, D))],
        out_shape=[
            pltpu.HBM((16, 128, 128), BF),
            pltpu.HBM((ROWS, D), BF),
        ],
        scratch_shapes=[pltpu.VMEM((ROWS, D), F32)] + held(4),
        compiler_params=params(45),
        cost_estimate=cost(4 * 2 * ROWS * D * D, 12 * MIB),
        name="turn",
    )(returned, cotangent, after, pinned(weights), *waits)


def whole_rows(ref):
    return jnp.concatenate([ref[:, 0].reshape(8, ROWS, 128)[pair] for pair in range(8)], 1)


def leave_kernel(returned_ref, tokens_ref, grad_after_ref, weights_ref, *rest):
    out_ref, total_ref = rest[-4:-2]
    step = pl.program_id(0)
    ready = fetch((0, 1, 2), weights_ref, *rest[-2:])
    product = dot_nt(whole_rows(returned_ref), ready())

    @pl.when(step == 0)
    def _():
        total_ref[...] = product

    @pl.when(step > 0)
    def _():
        total_ref[...] += product

    @pl.when(step == 2)
    def _():
        grads = (
            grad_after_ref[...].astype(F32) + normalize_back(tokens_ref[...], total_ref[...])
        ).astype(BF)
        out_ref[...] = reorder(grads, "a", "o")


def leave(returned, tokens, grad_after, weights, waits=()):
    return pl.pallas_call(
        leave_kernel,
        grid=(3,),
        in_specs=[
            pl.BlockSpec((16, 1, 128, 128), lambda i: (0, i, 0, 0)),
            fixed((ROWS, D)),
            fixed((ROWS, D)),
            unused,
        ]
        + [unused] * len(waits),
        out_specs=fixed((ROWS, D)),
        out_shape=jax.ShapeDtypeStruct((ROWS, D), BF),
        scratch_shapes=[pltpu.VMEM((ROWS, D), F32)] + held(3),
        compiler_params=params(45),
        cost_estimate=cost(3 * 2 * ROWS * D * D, 9 * MIB),
        name="leave",
    )(returned, tokens, grad_after, pinned(weights), *map(pinned, waits))


CORE, MODE, CHIP, Z, YLO, X, YHI = range(7)


def swap(values, axis, bits):
    size = lax.axis_size(axis)
    return lax.ppermute(values, axis, [(n, n ^ bits) for n in range(size)])


def swap_all(parts, axis, bit):
    return [parts[0]] + [swap(parts[o], axis, o * bit) for o in range(1, 4)]


def prefetched(kernel, ids, operands, in_specs, out_specs, out_shape, name, grid=(), scratch=()):
    return pl.pallas_call(
        kernel,
        grid_spec=pltpu.PrefetchScalarGridSpec(
            num_scalar_prefetch=1,
            grid=grid,
            in_specs=in_specs,
            out_specs=out_specs,
            scratch_shapes=list(scratch),
        ),
        out_shape=out_shape,
        compiler_params=params(),
        cost_estimate=cost(1e9, 5 * MIB),
        name=name,
    )(ids, *operands)


def rows_of(values, start, count):
    return values[pl.ds(pl.multiple_of(start, count), count), :]


def early_kernel(add, ids_ref, hidden_ref, mixed_ref, grads_ref, last_ref, *rest):
    step = pl.program_id(0)

    def finish(first, second, right):
        product = dot_tn(jnp.concatenate([first, second], 1), right)
        if add:
            arrived_ref, total_ref = rest[0], rest[-1]
            total_ref[...] = product + arrived_ref[0].astype(F32)
            for columns in range(2):
                for give in range(2):
                    out_ref = rest[2 * columns + give - 5]
                    near, far = ((0, 3), (1, 2))[give] if columns == 0 else ((0, 1), (3, 2))[give]
                    for place, partner in enumerate((near, far)):
                        rows = rows_of(total_ref, (ids_ref[Z] ^ partner) * 64, 64)
                        out_ref[0, 64 * place : 64 * place + 64] = rows[
                            :, 512 * columns : 512 * columns + 512
                        ].astype(BF)
        else:
            rest[-1][0] = product.astype(BF)

    @pl.when(step < 6)
    def _():
        right = jnp.concatenate([grads_ref[pair, 0] for pair in range(8)], 1)
        finish(hidden_ref[0], hidden_ref[1], right)

    @pl.when(step >= 6)
    def _():
        finish(mixed_ref[0, 0], mixed_ref[1, 0], last_ref[...])


def early_products(ids, hidden, returned, last, arrived=None, waits=()):
    def feature(i, ids_ref):
        return 2 * (i % 2) + ids_ref[CORE]

    in_specs = [
        pl.BlockSpec((2, ROWS, 128), lambda i, c: (feature(i, c), 0, 0)),
        pl.BlockSpec((2, 1, ROWS, 128), lambda i, c: (feature(i, c), 0, 0, 0)),
        pl.BlockSpec((8, 1, ROWS, 128), lambda i, c: (0, jnp.minimum(i // 2, 2) + 1, 0, 0)),
        pl.BlockSpec((ROWS, D), lambda i, c: (0, 0)),
    ]
    operands = [pinned(hidden), returned, returned, pinned(last)]
    if arrived is None:
        return prefetched(
            functools.partial(early_kernel, False), ids, operands + [pinned(wait) for wait in waits],
            in_specs + [unused] * len(waits),
            pl.BlockSpec((1, ROWS, D), lambda i, c: (i, 0, 0)),
            jax.ShapeDtypeStruct((8, ROWS, D), BF), "early_first", (8,),
        )
    return prefetched(
        functools.partial(early_kernel, True), ids, operands + [arrived, *map(pinned, waits)],
        in_specs + [pl.BlockSpec((1, ROWS, D), lambda i, c: (i, 0, 0))] + [unused] * len(waits),
        [pl.BlockSpec((1, 128, 512), lambda i, c: (i, 0, 0))] * 4,
        [pltpu.HBM((8, 128, 512), BF), jax.ShapeDtypeStruct((8, 128, 512), BF)] * 2, "early_add", (8,),
        [pltpu.VMEM((ROWS, D), F32)],
    )


def sum_split_kernel(split, count, inputs, ids_ref, *refs):
    total_ref = refs[-1]
    total = refs[0][0].astype(F32)
    for ref in refs[1:inputs]:
        total += ref[0].astype(F32)
    total_ref[...] = total
    share = total_ref.shape[0] // count
    for partner, out_ref in enumerate(refs[-1 - count : -1]):
        out_ref[0] = rows_of(total_ref, (ids_ref[split] ^ partner) * share, share).astype(BF)


def sum_split(ids, parts, split, count, name, waits=()):
    blocks, rows, columns = parts[0].shape
    return prefetched(
        functools.partial(sum_split_kernel, split, count, len(parts)), ids, [*parts, *map(pinned, waits)],
        [pl.BlockSpec((1, rows, columns), lambda i, c: (i, 0, 0))] * len(parts)
        + [unused] * len(waits),
        [pl.BlockSpec((1, rows // count, columns), lambda i, c: (i, 0, 0))] * count,
        [jax.ShapeDtypeStruct((blocks, rows // count, columns), BF)] * count, name, (blocks,),
        [pltpu.VMEM((rows, columns), F32)],
    )


def early_half_kernel(ids_ref, left_ref, left_in, right_ref, right_in, own_ref, *outs):
    for columns, (ref, arrived) in enumerate(((left_ref, left_in), (right_ref, right_in))):
        total = (ref[...].astype(F32) + arrived[...].astype(F32)).astype(BF)
        own_ref[:, :, 512 * columns : 512 * columns + 512] = total[:, :64]
        outs[columns][...] = total[:, 64:]


def early_half(ids, parts):
    narrow = pl.BlockSpec((1, 64, 512), lambda i, c: (i, 0, 0))
    return prefetched(
        early_half_kernel, ids, parts,
        [pl.BlockSpec((1, 128, 512), lambda i, c: (i, 0, 0))] * 4,
        [pl.BlockSpec((1, 64, D), lambda i, c: (i, 0, 0)), narrow, narrow],
        [pltpu.HBM((8, 64, D), BF)] + [jax.ShapeDtypeStruct((8, 64, 512), BF)] * 2,
        "early_half", (8,),
    )


def early_z_kernel(ids_ref, own_ref, left_ref, right_ref, *rest):
    for other, out_ref in enumerate(rest[-2:]):
        first = pl.multiple_of((ids_ref[YLO] ^ other) * 32, 32)
        for columns, ref in enumerate((left_ref, right_ref)):
            lanes = slice(512 * columns, 512 * columns + 512)
            out_ref[:, :, lanes] = (
                own_ref[:, pl.ds(first, 32), lanes].astype(F32)
                + ref[:, pl.ds(first, 32), :].astype(F32)
            ).astype(BF)


def early_sums(ids, own, left, right, waits):
    narrow = pl.BlockSpec((1, 64, 512), lambda i, c: (i, 0, 0))
    keep, give = prefetched(
        early_z_kernel, ids, [own, left, right, *map(pinned, waits)],
        [pl.BlockSpec((1, 64, D), lambda i, c: (i, 0, 0)), narrow, narrow] + [unused] * len(waits),
        [pl.BlockSpec((1, 32, D), lambda i, c: (i, 0, 0))] * 2,
        [pltpu.HBM((8, 32, D), BF), jax.ShapeDtypeStruct((8, 32, D), BF)], "early_z", (8,),
    )
    return keep, swap(give, "mode", 1)


WIDE = 384 + D


def gather_hidden(keep, give):
    chip = jnp.concatenate([keep, swap(give, "agent", 1)], 0)
    here = jnp.stack([chip, swap(chip, "agent", 2)])
    return here


def late_kernel(ids_ref, *refs):
    hiddens, first_ref, second_ref, mixed_ref, after_ref, mine_ref, *theirs_refs, total_ref = (
        refs[:4],
        *refs[4:8],
        *refs[-4:],
    )
    step = pl.program_id(0)
    core = ids_ref[CORE]

    @pl.when(step == 0)
    def _():
        total_ref[...] = jnp.zeros_like(total_ref)

    for partner, ref in enumerate(hiddens):

        @pl.when(step // 2 == partner)
        def _(ref=ref):
            right = jnp.concatenate(
                [
                    jnp.concatenate([source[0, slot] for slot in range(3)], 1)
                    for source in (first_ref, second_ref)
                ],
                0,
            )
            total_ref[...] += dot_tn(right, ref[0])

    for block in range(4):

        @pl.when(step == 8 + block)
        def _(block=block):
            rows = total_ref[:, 256 * block : 256 * block + 256].T.astype(BF)
            left = jnp.concatenate([mixed_ref[0], mixed_ref[1]], 1)
            other = dot_tn(left, after_ref[...]).astype(BF)

            @pl.when(core == block % 2)
            def _():
                mine_ref[block // 2, :, :384] = rows
                mine_ref[block // 2, :, 384:] = other

            @pl.when(core != block % 2)
            def _():
                theirs_refs[block // 2][:, :384] = rows
                theirs_refs[block // 2][:, 384:] = other


def late_products(ids, hiddens, grads, mixed, grad_after, waits):
    def source(i, c, other):
        chip = (c[X] ^ jnp.minimum(i // 2, 3)) * 2 + (c[YHI] ^ (i % 2))
        return 2 * chip + (c[CORE] ^ other)

    in_specs = [
        pl.BlockSpec((1, ROWS, D), lambda i, c, o=o: (jnp.clip(i - 2 * o, 0, 1), 0, 0))
        for o in range(4)
    ]
    in_specs += [
        pl.BlockSpec((1, 3, 128, 128), lambda i, c, o=o: (source(i, c, o), 0, 0, 0))
        for o in range(2)
    ]
    in_specs += [
        pl.BlockSpec((2, ROWS, 128), lambda i, c: (jnp.clip(i - 8, 0, 3), 0, 0)),
        pl.BlockSpec((ROWS, D), lambda i, c: (0, 0)),
    ]
    return prefetched(
        late_kernel, ids, list(map(pinned, hiddens)) + [grads, grads, pinned(mixed), grad_after, *map(pinned, waits)],
        in_specs + [unused] * len(waits),
        [pl.BlockSpec((2, ROWS, WIDE), lambda i, c: (0, 0, 0))]
        + [pl.BlockSpec((ROWS, WIDE), lambda i, c: (0, 0))] * 2,
        [jax.ShapeDtypeStruct((2, ROWS, WIDE), BF)]
        + [jax.ShapeDtypeStruct((ROWS, WIDE), BF)] * 2, "late_products", (12,),
        [pltpu.VMEM((384, D), F32)],
    )


def chips_kernel(ids_ref, early_ref, early_in, *rest):
    late, outs, total_ref = rest[:4], rest[4:-1], rest[-1]
    total_ref[...] = late[0][...].astype(F32)
    for ref in late[1:]:
        total_ref[...] += ref[...].astype(F32)
    for partner, out_ref in enumerate(outs):
        chip_x = ids_ref[X] ^ partner
        lanes = pl.ds(pl.multiple_of(jnp.minimum(chip_x, 2) * 128, 128), 128)
        for n in range(2):
            block = chip_x * 2 + n
            out_ref[n, :, :D] = (early_ref[block].astype(F32) + early_in[block].astype(F32)).astype(
                BF
            )
        out_ref[:, :, D : D + 128] = total_ref[:, :, lanes].astype(BF)
        out_ref[:, :, D + 128 :] = total_ref[:, :, 384:].astype(BF)


def cross_kernel(ids_ref, *refs):
    for other, out_ref in enumerate(refs[4:]):
        row = ids_ref[YHI] ^ other
        for source, target in ((0, 0), (D + 128, 384)):
            total = refs[0][row, :, source : source + D].astype(F32)
            for ref in refs[1:4]:
                total += ref[row, :, source : source + D].astype(F32)
            for place in range(4):
                out_ref[place, :, target : target + 256] = total[
                    :, 256 * place : 256 * place + 256
                ].astype(BF)
        for partner, ref in enumerate(refs[:4]):
            out_ref[partner, :, 256:384] = ref[row, :, D : D + 128]


def last_kernel(ids_ref, keep_ref, arrived_ref, agent_ref, mode_ref):
    for place in range(4):
        lanes = slice(256 * place, 256 * place + 256)
        mode_ref[:, lanes] = keep_ref[place, :, :256].astype(F32) + arrived_ref[
            place, :, :256
        ].astype(F32)

    @pl.when(ids_ref[X] < 3)
    def _():
        for other, ref in enumerate((keep_ref, arrived_ref)):
            for partner in range(4):
                pair = (ids_ref[X] ^ partner) * 2 + (ids_ref[YHI] ^ other)
                lanes = pl.ds(pl.multiple_of(pair * 128, 128), 128)
                agent_ref[:, lanes] = ref[partner, :, 256:384].astype(F32)

    @pl.when(ids_ref[X] == 3)
    def _():
        for place in range(4):
            lanes = slice(256 * place, 256 * place + 256)
            agent_ref[:, lanes] = keep_ref[place, :, 384:].astype(F32) + arrived_ref[
                place, :, 384:
            ].astype(F32)


def chip_sums(ids, early, late):
    parts = prefetched(
        chips_kernel, ids, [*early, *late],
        [fixed((8, 32, D))] * 2 + [fixed((2, 32, WIDE))] * 4, [fixed((2, 32, 128 + 2 * D))] * 4,
        [jax.ShapeDtypeStruct((2, 32, 128 + 2 * D), BF)] * 4, "chips", (1,),
        [pltpu.VMEM((2, 32, WIDE), F32)],
    )
    keep, give = prefetched(
        cross_kernel, ids, swap_all(parts, "agent", 4),
        [fixed((2, 32, 128 + 2 * D))] * 4, [fixed((4, 32, 640))] * 2,
        [jax.ShapeDtypeStruct((4, 32, 640), BF)] * 2, "cross", (1,),
    )
    return prefetched(
        last_kernel, ids, [keep, swap(give, "agent", 2)],
        [fixed((4, 32, 640))] * 2, [fixed((32, D))] * 2,
        [jax.ShapeDtypeStruct((32, D), F32)] * 2, "last", (1,),
    )


def late_add_kernel(ids_ref, mine_ref, first_ref, second_ref, *rest):
    total_ref = rest[-1]
    for block, ref in enumerate((first_ref, second_ref)):
        total_ref[...] = mine_ref[block].astype(F32) + ref[...].astype(F32)
        for partner, out_ref in enumerate(rest[-3:-1]):
            for z in range(4):
                first = z * 64 + (ids_ref[YLO] ^ partner) * 32
                out_ref[block, 32 * z : 32 * z + 32] = rows_of(total_ref, first, 32).astype(BF)


def late_sums(ids, mine, first, second, waits):
    keep, give = prefetched(
        late_add_kernel, ids,
        [mine, swap(first, "agent", 1), swap(second, "agent", 1)],
        [fixed((2, ROWS, WIDE))] + [fixed((ROWS, WIDE))] * 2,
        [fixed((2, 128, WIDE))] * 2,
        [pltpu.HBM((2, 128, WIDE), BF), jax.ShapeDtypeStruct((2, 128, WIDE), BF)],
        "late_add", (1,),
        [pltpu.VMEM((ROWS, WIDE), F32)],
    )
    parts = sum_split(ids, [keep, swap(give, "mode", 1)], Z, 4, "late_y", waits)
    return swap_all(parts, "mode", 2)


def exchange(values, axis):
    return lax.all_to_all(values, axis, split_axis=0, concat_axis=0, tiled=True)


def local(tokens, cotangent, weights, agent_mask):
    agent, mode = lax.axis_index("agent"), lax.axis_index("mode")
    ids = jnp.stack(
        [agent & 1, mode, agent >> 1, mode >> 1, mode & 1, agent >> 2, (agent >> 1) & 1]
    ).astype(jnp.int32)
    other_ids = ids.at[CORE].set(1 - ids[CORE])
    token_rows = tokens.reshape(ROWS, D)
    grad_rows = cotangent.reshape(ROWS, D)
    offset = jnp.where(agent_mask == 1, 0.0, masked_score).astype(F32).reshape(1, 128)

    outgoing, tokens_a, hidden_keep, hidden_give = enter(ids, token_rows, weights)
    arrived_one = exchange(outgoing, "agent")
    hidden_here = gather_hidden(hidden_keep, hidden_give)
    mixed, tables = agent_forward(arrived_one, offset)
    mixed_one = exchange(mixed, "agent").reshape(8, ROWS, 128)
    outgoing, after, hidden_two, cotangent_m = middle(
        tokens_a, mixed_one, grad_rows, weights, [hidden_here]
    )
    arrived_two = exchange(outgoing.reshape(8, 1024, 128), "mode").reshape(8, 4, ROWS, 128)
    hiddens = [hidden_here] + [swap(hidden_here, "agent", 4 * o) for o in range(1, 4)]
    returning = mode_attention(arrived_two, hiddens[1::2])
    returned_two = exchange(returning.reshape(8, 1024, 128), "mode").reshape(8, 4, ROWS, 128)
    early = (hidden_two, returned_two, cotangent_m)
    theirs = early_products(other_ids, *early, None, hiddens[2:3])
    outgoing, grad_after = turn(returned_two, cotangent_m, after, weights, [theirs])
    upstream = exchange(outgoing, "agent")
    parts = early_products(ids, *early, swap(theirs, "agent", 1), [grad_after])
    arrived_half = swap(parts[1], "mode", 2)
    returning = agent_backward(arrived_one, upstream, tables, [])
    own, left, right = early_half(ids, [parts[0], arrived_half, parts[2], swap(parts[3], "mode", 6)])
    left, right = swap(left, "mode", 6), swap(right, "mode", 2)
    returned_one = exchange(returning.reshape(16, 384, 128), "agent").reshape(16, 3, 128, 128)
    late_parts = late_products(ids, hiddens, returning, mixed_one, grad_after, [])
    token_grads = leave(returned_one, tokens_a, grad_after, weights)
    late = late_sums(ids, *late_parts, [])
    early = early_sums(ids, own, left, right, [token_grads])
    agent_weight_grads, mode_weight_grads = chip_sums(ids, early, late)
    return (token_grads.reshape(tokens.shape), agent_weight_grads, mode_weight_grads)


def solution(mesh):
    placed = (P("agent", "mode", None, None), P("agent", "mode", None, None), P(), P())
    return jax.shard_map(
        local,
        mesh=mesh,
        in_specs=placed,
        out_specs=(
            P("agent", "mode", None, None),
            P(("agent", "mode"), None),
            P(("agent", "mode"), None),
        ),
        check_vma=False,
    )
```
